32 devices in a mesh: dp: 8 (over z, x), tp: 4 (over y, core).
Axes of the slice: x: 2, y: 2, z: 4, core: 2. Of those that a mesh axis runs over, the one named last changes fastest.
Arguments:
- events: float32 [16384, 512], P('dp'), may hold values from -6 to 6
- valid_counts: int32 [8], replicated, may hold values from 1 to 2048, 8192 in all
- mix_cotangent: float32 [16384, 768], P('dp'), may hold values from -6 to 6
- expert_in: float32 [6, 512, 256], P(None, None, 'tp'), may hold values from -0.25 to 0.25
- expert_in_bias: float32 [6, 256], P(None, 'tp'), may hold values from -3 to 3
- expert_out: float32 [6, 256, 256], P(None, None, 'tp'), may hold values from -0.375 to 0.375
- expert_out_bias: float32 [6, 256], P(None, 'tp'), may hold values from -3 to 3
- norm_gain: float32 [6, 256], P(None, 'tp'), may hold values from 0.1 to 1.9
- norm_shift: float32 [6, 256], P(None, 'tp'), may hold values from -2 to 2
- gate_weight: float32 [512, 14], replicated, may hold values from -0.125 to 0.125
Outputs:
- mixtures: float32 [16384, 768], P('dp')
- events_grad: float32 [16384, 512], P('dp')
- expert_in_grad: float32 [6, 512, 256], P(None, None, 'tp')
- expert_in_bias_grad: float32 [6, 256], P(None, 'tp')
- expert_out_grad: float32 [6, 256, 256], P(None, None, 'tp')
- expert_out_bias_grad: float32 [6, 256], P(None, 'tp')
- norm_gain_grad: float32 [6, 256], P(None, 'tp')
- norm_shift_grad: float32 [6, 256], P(None, 'tp')
- gate_weight_grad: float32 [512, 14], replicated
The draws below stay inside these ranges and needn't reach their ends.
Inputs may be any that keep to these rules, and one draw needn't show every extreme that they name: valid_counts[i] is the number of valid rows of index i of dp, which are its first rows; the entries sum to 1024 times the number of indices of dp, and some entry equals 2048.
All inputs are finite; a program needn't handle non-finite values.
Results may differ from the reference program's by a relative error of at most 0.0003.
Values sent between devices are 32-bit elements; how exact they have to be, the bound alone decides.
No kernel may reach another device: no remote copies, remote signals or barrier semaphores. Data moves between devices by JAX's collectives and lax.ppermute only.
A program may use at most 128 MiB of HBM per device.

```python
import math
import jax
import jax.numpy as jnp
import numpy as np
from jax import lax

D = 512
H = 256
O = 256
E = 6
GATE_COLS = 14
BAL = 1024
CAP = 2048
ROWS = 16384
N_DP = 8


def levels(own_key, shape, cuts, smallest, high):
    loudness, own = 1.0, jax.random.fold_in(own_key, 6)
    for dim, shards_of in cuts:
        steps = jnp.exp(jax.random.uniform(jax.random.fold_in(own, dim), (shards_of,), jnp.float32, smallest / len(cuts), high / len(cuts)))
        loudness = loudness * jnp.repeat(steps, shape[dim] // shards_of).reshape([-1 if axis == dim else 1 for axis in range(len(shape))])
    return loudness


def split_up(number_of, total, limit, skew):
    loads = [(1 << 20) // math.isqrt(grade ** skew) + 1 for grade in range(2, number_of + 1)]
    rest, holding = total - limit - (number_of - 1), [1] * (number_of - 1)
    while rest > 0:
        movable = [i for i in range(number_of - 1) if holding[i] < limit]
        mass, remaining = sum([loads[i] for i in movable]), rest
        for i in movable:
            addition = min(limit - holding[i], max(1, remaining * loads[i] // mass), rest)
            holding[i] = holding[i] + addition
            rest = rest - addition
    return np.array([limit] + holding)


def uneven_parts(key, number_of, total, limit, skew):
    if number_of == 2:
        one = jax.random.randint(key, (), max(1, total - limit), min(limit, total - 1) + 1)
        return jnp.stack([one, total - one])
    lengths = jnp.asarray(split_up(number_of, total, limit, skew), jnp.int32)
    twos = (number_of - 1) // 2
    donor, taker = lengths[1:1 + 2 * twos:2], lengths[2:2 + 2 * twos:2]
    room = jnp.minimum(donor - 1, limit - taker)
    passed = jax.random.randint(jax.random.fold_in(key, 1), (twos,), 0, 1 << 20) % (room + 1)
    lengths = lengths.at[1:1 + 2 * twos:2].set(donor - passed).at[2:2 + 2 * twos:2].set(taker + passed)
    return lengths[jax.random.permutation(jax.random.fold_in(key, 2), number_of)]


def gaussian(rng, dims, width, reach, pieces=(), held_as=jnp.bfloat16):
    array = width * jax.random.normal(rng, dims, jnp.float32)
    if pieces:
        array = array * levels(rng, dims, pieces, -0.22, 0.18)
    return jnp.clip(array, -reach, reach).astype(held_as)


def setup_inputs(seed: int = 0) -> dict:
    key_list = jax.random.split(jax.random.key(seed), 11)
    return {
        "events": gaussian(key_list[0], (ROWS, D), 1.0, 6.0, ((0, 8),), jnp.float32),
        "valid_counts": uneven_parts(key_list[1], N_DP, BAL * N_DP, CAP, 2).astype(jnp.int32),
        "mix_cotangent": gaussian(key_list[2], (ROWS, 3 * O), 1.0, 6.0, ((0, 8),), jnp.float32),
        "expert_in": gaussian(key_list[3], (E, D, H), D ** -0.5, 0.25, ((2, 4),), jnp.float32),
        "expert_in_bias": gaussian(key_list[4], (E, H), 0.5, 3.0, ((1, 4),), jnp.float32),
        "expert_out": gaussian(key_list[5], (E, H, O), H ** -0.5, 0.375, ((2, 4),), jnp.float32),
        "expert_out_bias": gaussian(key_list[6], (E, O), 0.5, 3.0, ((1, 4),), jnp.float32),
        "norm_gain": jnp.clip(1.0 + 0.18 * jax.random.normal(key_list[7], (E, O), jnp.float32), 0.1, 1.9),
        "norm_shift": gaussian(key_list[8], (E, O), 0.3, 2.0, ((1, 4),), jnp.float32),
        "gate_weight": gaussian(key_list[9], (D, GATE_COLS), (4 * D) ** -0.5, 0.125, (), jnp.float32),
    }


highest = lax.Precision.HIGHEST
epsilon = 1e-05

@jax.custom_vjp
def low(v):
    return lax.optimization_barrier(v.astype(jnp.bfloat16)).astype(jnp.float32)

@jax.custom_vjp
def low_back(v):
    return v

def low_keep(v):
    return (low(v), None)

def low_pass(kept, grad):
    return (grad,)

def back_keep(v):
    return (v, None)

def back_low(kept, grad):
    return (low(grad),)
low.defvjp(low_keep, low_pass)
low_back.defvjp(back_keep, back_low)

def mixing(logits):
    task_a = jax.nn.softmax(logits[:, 0:4], axis=-1)
    task_b = jax.nn.softmax(logits[:, 4:8], axis=-1)
    shared = jax.nn.softmax(logits[:, 8:14], axis=-1)
    blank = jnp.zeros((logits.shape[0], 2), logits.dtype)
    row_a = jnp.concatenate([task_a[:, 0:2], blank, task_a[:, 2:4]], axis=1)
    row_b = jnp.concatenate([blank, task_b], axis=1)
    return jnp.stack([row_a, row_b, shared], axis=1)

def layer_forward(params, rows_x):
    w_in, b_in, w_out, b_out, gain, shift, gate_w = params
    pre = jnp.einsum('rd,edh->reh', rows_x, w_in, precision=highest) + b_in[None]
    hidden = jax.nn.silu(pre)
    normed_in = jnp.einsum('reh,eho->reo', hidden, w_out, precision=highest) + b_out[None]
    mean_z = lax.optimization_barrier(jnp.mean(normed_in, axis=-1, keepdims=True))
    var_z = lax.optimization_barrier(jnp.mean(normed_in * normed_in, axis=-1, keepdims=True)) - mean_z * mean_z
    unit = (normed_in - mean_z) * lax.rsqrt(var_z + epsilon)
    expert_y = unit * gain[None] + shift[None]
    coef = mixing(jnp.dot(rows_x, gate_w, precision=highest))
    mixed = jnp.einsum('rte,reo->rto', coef, expert_y, precision=highest)
    return mixed.reshape(rows_x.shape[0], 3 * O)

def reference(events, valid_counts, mix_cotangent, expert_in, expert_in_bias, expert_out, expert_out_bias, norm_gain, norm_shift, gate_weight):
    params = (expert_in, expert_in_bias, expert_out, expert_out_bias, norm_gain, norm_shift, gate_weight)
    mask = (jnp.arange(CAP, dtype=jnp.int32)[None, :] < valid_counts[:, None]).astype(events.dtype)
    blocks_x = events.reshape(N_DP, CAP, D)
    blocks_cot = mix_cotangent.reshape(N_DP, CAP, 3 * O)

    def step(total, item):
        block_x, block_cot, block_mask = item

        def masked(weights, values):
            return layer_forward(weights, values) * block_mask[:, None]
        mixed, pull = jax.vjp(masked, params, block_x)
        weight_grads, x_grad = pull(block_cot)
        return (jax.tree.map(jnp.add, total, weight_grads), (mixed, x_grad))
    start = jax.tree.map(jnp.zeros_like, params)
    total, (mixed, x_grad) = lax.scan(step, start, (blocks_x, blocks_cot, mask))
    return (mixed.reshape(ROWS, 3 * O), x_grad.reshape(ROWS, D), total[0], total[1], total[2], total[3], total[4], total[5], total[6])
```

```python
import functools

import jax
import jax.numpy as jnp
from jax import lax
from jax.experimental import pallas as pl
from jax.experimental.pallas import tpu as pltpu
from jax.sharding import PartitionSpec as P

D = 512
H = 256
O = 256
E = 6
GATE_COLS = 14
SLICE = 64
WIDE = D + H
LANES = 128
RB = 256
EPSILON = 1e-05
GROUPS = ((0, 1), (2, 3), (4, 5))
COLUMN = (
    {0: 0, 1: 1, 4: 2, 5: 3},
    {2: 4, 3: 5, 4: 6, 5: 7},
    {e: 8 + e for e in range(E)},
)
F32 = jnp.float32
BF16 = jnp.bfloat16
NN = (((1,), (0,)), ((), ()))
NT = (((1,), (1,)), ((), ()))
TN = (((0,), (0,)), ((), ()))


def split(v):
    high = v.astype(BF16)
    return high, (v - high.astype(F32)).astype(BF16)


def dot3(a, b, dims):
    def one(u, v):
        return lax.dot_general(u, v, dims, preferred_element_type=F32)

    return one(a[0], b[0]) + (one(a[0], b[1]) + one(a[1], b[0]))


def half_of(v, upper):
    return jnp.where(upper, v[:, LANES:], v[:, :LANES])


def params(mib, semantics=None):
    return pltpu.CompilerParams(vmem_limit_bytes=mib << 20, dimension_semantics=semantics)


def gate_kernel(pos, ev_ref, gw_ref, high_ref, low_ref, p_ref, gw):
    gw[...] = jnp.zeros_like(gw)
    gw[:GATE_COLS, :] = gw_ref[...]
    events = split(ev_ref[...])
    high_ref[...], low_ref[...] = events
    logits = dot3(events, split(gw[...]), NT)
    lane = lax.broadcasted_iota(jnp.int32, logits.shape, 1)
    sets = (lane < 4, (lane >= 4) & (lane < 8), (lane >= 8) & (lane < GATE_COLS))

    def per_set(values, empty, reduce):
        a, b, s = (reduce(jnp.where(m, values, empty), axis=1, keepdims=True) for m in sets)
        return jnp.where(sets[0], a, jnp.where(sets[1], b, s))

    top = per_set(logits, -3e38, jnp.max)
    shares = jnp.where(lane < GATE_COLS, jnp.exp(logits - top), 0.0)
    p = shares / per_set(shares, 0.0, jnp.sum)
    rows = pl.num_programs(0) * RB
    row = (pos[0] & 1) * rows + pl.program_id(0) * RB
    row = row + lax.broadcasted_iota(jnp.int32, logits.shape, 0)
    p_ref[...] = jnp.where((row < pos[1]) & (lane < GATE_COLS), p, 0.0)


def gates(pos, events, gate_w, rows):
    steps = rows // RB
    spec = lambda width: pl.BlockSpec((RB, width), lambda i, pos: (i, 0))
    return pl.pallas_call(
        gate_kernel,
        grid_spec=pltpu.PrefetchScalarGridSpec(
            num_scalar_prefetch=1,
            grid=(steps,),
            in_specs=[
                pl.BlockSpec((RB, D), lambda i, pos: ((pos[0] & 1) * steps + i, 0)),
                pl.BlockSpec((GATE_COLS, D), lambda i, pos: (0, 0)),
            ],
            out_specs=[spec(D), spec(D), spec(LANES)],
            scratch_shapes=[pltpu.VMEM((LANES, D), F32)],
        ),
        out_shape=[
            jax.ShapeDtypeStruct((rows, D), BF16),
            jax.ShapeDtypeStruct((rows, D), BF16),
            jax.ShapeDtypeStruct((rows, LANES), F32),
        ],
        compiler_params=params(24),
        cost_estimate=pl.CostEstimate(flops=6 * rows * D * LANES, bytes_accessed=rows * D * 8, transcendentals=0),
    )(pos, events, gate_w)


def expert_kernel(group, first, last, *refs):
    n = len(group)
    refs = list(refs)
    pos, evh_ref, evl_ref, cot_ref, p_ref = refs[:5]
    shards, small_ref = refs[5:9], refs[9]
    del refs[:10]
    mix_in = None if first else refs.pop(0)
    if last:
        dp_before, sums_before = refs[: len(GROUPS) - 1], refs[len(GROUPS) - 1 : 2 * len(GROUPS) - 2]
        del refs[: 2 * len(GROUPS) - 2]
    mix_ref, dp_ref, dph_ref, dpl_ref, winh, winl, own_ref, part_ref, sums_ref = refs[:9]
    del refs[:9]
    wouth, woutl, small, acc, sums = refs[:5]
    gate_acc = refs[5] if last else None
    step, steps = pl.program_id(0), pl.num_programs(0)
    me = pos[0]
    upper = (me >> 1) == 1

    @pl.when(step == 0)
    def _():
        acc[...] = jnp.zeros_like(acc)
        sums[...] = jnp.zeros_like(sums)
        if last:
            gate_acc[...] = jnp.zeros_like(gate_acc)
        for i, e in enumerate(group):
            parts = [shard[i] for shard in shards]
            centre = sum(jnp.sum(part[:, D:], axis=0, keepdims=True) for part in parts) / O
            for k, part in enumerate(parts):
                at = pl.multiple_of((me ^ k) * SLICE, SLICE)
                winh[pl.ds(i * H + at, SLICE), :], winl[pl.ds(i * H + at, SLICE), :] = split(part[:, :D])
                out = split(part[:, D:] - centre)
                wouth[i, pl.ds(at, SLICE), :], woutl[i, pl.ds(at, SLICE), :] = out
            for k in range(4):
                small[i, k : k + 1, :] = jnp.concatenate(
                    [small_ref[j, k, e : e + 1, :] for j in range(4)], axis=1
                )
            small[i, 1:2, :] = small[i, 1:2, :] - jnp.mean(small[i, 1:2, :], axis=1, keepdims=True)

    events = evh_ref[...], evl_ref[...]
    p = p_ref[...]
    lane = lax.broadcasted_iota(jnp.int32, p.shape, 1)
    dp = jnp.zeros_like(p)
    mixed = {}
    dpre_halves = []
    for i, e in enumerate(group):
        win = winh[i * H : (i + 1) * H, :], winl[i * H : (i + 1) * H, :]
        wout = wouth[i], woutl[i]
        b_in, b_out, gain, shift = (small[i, k : k + 1, :] for k in range(4))
        pre = dot3(events, win, NT) + b_in
        sigma = jax.nn.sigmoid(pre)
        hidden = pre * sigma
        hidden_parts = split(hidden)
        centred = dot3(hidden_parts, wout, NT) + b_out
        rstd = lax.rsqrt(jnp.mean(centred * centred, axis=1, keepdims=True) + EPSILON)
        unit = centred * rstd
        y = unit * gain + shift
        dy = None
        for t in range(3):
            if e not in COLUMN[t]:
                continue
            column = COLUMN[t][e]
            cot = cot_ref[:, t * O : (t + 1) * O]
            coef = p[:, column : column + 1]
            mixed[t] = coef * y + mixed[t] if t in mixed else coef * y
            dp = jnp.where(lane == column, jnp.sum(cot * y, axis=1, keepdims=True), dp)
            dy = coef * cot if dy is None else dy + coef * cot
        dunit = dy * gain
        back_first = jnp.mean(dunit, axis=1, keepdims=True)
        back_second = jnp.mean(dunit * unit, axis=1, keepdims=True)
        dnormed = rstd * (dunit - back_first - unit * back_second)
        dnormed_parts = split(dnormed)
        dhidden = dot3(dnormed_parts, wout, NN)
        dpre = dhidden * (sigma + hidden * (1.0 - sigma))
        dpre_parts = split(dpre)
        dph_ref[:, i * H : (i + 1) * H], dpl_ref[:, i * H : (i + 1) * H] = dpre_parts
        dpre_halves.append(tuple(half_of(v, upper) for v in dpre_parts))
        out_halves = tuple(half_of(v, upper) for v in dnormed_parts)
        acc[i * LANES : (i + 1) * LANES, D:] += dot3(out_halves, hidden_parts, TN)
        dy_half = half_of(dy, upper)
        for k, v in enumerate(
            (half_of(dpre, upper), half_of(dnormed, upper), dy_half * half_of(unit, upper), dy_half)
        ):
            sums[4 * i + k : 4 * i + k + 1, :] += jnp.sum(v, axis=0, keepdims=True)
    dpre_half = tuple(jnp.concatenate([h[k] for h in dpre_halves], axis=1) for k in range(2))
    acc[:, :D] += dot3(dpre_half, events, TN)
    for t in range(3):
        at = slice(t * O, (t + 1) * O)
        if t in mixed:
            mix_ref[:, at] = mixed[t] if first else mix_in[:, at] + mixed[t]
        else:
            mix_ref[:, at] = jnp.zeros_like(mix_ref[:, at]) if first else mix_in[:, at]
    if last:
        for other in dp_before:
            dp = dp + other[...]
        weighted = p * dp
        sets = (lane < 4, (lane >= 4) & (lane < 8), (lane >= 8) & (lane < GATE_COLS))
        a, b, s = (jnp.sum(jnp.where(m, weighted, 0.0), axis=1, keepdims=True) for m in sets)
        dlogits = weighted - p * jnp.where(sets[0], a, jnp.where(sets[1], b, s))
        dp_ref[...] = dlogits
        gate_acc[...] += dot3(split(dlogits), events, TN)
    else:
        dp_ref[...] = dp

    @pl.when(step == steps - 1)
    def _():
        mine = pl.multiple_of((me & 1) * SLICE, SLICE)
        other = pl.multiple_of(SLICE - mine, SLICE)
        for i in range(n):
            for t in range(WIDE // LANES):
                at = slice((t * n + i) * SLICE, (t * n + i + 1) * SLICE)
                lanes = slice(t * LANES, (t + 1) * LANES)
                own_ref[at, :] = acc[pl.ds(i * LANES + mine, SLICE), lanes]
                part_ref[at, :] = acc[pl.ds(i * LANES + other, SLICE), lanes]
        if last:
            sums_ref[...] = jnp.zeros_like(sums_ref)
            for g, before in enumerate(sums_before):
                sums_ref[8 * g : 8 * g + 8, :] = before[...]
            g = len(GROUPS) - 1
            sums_ref[8 * g : 8 * g + 8, :] = sums[...]
            for t in range(D // LANES):
                sums_ref[64 + 16 * t : 80 + 16 * t, :] = gate_acc[:16, t * LANES : (t + 1) * LANES]
        else:
            sums_ref[...] = sums[...]


def experts(pos, group, rows, high, low, cot, p, shards, small, mix, before):
    n = len(group)
    first, last = mix is None, before is not None
    steps = rows // RB
    block = lambda width: pl.BlockSpec((RB, width), lambda i, pos: (i, 0))
    whole = lambda shape: pl.BlockSpec(shape, lambda i, pos: (0,) * len(shape))
    in_specs = [
        block(D),
        block(D),
        pl.BlockSpec((RB, 3 * O), lambda i, pos: ((pos[0] & 1) * steps + i, 0)),
        block(LANES),
        *[whole((n, SLICE, WIDE))] * 4,
        whole(small.shape),
    ]
    args = [high, low, cot, p, *shards, small]
    aliases = {}
    if not first:
        aliases = {len(args) + 1: 0}
        in_specs.append(block(3 * O))
        args.append(mix)
    if last:
        in_specs += [block(LANES)] * len(before[0]) + [whole((8, LANES))] * len(before[1])
        args += [*before[0], *before[1]]
    payload = WIDE // LANES * n * SLICE
    sums_shape = (2 * LANES // 2, LANES) if last else (8, LANES)
    scratch = [
        pltpu.VMEM((n, O, H), BF16),
        pltpu.VMEM((n, O, H), BF16),
        pltpu.VMEM((n, 8, H), F32),
        pltpu.VMEM((n * LANES, WIDE), F32),
        pltpu.VMEM((8, LANES), F32),
    ]
    if last:
        scratch.append(pltpu.VMEM((LANES, D), F32))
    return pl.pallas_call(
        functools.partial(expert_kernel, group, first, last),
        grid_spec=pltpu.PrefetchScalarGridSpec(
            num_scalar_prefetch=1,
            grid=(steps,),
            in_specs=in_specs,
            out_specs=[
                block(3 * O),
                block(LANES),
                block(n * H),
                block(n * H),
                whole((n * H, D)),
                whole((n * H, D)),
                whole((payload, LANES)),
                whole((payload, LANES)),
                whole(sums_shape),
            ],
            scratch_shapes=scratch,
        ),
        out_shape=[
            jax.ShapeDtypeStruct((rows, 3 * O), F32),
            jax.ShapeDtypeStruct((rows, LANES), F32),
            jax.ShapeDtypeStruct((rows, n * H), BF16),
            jax.ShapeDtypeStruct((rows, n * H), BF16),
            jax.ShapeDtypeStruct((n * H, D), BF16),
            jax.ShapeDtypeStruct((n * H, D), BF16),
            jax.ShapeDtypeStruct((payload, LANES), F32),
            jax.ShapeDtypeStruct((payload, LANES), F32),
            jax.ShapeDtypeStruct(sums_shape, F32),
        ],
        input_output_aliases=aliases,
        compiler_params=params(48),
        cost_estimate=pl.CostEstimate(flops=n * rows * 6 * 720896, bytes_accessed=rows * 14000, transcendentals=0),
    )(pos, *args)


def event_kernel(n_groups, pos, *refs):
    highs, lows = refs[:n_groups], refs[n_groups : 2 * n_groups]
    winh, winl = refs[2 * n_groups : 3 * n_groups], refs[3 * n_groups : 4 * n_groups]
    dlogits, gw_ref, out, gw = refs[4 * n_groups :]
    gw[...] = jnp.zeros_like(gw)
    gw[:GATE_COLS, :] = gw_ref[...]
    total = dot3(split(dlogits[...]), split(gw[...]), NN)
    for g in range(n_groups):
        total = total + dot3((highs[g][...], lows[g][...]), (winh[g][...], winl[g][...]), NN)
    out[...] = total


def event_grads(pos, rows, highs, lows, winh, winl, dlogits, gate_w):
    n_groups = len(highs)
    block = lambda width: pl.BlockSpec((RB, width), lambda i, pos: (i, 0))
    whole = lambda shape: pl.BlockSpec(shape, lambda i, pos: (0, 0))
    return pl.pallas_call(
        functools.partial(event_kernel, n_groups),
        grid_spec=pltpu.PrefetchScalarGridSpec(
            num_scalar_prefetch=1,
            grid=(rows // RB,),
            in_specs=[block(v.shape[1]) for v in (*highs, *lows)]
            + [whole(v.shape) for v in (*winh, *winl)]
            + [block(LANES), whole((GATE_COLS, D))],
            out_specs=block(D),
            scratch_shapes=[pltpu.VMEM((LANES, D), F32)],
        ),
        out_shape=jax.ShapeDtypeStruct((rows, D), F32),
        compiler_params=params(40),
        cost_estimate=pl.CostEstimate(flops=6 * rows * D * E * H, bytes_accessed=rows * 10000, transcendentals=0),
    )(pos, *highs, *lows, *winh, *winl, dlogits, gate_w)


def place_kernel(pos, own, other, out):
    mine = (pl.program_id(0) >= pl.num_programs(0) // 2) == ((pos[0] & 1) == 1)

    @pl.when(mine)
    def _():
        out[...] = own[...]

    @pl.when(jnp.logical_not(mine))
    def _():
        out[...] = other[...]


def place(pos, own, other):
    rows, width = own.shape
    steps = rows // RB

    def source(which):
        def index(i, pos):
            start = ((pos[0] & 1) ^ which) * steps
            return (jnp.clip(i - start, 0, steps - 1), 0)

        return pl.BlockSpec((RB, width), index)

    return pl.pallas_call(
        place_kernel,
        grid_spec=pltpu.PrefetchScalarGridSpec(
            num_scalar_prefetch=1,
            grid=(2 * steps,),
            in_specs=[source(0), source(1)],
            out_specs=pl.BlockSpec((RB, width), lambda i, pos: (i, 0)),
        ),
        out_shape=jax.ShapeDtypeStruct((2 * rows, width), F32),
        compiler_params=params(24),
        cost_estimate=pl.CostEstimate(flops=0, bytes_accessed=rows * width * 16, transcendentals=0),
    )(pos, own, other)


def in_vmem(kernel, out_shape, scratch, *args):
    total = sum(a.size * 4 for a in args)
    return pl.pallas_call(
        kernel,
        in_specs=[pl.BlockSpec(memory_space=pltpu.SMEM)] + [pl.BlockSpec(memory_space=pltpu.VMEM)] * (len(args) - 1),
        out_specs=[pl.BlockSpec(memory_space=pltpu.VMEM)] * len(out_shape),
        out_shape=out_shape,
        scratch_shapes=scratch,
        compiler_params=params(16),
        cost_estimate=pl.CostEstimate(flops=0, bytes_accessed=2 * total, transcendentals=0),
    )(*args)


def padded(rows, parts):
    unit = 8 * parts
    return -(-rows // unit) * unit


def halves_kernel(n_parts, total, pos, *refs):
    own, got = refs[:n_parts], refs[n_parts : 2 * n_parts]
    keep, send, both = refs[2 * n_parts :]
    at = 0
    for a, b in zip(own, got):
        both[at : at + a.shape[0], :] = a[...] + b[...]
        at += a.shape[0]
    if at < total:
        both[at:, :] = jnp.zeros((total - at, LANES), F32)
    half = total // 2
    mine = pl.multiple_of((pos[2] & 1) * half, 8)
    keep[...] = both[pl.ds(mine, half), :]
    send[...] = both[pl.ds(half - mine, half), :]


def chunks_kernel(outer, keep, got, pos, *refs):
    pass


def split_kernel(outer, pos, own, got, *refs):
    outs, both = refs[:outer], refs[outer]
    both[...] = own[...] + got[...]
    rows = outs[0].shape[0]
    for k in range(outer):
        outs[k][...] = both[pl.ds(pl.multiple_of(((pos[2] >> 1) ^ k) * rows, 8), rows), :]


def join_kernel(outer, pos, *refs):
    out = refs[outer]
    rows = refs[0].shape[0]
    for k in range(outer):
        out[pl.ds(pl.multiple_of(((pos[2] >> 1) ^ k) * rows, 8), rows), :] = refs[k][...]


def summed_over_dp(pos, parts, partner_parts, n_dp):
    outer = n_dp // 2
    got = [lax.ppermute(v, "tp", [(i, i ^ 1) for i in range(4)]) for v in partner_parts]
    total = padded(sum(v.shape[0] for v in parts), 2 * outer)
    half = jax.ShapeDtypeStruct((total // 2, LANES), F32)
    chunk = jax.ShapeDtypeStruct((total // 2 // outer, LANES), F32)
    over_x = [(i, i ^ 1) for i in range(n_dp)]
    over_z = [[(i, i ^ (2 * k)) for i in range(n_dp)] for k in range(outer)]
    keep, send = in_vmem(
        functools.partial(halves_kernel, len(parts), total), [half, half], [pltpu.VMEM((total, LANES), F32)], pos, *parts, *got
    )
    got = lax.ppermute(send, "dp", over_x)
    chunks = in_vmem(
        functools.partial(split_kernel, outer), [chunk] * outer, [pltpu.VMEM((total // 2, LANES), F32)], pos, keep, got
    )
    mine = chunks[0]
    for v in [lax.ppermute(chunks[k], "dp", over_z[k]) for k in range(1, outer)]:
        mine = mine + v
    chunks = [mine] + [lax.ppermute(mine, "dp", over_z[k]) for k in range(1, outer)]
    (done,) = in_vmem(functools.partial(join_kernel, outer), [half], [], pos, *chunks)
    return done, lax.ppermute(done, "dp", over_x)


def finish_kernel(groups, pos, *refs):
    n = len(groups)
    halves = refs[: 2 * n]
    in_grad, in_bias, out_grad, out_bias, gain, shift, gate = refs[2 * n : 2 * n + 7]
    both = refs[2 * n + 7 :]
    odd = (pos[0] & 1) == 1
    for g, group in enumerate(groups):
        half = halves[2 * g].shape[0]
        mine = pl.multiple_of((pos[2] & 1) * half, 8)
        both[g][pl.ds(mine, half), :] = halves[2 * g][...]
        both[g][pl.ds(half - mine, half), :] = halves[2 * g + 1][...]
        for i, e in enumerate(group):
            for t in range(WIDE // LANES):
                at = (t * len(group) + i) * SLICE
                tile = both[g][at : at + SLICE, :]
                if t < D // LANES:
                    in_grad[e, :, t * LANES : (t + 1) * LANES] = tile
                else:
                    out_grad[e, :, t * LANES - D : (t + 1) * LANES - D] = tile
    rest = WIDE // LANES * len(groups[-1]) * SLICE
    sums = both[-1][rest : rest + 24, :]
    sums = jnp.where(odd, sums[:, SLICE:], sums[:, :SLICE])
    for g, group in enumerate(groups):
        for i, e in enumerate(group):
            for k, ref in enumerate((in_bias, out_bias, gain, shift)):
                ref[e : e + 1, :] = sums[8 * g + 4 * i + k : 8 * g + 4 * i + k + 1, :]
    for t in range(D // LANES):
        gate[:, t * LANES : (t + 1) * LANES] = both[-1][rest + 64 + 16 * t : rest + 64 + 16 * t + GATE_COLS, :]


def per_device(
    events,
    valid_counts,
    mix_cotangent,
    expert_in,
    expert_in_bias,
    expert_out,
    expert_out_bias,
    norm_gain,
    norm_shift,
    gate_weight,
):
    n_dp = lax.axis_size("dp")
    rank = lax.axis_index("dp")
    me = lax.axis_index("tp")
    rows = events.shape[0] // 2
    pos = jnp.stack([me, valid_counts[rank], rank]).astype(jnp.int32)
    w_in = jnp.swapaxes(expert_in, 1, 2)
    w_out = jnp.swapaxes(expert_out, 1, 2)
    gate_w = jnp.swapaxes(gate_weight, 0, 1)
    core = [(i, i ^ 1) for i in range(4)]
    across = [(i, i ^ 2) for i in range(4)]
    small = lax.all_gather(jnp.stack([expert_in_bias, expert_out_bias, norm_gain, norm_shift]), "tp")
    shards = []
    ready = None
    for group in GROUPS:
        lo, hi = group[0], group[-1] + 1
        own = jnp.concatenate([w_in[lo:hi], w_out[lo:hi]], axis=2)
        beside = lax.ppermute(own, "tp", core)
        if ready is not None:
            own, _ = lax.optimization_barrier((own, ready))
        ready = lax.ppermute(own, "tp", across)
        shards.append((own, beside, ready, lax.ppermute(ready, "tp", core)))
    high, low, p = gates(pos, events, gate_w, rows)
    mix = None
    dps, sums, highs, lows, winh, winl, summed = [], [], [], [], [], [], []
    for g, group in enumerate(GROUPS):
        before = (dps, sums) if g == len(GROUPS) - 1 else None
        mix, dp, h, l, wh, wl, own, part, s = experts(
            pos, group, rows, high, low, mix_cotangent, p, shards[g], small, mix, before
        )
        for held, v in zip((dps, sums, highs, lows, winh, winl), (dp, s, h, l, wh, wl)):
            held.append(v)
        if before is None:
            summed.append(summed_over_dp(pos, [own], [part], n_dp))
        else:
            summed.append(summed_over_dp(pos, [own, s], [part, s], n_dp))
    x_grad = event_grads(pos, rows, highs, lows, winh, winl, dps[-1], gate_w)
    mixtures = place(pos, mix, lax.ppermute(mix, "tp", core))
    x_grad = place(pos, x_grad, lax.ppermute(x_grad, "tp", core))
    flat = [v for pair in summed for v in pair]
    per_expert = jax.ShapeDtypeStruct((E, SLICE), F32)
    in_grad, in_bias, out_grad, out_bias, gain, shift, gate = in_vmem(
        functools.partial(finish_kernel, GROUPS),
        [
            jax.ShapeDtypeStruct((E, SLICE, D), F32),
            per_expert,
            jax.ShapeDtypeStruct((E, SLICE, H), F32),
            per_expert,
            per_expert,
            per_expert,
            jax.ShapeDtypeStruct((GATE_COLS, D), F32),
        ],
        [pltpu.VMEM((2 * a.shape[0], LANES), F32) for a, _ in summed],
        pos,
        *flat,
    )
    return (
        mixtures,
        x_grad,
        jnp.swapaxes(in_grad, 1, 2),
        in_bias,
        jnp.swapaxes(out_grad, 1, 2),
        out_bias,
        gain,
        shift,
        jnp.swapaxes(gate, 0, 1),
    )


def solution(mesh):
    return jax.shard_map(
        per_device,
        mesh=mesh,
        in_specs=(
            P("dp", None),
            P(),
            P("dp", None),
            P(None, None, "tp"),
            P(None, "tp"),
            P(None, None, "tp"),
            P(None, "tp"),
            P(None, "tp"),
            P(None, "tp"),
            P(),
        ),
        out_specs=(
            P("dp", None),
            P("dp", None),
            P(None, None, "tp"),
            P(None, "tp"),
            P(None, None, "tp"),
            P(None, "tp"),
            P(None, "tp"),
            P(None, "tp"),
            P(),
        ),
        check_vma=False,
    )
```

```python
import functools

import jax
import jax.numpy as jnp
from jax import lax
from jax.experimental import pallas as pl
from jax.experimental.pallas import tpu as pltpu
from jax.sharding import PartitionSpec as P

D = 512
H = 256
O = 256
E = 6
GATE_COLS = 14
SLICE = 64
WIDE = D + H
LANES = 128
TOKEN = (8, LANES)
RB = 512
ROW_BLOCK = 256
SUB = 256
LAG = 1
EPSILON = 1e-05
GROUPS = ((0, 1), (2, 3), (4, 5))
COLUMN = (
    {0: 0, 1: 1, 4: 2, 5: 3},
    {2: 4, 3: 5, 4: 6, 5: 7},
    {e: 8 + e for e in range(E)},
)
F32 = jnp.float32
BF16 = jnp.bfloat16
NN = (((1,), (0,)), ((), ()))
NT = (((1,), (1,)), ((), ()))
TN = (((0,), (0,)), ((), ()))


def split(v):
    high = v.astype(BF16)
    return high, (v - high.astype(F32)).astype(BF16)


def dot3(a, b, dims):
    def one(u, v):
        return lax.dot_general(u, v, dims, preferred_element_type=F32)

    return one(a[0], b[0]) + (one(a[0], b[1]) + one(a[1], b[0]))


def half_of(v, upper):
    return jnp.where(upper, v[:, LANES:], v[:, :LANES])


LARGE = 60


def params(mib):
    return pltpu.CompilerParams(vmem_limit_bytes=mib << 20)


def gate_kernel(n_deps, pos, ev_ref, gw_ref, *refs):
    high_ref, low_ref, p_ref, gw = refs[n_deps:]
    gw[...] = jnp.zeros_like(gw)
    gw[:GATE_COLS, :] = gw_ref[...]
    events = split(ev_ref[...])
    high_ref[...], low_ref[...] = events
    logits = dot3(events, split(gw[...]), NT)
    lane = lax.broadcasted_iota(jnp.int32, logits.shape, 1)
    sets = (lane < 4, (lane >= 4) & (lane < 8), (lane >= 8) & (lane < GATE_COLS))

    def per_set(values, empty, reduce):
        a, b, s = (reduce(jnp.where(m, values, empty), axis=1, keepdims=True) for m in sets)
        return jnp.where(sets[0], a, jnp.where(sets[1], b, s))

    top = per_set(logits, -3e38, jnp.max)
    shares = jnp.where(lane < GATE_COLS, jnp.exp(logits - top), 0.0)
    p = shares / per_set(shares, 0.0, jnp.sum)
    rows = pl.num_programs(0) * ROW_BLOCK
    row = (pos[0] & 1) * rows + pl.program_id(0) * ROW_BLOCK
    row = row + lax.broadcasted_iota(jnp.int32, logits.shape, 0)
    p_ref[...] = jnp.where((row < pos[1]) & (lane < GATE_COLS), p, 0.0)


def gates(pos, events, gate_w, rows, deps):
    steps = rows // ROW_BLOCK
    spec = lambda width: pl.BlockSpec((ROW_BLOCK, width), lambda i, pos: (i, 0))
    return pl.pallas_call(
        functools.partial(gate_kernel, len(deps)),
        grid_spec=pltpu.PrefetchScalarGridSpec(
            num_scalar_prefetch=1,
            grid=(steps,),
            in_specs=[
                pl.BlockSpec((ROW_BLOCK, D), lambda i, pos: ((pos[0] & 1) * steps + i, 0)),
                pl.BlockSpec((GATE_COLS, D), lambda i, pos: (0, 0)),
            ]
            + [pl.BlockSpec(memory_space=pl.ANY)] * len(deps),
            out_specs=[spec(D), spec(D), spec(LANES)],
            scratch_shapes=[pltpu.VMEM((LANES, D), F32)],
        ),
        out_shape=[
            jax.ShapeDtypeStruct((rows, D), BF16),
            jax.ShapeDtypeStruct((rows, D), BF16),
            jax.ShapeDtypeStruct((rows, LANES), F32),
        ],
        compiler_params=params(LARGE),
        cost_estimate=pl.CostEstimate(flops=6 * rows * D * LANES, bytes_accessed=rows * D * 8, transcendentals=0),
    )(pos, events, gate_w, *deps)


def payload_kernel(n_deps, w_in, w_out, *refs):
    out = refs[n_deps]
    out[:, :, :D] = w_in[...]
    out[:, :, D:] = w_out[...]


def payload(group, w_in, w_out, deps):
    n = len(group)
    return pl.pallas_call(
        functools.partial(payload_kernel, len(deps)),
        grid=(n,),
        in_specs=[
            pl.BlockSpec((1, SLICE, D), lambda i: (group[0] + i, 0, 0)),
            pl.BlockSpec((1, SLICE, H), lambda i: (group[0] + i, 0, 0)),
        ]
        + [pl.BlockSpec(memory_space=pl.ANY)] * len(deps),
        out_specs=pl.BlockSpec((1, SLICE, WIDE), lambda i: (i, 0, 0)),
        out_shape=jax.ShapeDtypeStruct((n, SLICE, WIDE), F32),
        compiler_params=params(LARGE),
        cost_estimate=pl.CostEstimate(flops=0, bytes_accessed=n * SLICE * WIDE * 8, transcendentals=0),
    )(w_in, w_out, *deps)


def expert_kernel(group, first, last, n_deps, *refs):
    n = len(group)
    refs = list(refs)
    pos, evh_ref, evl_ref, cot_ref, p_ref = refs[:5]
    shards, smalls = refs[5:9], refs[9:13]
    del refs[:13]
    mix_in = None if first else refs.pop(0)
    if last:
        dp_before, sums_before = refs[: len(GROUPS) - 1], refs[len(GROUPS) - 1 : 2 * len(GROUPS) - 2]
        del refs[: 2 * len(GROUPS) - 2]
    del refs[:n_deps]
    mix_ref, dp_ref, dph_ref, dpl_ref, winh, winl, own_ref, part_ref, sums_ref = refs[:9]
    del refs[:9]
    wouth, woutl, small, acc, sums = refs[:5]
    gate_acc = refs[5] if last else None
    step, steps = pl.program_id(0), pl.num_programs(0)
    odd = pos[0] & 1
    chip = pos[0] >> 1

    def tile(start, other):
        return pl.ds(pl.multiple_of(start + (chip ^ other) * LANES, LANES), LANES)

    @pl.when(step == 0)
    def _():
        acc[...] = jnp.zeros_like(acc)
        sums[...] = jnp.zeros_like(sums)
        if last:
            gate_acc[...] = jnp.zeros_like(gate_acc)
        orders = (jnp.concatenate([smalls[k ^ c][...] for k in range(4)], axis=1) for c in range(2))
        even_order, odd_order = orders
        small[...] = jnp.where(odd == 1, odd_order, even_order)
        for i, e in enumerate(group):
            parts = [
                (shard[i, :, :D], jnp.concatenate([shard[i, :, tile(D, 0)], shard[i, :, tile(D, 1)]], axis=1))
                for shard in shards
            ]
            centre = sum(jnp.sum(out, axis=0, keepdims=True) for _, out in parts) / O
            for k, (into, out) in enumerate(parts):
                at = pl.multiple_of((odd ^ k) * SLICE, SLICE)
                winh[pl.ds(i * H + at, SLICE), :], winl[pl.ds(i * H + at, SLICE), :] = split(into)
                wouth[i, pl.ds(at, SLICE), :], woutl[i, pl.ds(at, SLICE), :] = split(out - centre)
            row = E + e
            small[row : row + 1, :] = small[row : row + 1, :] - jnp.mean(small[row : row + 1, :], axis=1, keepdims=True)

    subs = RB // SUB
    rows_of = [slice(s * SUB, (s + 1) * SUB) for s in range(subs)]
    lane = lax.broadcasted_iota(jnp.int32, (SUB, LANES), 1)
    vector = lambda k, e: small[k * E + e : k * E + e + 1, :]
    state = [dict() for _ in range(subs)]

    def m1(s):
        events = evh_ref[rows_of[s], :], evl_ref[rows_of[s], :]
        state[s]["events"] = events
        pre = dot3(events, (winh[...], winl[...]), NT)
        state[s]["pre"] = [pre[:, i * H : (i + 1) * H] for i in range(n)]

    def v1(s):
        st = state[s]
        st["sigma"], st["hidden"], st["hidden_parts"] = [], [], []
        for i, e in enumerate(group):
            pre = st["pre"][i] + vector(0, e)
            sigma = jax.nn.sigmoid(pre)
            hidden = pre * sigma
            st["sigma"].append(sigma)
            st["hidden"].append(hidden)
            st["hidden_parts"].append(split(hidden))

    def m2(s):
        st = state[s]
        st["centred"] = [dot3(st["hidden_parts"][i], (wouth[i], woutl[i]), NT) for i in range(n)]

    def v2(s):
        st = state[s]
        p = p_ref[rows_of[s], :]
        dp = jnp.zeros_like(p)
        mixed = {}
        cots = [
            jnp.concatenate([cot_ref[rows_of[s], tile(t * O, 0)], cot_ref[rows_of[s], tile(t * O, 1)]], axis=1)
            for t in range(3)
        ]
        st["dnormed"] = []
        for i, e in enumerate(group):
            gain, shift = vector(2, e), vector(3, e)
            centred = st["centred"][i] + vector(1, e)
            rstd = lax.rsqrt(jnp.mean(centred * centred, axis=1, keepdims=True) + EPSILON)
            unit = centred * rstd
            y = unit * gain + shift
            dy = None
            for t in range(3):
                if e not in COLUMN[t]:
                    continue
                column = COLUMN[t][e]
                coef = p[:, column : column + 1]
                mixed[t] = coef * y + mixed[t] if t in mixed else coef * y
                dp = jnp.where(lane == column, jnp.sum(cots[t] * y, axis=1, keepdims=True), dp)
                dy = coef * cots[t] if dy is None else dy + coef * cots[t]
            dunit = dy * gain
            back_first = jnp.mean(dunit, axis=1, keepdims=True)
            back_second = jnp.mean(dunit * unit, axis=1, keepdims=True)
            dnormed = rstd * (dunit - back_first - unit * back_second)
            st["dnormed"].append(split(dnormed))
            dy_half = dy[:, :LANES]
            for k, v in enumerate((dnormed[:, :LANES], dy_half * unit[:, :LANES], dy_half)):
                sums[4 * i + k + 1 : 4 * i + k + 2, :] += jnp.sum(v, axis=0, keepdims=True)
        for t in range(3):
            for other in range(2):
                at = tile(t * O, other)
                if t in mixed:
                    value = mixed[t][:, other * LANES : (other + 1) * LANES]
                    mix_ref[rows_of[s], at] = value if first else mix_in[rows_of[s], at] + value
                elif first:
                    mix_ref[rows_of[s], at] = jnp.zeros((SUB, LANES), F32)
                else:
                    mix_ref[rows_of[s], at] = mix_in[rows_of[s], at]
        if last:
            for other in dp_before:
                dp = dp + other[rows_of[s], :]
            weighted = p * dp
            sets = (lane < 4, (lane >= 4) & (lane < 8), (lane >= 8) & (lane < GATE_COLS))
            a, b, c = (jnp.sum(jnp.where(m, weighted, 0.0), axis=1, keepdims=True) for m in sets)
            dp = weighted - p * jnp.where(sets[0], a, jnp.where(sets[1], b, c))
            st["dlogits"] = dp
        dp_ref[rows_of[s], :] = dp

    def m3(s):
        st = state[s]
        st["dhidden"] = [dot3(st["dnormed"][i], (wouth[i], woutl[i]), NN) for i in range(n)]

    def v3(s):
        st = state[s]
        st["dpre"] = []
        for i, e in enumerate(group):
            sigma, hidden = st["sigma"][i], st["hidden"][i]
            dpre = st["dhidden"][i] * (sigma + hidden * (1.0 - sigma))
            parts = split(dpre)
            dph_ref[rows_of[s], i * H : (i + 1) * H], dpl_ref[rows_of[s], i * H : (i + 1) * H] = parts
            st["dpre"].append(tuple(v[:, :LANES] for v in parts))
            sums[4 * i : 4 * i + 1, :] += jnp.sum(dpre[:, :LANES], axis=0, keepdims=True)

    def m4(s):
        st = state[s]
        for i in range(n):
            halves = tuple(v[:, :LANES] for v in st["dnormed"][i])
            acc[i * LANES : (i + 1) * LANES, D:] += dot3(halves, st["hidden_parts"][i], TN)
        beside = [split(st["dlogits"])] if last else []
        left = tuple(jnp.concatenate([h[k] for h in st["dpre"] + beside], axis=1) for k in range(2))
        both = dot3(left, st["events"], TN)
        acc[:, :D] += both[: n * LANES]
        if last:
            gate_acc[...] += both[n * LANES : n * LANES + 16]

    stages = (m1, v1, m2, v2, m3, v3, m4)
    for turn in range(len(stages) + LAG * (subs - 1)):
        for s in range(subs):
            if 0 <= turn - LAG * s < len(stages):
                stages[turn - LAG * s](s)

    @pl.when(step == steps - 1)
    def _():
        mine = pl.multiple_of(odd * SLICE, SLICE)
        other = pl.multiple_of(SLICE - mine, SLICE)
        for i in range(n):
            for t in range(WIDE // LANES):
                at = slice((t * n + i) * SLICE, (t * n + i + 1) * SLICE)
                lanes = slice(t * LANES, (t + 1) * LANES) if t < D // LANES else tile(D, t - D // LANES)
                own_ref[at, :] = acc[pl.ds(i * LANES + mine, SLICE), lanes]
                part_ref[at, :] = acc[pl.ds(i * LANES + other, SLICE), lanes]
        if last:
            sums_ref[...] = jnp.zeros_like(sums_ref)
            for g, before in enumerate(sums_before):
                sums_ref[8 * g : 8 * g + 8, :] = before[...]
            g = len(GROUPS) - 1
            sums_ref[8 * g : 8 * g + 8, :] = sums[...]
            for t in range(D // LANES):
                sums_ref[64 + 16 * t : 80 + 16 * t, :] = gate_acc[:, t * LANES : (t + 1) * LANES]
        else:
            sums_ref[...] = sums[...]


def experts(pos, group, rows, high, low, cot, p, shards, smalls, mix, before, deps):
    n = len(group)
    first, last = mix is None, before is not None
    steps = rows // RB
    block = lambda width: pl.BlockSpec((RB, width), lambda i, pos: (i, 0))
    whole = lambda shape: pl.BlockSpec(shape, lambda i, pos: (0,) * len(shape))
    in_specs = [
        block(D),
        block(D),
        pl.BlockSpec((RB, 3 * O), lambda i, pos: ((pos[0] & 1) * steps + i, 0)),
        block(LANES),
        *[whole((n, SLICE, WIDE))] * 4,
        *[whole(smalls[0].shape)] * 4,
    ]
    args = [high, low, cot, p, *shards, *smalls]
    aliases = {}
    if not first:
        aliases = {len(args) + 1: 0}
        in_specs.append(block(3 * O))
        args.append(mix)
    if last:
        in_specs += [block(LANES)] * len(before[0]) + [whole((8, LANES))] * len(before[1])
        args += [*before[0], *before[1]]
    in_specs += [pl.BlockSpec(memory_space=pl.ANY)] * len(deps)
    args += deps
    payload = WIDE // LANES * n * SLICE
    sums_shape = (2 * LANES // 2, LANES) if last else (8, LANES)
    scratch = [
        pltpu.VMEM((n, O, H), BF16),
        pltpu.VMEM((n, O, H), BF16),
        pltpu.VMEM((4 * E, H), F32),
        pltpu.VMEM((n * LANES, WIDE), F32),
        pltpu.VMEM((8, LANES), F32),
    ]
    if last:
        scratch.append(pltpu.VMEM((16, D), F32))
    return pl.pallas_call(
        functools.partial(expert_kernel, group, first, last, len(deps)),
        grid_spec=pltpu.PrefetchScalarGridSpec(
            num_scalar_prefetch=1,
            grid=(steps,),
            in_specs=in_specs,
            out_specs=[
                block(3 * O),
                block(LANES),
                block(n * H),
                block(n * H),
                whole((n * H, D)),
                whole((n * H, D)),
                whole((payload, LANES)),
                whole((payload, LANES)),
                whole(sums_shape),
            ],
            scratch_shapes=scratch,
        ),
        out_shape=[
            jax.ShapeDtypeStruct((rows, 3 * O), F32),
            jax.ShapeDtypeStruct((rows, LANES), F32),
            jax.ShapeDtypeStruct((rows, n * H), BF16),
            jax.ShapeDtypeStruct((rows, n * H), BF16),
            jax.ShapeDtypeStruct((n * H, D), BF16),
            jax.ShapeDtypeStruct((n * H, D), BF16),
            jax.ShapeDtypeStruct((payload, LANES), F32),
            jax.ShapeDtypeStruct((payload, LANES), F32),
            jax.ShapeDtypeStruct(sums_shape, F32),
        ],
        input_output_aliases=aliases,
        compiler_params=params(LARGE),
        cost_estimate=pl.CostEstimate(flops=n * rows * 6 * 720896, bytes_accessed=rows * 14000, transcendentals=0),
    )(pos, *args)


def event_kernel(gated, added, pos, high, low, winh, winl, *refs):
    total = dot3((high[...], low[...]), (winh[...], winl[...]), NN)
    if gated:
        dlogits, gw_ref, gw = refs[0], refs[1], refs[-1]
        refs = refs[2:]
        gw[...] = jnp.zeros_like(gw)
        gw[:GATE_COLS, :] = gw_ref[...]
        total = total + dot3(split(dlogits[...]), split(gw[...]), NN)
    if added:
        total = total + refs[0][...]
    refs[-3][...] = total
    refs[-2][...] = jnp.zeros_like(refs[-2])


def event_grads(pos, rows, high, low, winh, winl, gating, before, deps):
    block = lambda width: pl.BlockSpec((ROW_BLOCK, width), lambda i, pos: (i, 0))
    whole = lambda shape: pl.BlockSpec(shape, lambda i, pos: (0, 0))
    args = [high, low, winh, winl]
    in_specs = [block(high.shape[1])] * 2 + [whole(winh.shape)] * 2
    aliases = {}
    if gating:
        args += gating
        in_specs += [block(LANES), whole((GATE_COLS, D))]
    if before is not None:
        aliases = {len(args) + 1: 0}
        args.append(before)
        in_specs.append(block(D))
    return pl.pallas_call(
        functools.partial(event_kernel, bool(gating), before is not None),
        grid_spec=pltpu.PrefetchScalarGridSpec(
            num_scalar_prefetch=1,
            grid=(rows // ROW_BLOCK,),
            in_specs=in_specs + [pl.BlockSpec(memory_space=pl.ANY)] * len(deps),
            out_specs=[block(D), whole(TOKEN)],
            scratch_shapes=[pltpu.VMEM((LANES, D), F32)],
        ),
        out_shape=[jax.ShapeDtypeStruct((rows, D), F32), jax.ShapeDtypeStruct(TOKEN, F32)],
        input_output_aliases=aliases,
        compiler_params=params(LARGE),
        cost_estimate=pl.CostEstimate(flops=6 * rows * D * winh.shape[0], bytes_accessed=rows * 6000, transcendentals=0),
    )(pos, *args, *deps)


def place_kernel(pos, own, other, *refs):
    out, token = refs[-2:]
    token[...] = jnp.zeros_like(token)
    mine = (pl.program_id(0) >= pl.num_programs(0) // 2) == ((pos[0] & 1) == 1)

    @pl.when(mine)
    def _():
        out[...] = own[...]

    @pl.when(jnp.logical_not(mine))
    def _():
        out[...] = other[...]


def place(pos, own, other, deps):
    rows, width = own.shape
    steps = rows // ROW_BLOCK

    def source(which):
        def index(i, pos):
            start = ((pos[0] & 1) ^ which) * steps
            return (jnp.clip(i - start, 0, steps - 1), 0)

        return pl.BlockSpec((ROW_BLOCK, width), index)

    return pl.pallas_call(
        place_kernel,
        grid_spec=pltpu.PrefetchScalarGridSpec(
            num_scalar_prefetch=1,
            grid=(2 * steps,),
            in_specs=[source(0), source(1)] + [pl.BlockSpec(memory_space=pl.ANY)] * len(deps),
            out_specs=[
                pl.BlockSpec((ROW_BLOCK, width), lambda i, pos: (i, 0)),
                pl.BlockSpec(TOKEN, lambda i, pos: (0, 0)),
            ],
        ),
        out_shape=[jax.ShapeDtypeStruct((2 * rows, width), F32), jax.ShapeDtypeStruct(TOKEN, F32)],
        compiler_params=params(LARGE),
        cost_estimate=pl.CostEstimate(flops=0, bytes_accessed=rows * width * 16, transcendentals=0),
    )(pos, own, other, *deps)


class Job:
    def __init__(self, args, shapes, body, scratch=()):
        self.args, self.body, self.scratch = args, body, list(scratch)
        self.shapes = [jax.ShapeDtypeStruct(shape, F32) for shape in shapes]


def copy_job(*arrays):
    def body(pos, ins, outs, scratch):
        for a, b in zip(ins, outs):
            b[...] = a[...]

    return Job(arrays, [a.shape for a in arrays], body)


def run(pos, jobs, deps=(), through=()):
    args = [a for job in jobs for a in job.args]
    shapes = [o for job in jobs for o in job.shapes]
    scratch = [v for job in jobs for v in job.scratch]
    first = 1 + len(args)

    def kernel(pos_ref, *refs):
        ins, refs = refs[: len(args)], refs[len(args) + len(through) + len(deps) :]
        outs, token, kept = refs[: len(shapes)], refs[len(shapes) + len(through)], refs[len(shapes) + len(through) + 1 :]
        token[...] = jnp.zeros_like(token)
        i = o = k = 0
        for job in jobs:
            ni, no, nk = len(job.args), len(job.shapes), len(job.scratch)
            job.body(pos_ref, ins[i : i + ni], outs[o : o + no], kept[k : k + nk])
            i, o, k = i + ni, o + no, k + nk

    vmem, anywhere = pl.BlockSpec(memory_space=pltpu.VMEM), pl.BlockSpec(memory_space=pl.ANY)
    flat = pl.pallas_call(
        kernel,
        in_specs=[pl.BlockSpec(memory_space=pltpu.SMEM)] + [vmem] * len(args) + [anywhere] * (len(through) + len(deps)),
        out_specs=[vmem] * len(shapes) + [anywhere] * len(through) + [vmem],
        out_shape=shapes
        + [jax.ShapeDtypeStruct(v.shape, v.dtype) for v in through]
        + [jax.ShapeDtypeStruct(TOKEN, F32)],
        scratch_shapes=scratch,
        input_output_aliases={first + k: len(shapes) + k for k in range(len(through))},
        compiler_params=params(LARGE),
        cost_estimate=pl.CostEstimate(flops=0, bytes_accessed=sum(8 * a.size for a in args), transcendentals=0),
    )(pos, *args, *through, *deps)
    result = []
    for job in jobs:
        result.append(list(flat[: len(job.shapes)]))
        flat = flat[len(job.shapes) :]
    return result, list(flat[:-1]), flat[-1]


def part_of(ref, index, rows):
    return ref.at[pl.ds(pl.multiple_of(index * rows, 8), rows), :]


class Reduction:
    def __init__(self, pos, own, partner, n_dp):
        self.pos, self.own, self.partner = pos, own, partner
        self.bits = n_dp.bit_length() - 1
        unit = 8 << (self.bits - 1)
        self.rows = -(-sum(v.shape[0] for v in own) // unit) * unit
        self.swap = [[(i, i ^ (1 << b)) for i in range(n_dp)] for b in range(self.bits)]
        self.stage = -1

    def over(self, values, bit):
        return [lax.ppermute(v, "dp", self.swap[bit]) for v in values]

    @property
    def finished(self):
        return self.stage == 2 * self.bits

    def job(self):
        stage, bits = self.stage, self.bits
        if stage < 0:
            return copy_job(*self.partner)
        if stage == 0:
            args = [*self.own, *self.got]
            rows = self.rows
        elif stage <= bits:
            args = [self.keep, *self.got]
            rows = self.keep.shape[0]
        else:
            args = [self.keep, *self.got]
            rows = 2 * self.keep.shape[0]
        n = len(args) // 2
        gather = stage > bits
        bit = stage if stage < bits else 2 * bits - 1 - stage
        halving = stage < bits - 1

        def body(pos, ins, outs, scratch):
            to = scratch[0] if halving else outs[0]
            if gather:
                side = (pos[2] >> bit) & 1
                part_of(to, side, rows // 2)[...] = ins[0][...]
                part_of(to, 1 - side, rows // 2)[...] = ins[1][...]
                return
            at = 0
            for a, b in zip(ins[:n], ins[n:]):
                to[at : at + a.shape[0], :] = a[...] + b[...]
                at += a.shape[0]
            if at < rows:
                to[at:, :] = jnp.zeros((rows - at, LANES), F32)
            if halving:
                side = (pos[2] >> bit) & 1
                outs[0][...] = part_of(to, side, rows // 2)[...]
                outs[1][...] = part_of(to, 1 - side, rows // 2)[...]

        if halving:
            return Job(args, [(rows // 2, LANES)] * 2, body, [pltpu.VMEM((rows, LANES), F32)])
        return Job(args, [(rows, LANES)], body)

    def take(self, outs):
        stage, bits = self.stage, self.bits
        if stage < 0:
            self.got = [lax.ppermute(v, "tp", [(i, i ^ 1) for i in range(4)]) for v in outs]
        else:
            self.keep = outs[0]
            bit = stage if stage < bits else 2 * bits - 2 - stage
            if bit >= 0:
                self.got = self.over([outs[-1]], bit)
        self.stage += 1


def finish_body(groups, pos, halves, outs, both):
    in_grad, in_bias, out_grad, out_bias, gain, shift, gate = outs
    n, whole = len(groups), []
    odd = (pos[0] & 1) == 1
    for g, group in enumerate(groups):
        if g < n - 1:
            whole.append(halves[g])
        else:
            half = halves[g].shape[0]
            whole.append(both[0])
            part_of(both[0], pos[2] & 1, half)[...] = halves[g][...]
            part_of(both[0], 1 - (pos[2] & 1), half)[...] = halves[g + 1][...]
        for i, e in enumerate(group):
            for t in range(WIDE // LANES):
                at = (t * len(group) + i) * SLICE
                tile = whole[g][at : at + SLICE, :]
                if t < D // LANES:
                    in_grad[e, :, t * LANES : (t + 1) * LANES] = tile
                else:
                    out_grad[e, :, t * LANES - D : (t + 1) * LANES - D] = tile
    rest = WIDE // LANES * len(groups[-1]) * SLICE
    sums = whole[-1][rest : rest + 24, :]
    sums = jnp.where(odd, sums[:, SLICE:], sums[:, :SLICE])
    for g, group in enumerate(groups):
        for i, e in enumerate(group):
            for k, ref in enumerate((in_bias, out_bias, gain, shift)):
                ref[e : e + 1, :] = sums[8 * g + 4 * i + k : 8 * g + 4 * i + k + 1, :]
    for t in range(D // LANES):
        gate[:, t * LANES : (t + 1) * LANES] = whole[-1][rest + 64 + 16 * t : rest + 64 + 16 * t + GATE_COLS, :]


def per_device(
    events,
    valid_counts,
    mix_cotangent,
    expert_in,
    expert_in_bias,
    expert_out,
    expert_out_bias,
    norm_gain,
    norm_shift,
    gate_weight,
):
    n_dp = lax.axis_size("dp")
    rank = lax.axis_index("dp")
    me = lax.axis_index("tp")
    rows = events.shape[0] // 2
    pos = jnp.stack([me, valid_counts[rank], rank]).astype(jnp.int32)
    w_in = jnp.swapaxes(expert_in, 1, 2)
    w_out = jnp.swapaxes(expert_out, 1, 2)
    gate_w = jnp.swapaxes(gate_weight, 0, 1)
    core = [(i, i ^ 1) for i in range(4)]
    across = [(i, i ^ 2) for i in range(4)]
    small = jnp.concatenate([expert_in_bias, expert_out_bias, norm_gain, norm_shift], axis=0)
    smalls = [small] + [lax.ppermute(small, "tp", [(i, i ^ k) for i in range(4)]) for k in range(1, 4)]
    own = [payload(GROUPS[0], w_in, w_out, [])]
    far = [lax.ppermute(own[0], "tp", across)]
    beside = [lax.ppermute(own[0], "tp", core)]
    relayed = []
    summing = []
    high, low, p = gates(pos, events, gate_w, rows, own)

    def between(deps, through=(), others=()):
        active = [r for r in summing if not r.finished]
        jobs = [r.job() for r in active] + list(others)
        fetched = len(relayed)
        fetching = fetched < len(far)
        if fetching:
            jobs.append(copy_job(far[fetched]))
        outs, through, token = run(pos, jobs, deps, through)
        if fetching:
            relayed.append(lax.ppermute(outs[-1][0], "tp", core))
        for r, o in zip(active, outs):
            r.take(o)
        if len(own) < len(GROUPS):
            own.append(payload(GROUPS[len(own)], w_in, w_out, [token]))
            far.append(lax.ppermute(own[-1], "tp", across))
            beside.append(lax.ppermute(own[-1], "tp", core))
            token = own[-1]
        return [token], through, outs[len(active) :]

    deps, _, outs = between([p], others=[copy_job(*smalls[1:])])
    smalls = smalls[:1] + outs[0]
    mix = x_grad = None
    dps, sums = [], []
    for g, group in enumerate(GROUPS):
        last = g == len(GROUPS) - 1
        shards = (own[g], beside[g], far[g], relayed[g])
        mix, dp, h, l, wh, wl, mine, part, s = experts(
            pos, group, rows, high, low, mix_cotangent, p, shards, smalls, mix, (dps, sums) if last else None, deps
        )
        dps.append(dp)
        sums.append(s)
        summing.append(Reduction(pos, *(([mine, s], [part, s]) if last else ([mine], [part])), n_dp))
        deps, _, _ = between([s])
        x_grad, token = event_grads(pos, rows, h, l, wh, wl, [dp, gate_w] if last else [], x_grad, deps)
        deps = [token]
    deps, (mix, x_grad), _ = between(deps, [mix, x_grad])
    other_mix, other_grad = lax.ppermute(mix, "tp", core), lax.ppermute(x_grad, "tp", core)
    deps, _, _ = between(deps)
    mixtures, token = place(pos, mix, other_mix, deps)
    deps, _, _ = between([token])
    x_grad, token = place(pos, x_grad, other_grad, deps)
    deps = [token]
    while summing[-1].stage < 2 * summing[-1].bits - 1:
        deps, _, _ = between(deps)
    halves = [r.keep for r in summing] + summing[-1].got
    per_expert = (E, SLICE)
    shapes = [(E, SLICE, D), per_expert, (E, SLICE, H), per_expert, per_expert, per_expert, (GATE_COLS, D)]
    scratch = [pltpu.VMEM((summing[-1].rows, LANES), F32)]
    job = Job(halves, shapes, functools.partial(finish_body, GROUPS), scratch)
    (((in_grad, in_bias, out_grad, out_bias, gain, shift, gate),), _, _) = run(pos, [job], deps)
    return (
        mixtures,
        x_grad,
        jnp.swapaxes(in_grad, 1, 2),
        in_bias,
        jnp.swapaxes(out_grad, 1, 2),
        out_bias,
        gain,
        shift,
        jnp.swapaxes(gate, 0, 1),
    )


def solution(mesh):
    return jax.shard_map(
        per_device,
        mesh=mesh,
        in_specs=(
            P("dp", None),
            P(),
            P("dp", None),
            P(None, None, "tp"),
            P(None, "tp"),
            P(None, None, "tp"),
            P(None, "tp"),
            P(None, "tp"),
            P(None, "tp"),
            P(),
        ),
        out_specs=(
            P("dp", None),
            P("dp", None),
            P(None, None, "tp"),
            P(None, "tp"),
            P(None, None, "tp"),
            P(None, "tp"),
            P(None, "tp"),
            P(None, "tp"),
            P(),
        ),
        check_vma=False,
    )
```

```python
import functools

import jax
import jax.numpy as jnp
from jax import lax
from jax.experimental import pallas as pl
from jax.experimental.pallas import tpu as pltpu
from jax.sharding import PartitionSpec as P

D = 512
H = 256
O = 256
E = 6
GATE_COLS = 14
SLICE = 64
WIDE = D + H
LANES = 128
TOKEN = (8, LANES)
RB = 512
ROW_BLOCK = 256
SUB = 256
LAG = 1
EPSILON = 1e-05
GROUPS = ((0,), (1, 2), (3, 4), (5,))
UNITS = ((0, 1), (2,), (3,))
COLUMN = (
    {0: 0, 1: 1, 4: 2, 5: 3},
    {2: 4, 3: 5, 4: 6, 5: 7},
    {e: 8 + e for e in range(E)},
)
F32 = jnp.float32
BF16 = jnp.bfloat16
NN = (((1,), (0,)), ((), ()))
NT = (((1,), (1,)), ((), ()))
TN = (((0,), (0,)), ((), ()))


def split(v):
    high = v.astype(BF16)
    return high, (v - high.astype(F32)).astype(BF16)


def dot3(a, b, dims):
    def one(u, v):
        return lax.dot_general(u, v, dims, preferred_element_type=F32)

    return one(a[0], b[0]) + (one(a[0], b[1]) + one(a[1], b[0]))


def half_of(v, upper):
    return jnp.where(upper, v[:, LANES:], v[:, :LANES])


LARGE = 60
EXPERT_MIB, EVENT_MIB, GATE_MIB, PAYLOAD_MIB, SMALL_MIB = 28, 16, 54, 62, 8


def params(mib):
    return pltpu.CompilerParams(vmem_limit_bytes=mib << 20)


def gate_kernel(n_deps, counts, ev_ref, cot_ref, gw_ref, *refs):
    high_ref, low_ref, p_ref, cot_out, gw, held, sems = refs[n_deps:]
    rows = held.shape[0]
    steps = rows // ROW_BLOCK
    start = pl.multiple_of((lax.axis_index("tp") & 1) * rows, ROW_BLOCK)
    valid = counts[lax.axis_index("dp")]
    blocks = [slice(i * ROW_BLOCK, (i + 1) * ROW_BLOCK) for i in range(steps)]
    copies = [
        pltpu.make_async_copy(ev_ref.at[pl.ds(start + at.start, ROW_BLOCK), :], held.at[at, :], sems.at[i])
        for i, at in enumerate(blocks)
    ]
    copies.append(pltpu.make_async_copy(cot_ref.at[pl.ds(start, rows), :], cot_out, sems.at[steps]))
    for copy in copies:
        copy.start()
    gw[...] = jnp.zeros_like(gw)
    gw[:GATE_COLS, :] = gw_ref[...]
    gate = split(gw[...])
    lane = lax.broadcasted_iota(jnp.int32, (ROW_BLOCK, LANES), 1)
    sets = (lane < 4, (lane >= 4) & (lane < 8), (lane >= 8) & (lane < GATE_COLS))

    def per_set(values, empty, reduce):
        a, b, s = (reduce(jnp.where(m, values, empty), axis=1, keepdims=True) for m in sets)
        return jnp.where(sets[0], a, jnp.where(sets[1], b, s))

    for i, at in enumerate(blocks):
        copies[i].wait()
        events = split(held[at, :])
        high_ref[at, :], low_ref[at, :] = events
        logits = dot3(events, gate, NT)
        top = per_set(logits, -3e38, jnp.max)
        shares = jnp.where(lane < GATE_COLS, jnp.exp(logits - top), 0.0)
        p = shares / per_set(shares, 0.0, jnp.sum)
        row = start + at.start + lax.broadcasted_iota(jnp.int32, logits.shape, 0)
        p_ref[at, :] = jnp.where((row < valid) & (lane < GATE_COLS), p, 0.0)
    copies[-1].wait()


def gates(counts, events, cot, gate_w, rows, deps):
    vmem, hbm = pl.BlockSpec(memory_space=pltpu.VMEM), pl.BlockSpec(memory_space=pltpu.HBM)
    steps = rows // ROW_BLOCK
    return pl.pallas_call(
        functools.partial(gate_kernel, len(deps)),
        in_specs=[pl.BlockSpec(memory_space=pltpu.SMEM), hbm, hbm, vmem]
        + [pl.BlockSpec(memory_space=pl.ANY)] * len(deps),
        out_specs=[vmem] * 4,
        out_shape=[
            jax.ShapeDtypeStruct((rows, D), BF16),
            jax.ShapeDtypeStruct((rows, D), BF16),
            jax.ShapeDtypeStruct((rows, LANES), F32),
            jax.ShapeDtypeStruct((rows, 3 * O), F32),
        ],
        scratch_shapes=[
            pltpu.VMEM((LANES, D), F32),
            pltpu.VMEM((rows, D), F32),
            pltpu.SemaphoreType.DMA((steps + 1,)),
        ],
        compiler_params=params(GATE_MIB),
        cost_estimate=pl.CostEstimate(flops=6 * rows * D * LANES, bytes_accessed=rows * D * 8, transcendentals=0),
    )(counts, events, cot, gate_w, *deps)


def payload_kernel(groups, vectors, n_deps, w_in, w_out, *refs):
    given = refs[:4] if vectors else ()
    outs, sems = refs[len(given) + n_deps :][: len(groups)], refs[-1]
    copies = []
    for out, group in zip(outs, groups):
        experts_of, rows = pl.ds(group[0], len(group)), slice(0, SLICE)
        for part, lanes in ((w_in, slice(0, D)), (w_out, slice(D, WIDE))):
            copies.append(pltpu.make_async_copy(part.at[experts_of], out.at[:, rows, lanes], sems.at[len(copies)]))
    for copy in copies:
        copy.start()
    if vectors:
        held = refs[-2]
        for k, v in enumerate(given):
            held[k * E : (k + 1) * E, :] = v[...]
        outs[0][:, SLICE:, :] = jnp.zeros((len(groups[0]), 8, WIDE), F32)
        for j in range(4 * E // 8):
            outs[0][0, SLICE:, j * LANES : j * LANES + SLICE] = held[8 * j : 8 * j + 8, :]
    for copy in copies:
        copy.wait()


def payload(groups, w_in, w_out, vectors, deps):
    vmem, hbm = pl.BlockSpec(memory_space=pltpu.VMEM), pl.BlockSpec(memory_space=pltpu.HBM)
    rows = SLICE + 8 if vectors else SLICE
    return pl.pallas_call(
        functools.partial(payload_kernel, groups, bool(vectors), len(deps)),
        in_specs=[hbm, hbm] + [vmem] * len(vectors) + [pl.BlockSpec(memory_space=pl.ANY)] * len(deps),
        out_specs=[vmem] * len(groups),
        out_shape=[jax.ShapeDtypeStruct((len(group), rows, WIDE), F32) for group in groups],
        scratch_shapes=[pltpu.VMEM((4 * E, SLICE), F32), pltpu.SemaphoreType.DMA((2 * len(groups),))],
        compiler_params=params(PAYLOAD_MIB),
        cost_estimate=pl.CostEstimate(flops=0, bytes_accessed=SLICE * WIDE * 16, transcendentals=0),
    )(w_in, w_out, *vectors, *deps)


def expert_kernel(group, first, last, n_deps, *refs):
    n = len(group)
    refs = list(refs)
    evh_ref, evl_ref, cot_ref, p_ref = refs[:4]
    shards = refs[4:8]
    del refs[:8]
    small = None if first else refs.pop(0)
    mix_in = None if first else refs.pop(0)
    if last:
        dp_before, sums_before = refs[: len(GROUPS) - 1], refs[len(GROUPS) - 1 : 2 * len(GROUPS) - 2]
        del refs[: 2 * len(GROUPS) - 2]
    del refs[:n_deps]
    mix_ref, dp_ref, dph_ref, dpl_ref, winh, winl, own_ref, part_ref, sums_ref = refs[:9]
    del refs[:9]
    if first:
        small = refs.pop(0)
    wouth, woutl, acc, sums = refs[:4]
    gate_acc = refs[4] if last else None
    step, steps = pl.program_id(0), pl.num_programs(0)
    odd = lax.axis_index("tp") & 1
    chip = lax.axis_index("tp") >> 1

    def tile(start, other):
        return pl.ds(pl.multiple_of(start + (chip ^ other) * LANES, LANES), LANES)

    @pl.when(step == 0)
    def _():
        acc[...] = jnp.zeros_like(acc)
        sums[...] = jnp.zeros_like(sums)
        if last:
            gate_acc[...] = jnp.zeros_like(gate_acc)
        for j in range(4 * E // 8 if first else 0):
            vectors = [shard[0, SLICE:, j * LANES : j * LANES + SLICE] for shard in shards]
            even_order, odd_order = (jnp.concatenate([vectors[k ^ c] for k in range(4)], axis=1) for c in range(2))
            small[8 * j : 8 * j + 8, :] = jnp.where(odd == 1, odd_order, even_order)
        if first:
            bias = small[E : 2 * E, :]
            small[E : 2 * E, :] = bias - jnp.mean(bias, axis=1, keepdims=True)
        own_rows = slice(0, SLICE)
        for i, e in enumerate(group):
            parts = [
                (shard[i, own_rows, :D], jnp.concatenate([shard[i, own_rows, tile(D, k)] for k in range(2)], axis=1))
                for shard in shards
            ]
            centre = sum(jnp.sum(out, axis=0, keepdims=True) for _, out in parts) / O
            for k, (into, out) in enumerate(parts):
                at = pl.multiple_of((odd ^ k) * SLICE, SLICE)
                winh[pl.ds(i * H + at, SLICE), :], winl[pl.ds(i * H + at, SLICE), :] = split(into)
                wouth[i, pl.ds(at, SLICE), :], woutl[i, pl.ds(at, SLICE), :] = split(out - centre)

    subs = RB // SUB
    rows_of = [slice(s * SUB, (s + 1) * SUB) for s in range(subs)]
    lane = lax.broadcasted_iota(jnp.int32, (SUB, LANES), 1)
    vector = lambda k, e: small[k * E + e : k * E + e + 1, :]
    state = [dict() for _ in range(subs)]

    def m1(s):
        events = evh_ref[rows_of[s], :], evl_ref[rows_of[s], :]
        state[s]["events"] = events
        pre = dot3(events, (winh[...], winl[...]), NT)
        state[s]["pre"] = [pre[:, i * H : (i + 1) * H] for i in range(n)]

    def v1(s):
        st = state[s]
        st["sigma"], st["hidden"], st["hidden_parts"] = [], [], []
        for i, e in enumerate(group):
            pre = st["pre"][i] + vector(0, e)
            sigma = jax.nn.sigmoid(pre)
            hidden = pre * sigma
            st["sigma"].append(sigma)
            st["hidden"].append(hidden)
            st["hidden_parts"].append(split(hidden))

    def m2(s):
        st = state[s]
        st["centred"] = [dot3(st["hidden_parts"][i], (wouth[i], woutl[i]), NT) for i in range(n)]

    def v2(s):
        st = state[s]
        p = p_ref[rows_of[s], :]
        dp = jnp.zeros_like(p)
        mixed = {}
        cots = [
            jnp.concatenate([cot_ref[rows_of[s], tile(t * O, 0)], cot_ref[rows_of[s], tile(t * O, 1)]], axis=1)
            for t in range(3)
        ]
        st["dnormed"] = []
        for i, e in enumerate(group):
            gain, shift = vector(2, e), vector(3, e)
            centred = st["centred"][i] + vector(1, e)
            rstd = lax.rsqrt(jnp.mean(centred * centred, axis=1, keepdims=True) + EPSILON)
            unit = centred * rstd
            y = unit * gain + shift
            dy = None
            for t in range(3):
                if e not in COLUMN[t]:
                    continue
                column = COLUMN[t][e]
                coef = p[:, column : column + 1]
                mixed[t] = coef * y + mixed[t] if t in mixed else coef * y
                dp = jnp.where(lane == column, jnp.sum(cots[t] * y, axis=1, keepdims=True), dp)
                dy = coef * cots[t] if dy is None else dy + coef * cots[t]
            dunit = dy * gain
            back_first = jnp.mean(dunit, axis=1, keepdims=True)
            back_second = jnp.mean(dunit * unit, axis=1, keepdims=True)
            dnormed = rstd * (dunit - back_first - unit * back_second)
            st["dnormed"].append(split(dnormed))
            dy_half = dy[:, :LANES]
            for k, v in enumerate((dnormed[:, :LANES], dy_half * unit[:, :LANES], dy_half)):
                sums[4 * i + k + 1 : 4 * i + k + 2, :] += jnp.sum(v, axis=0, keepdims=True)
        for t in range(3):
            for other in range(2):
                at = tile(t * O, other)
                if t in mixed:
                    value = mixed[t][:, other * LANES : (other + 1) * LANES]
                    mix_ref[rows_of[s], at] = value if first else mix_in[rows_of[s], at] + value
                elif first:
                    mix_ref[rows_of[s], at] = jnp.zeros((SUB, LANES), F32)
                else:
                    mix_ref[rows_of[s], at] = mix_in[rows_of[s], at]
        if last:
            for other in dp_before:
                dp = dp + other[rows_of[s], :]
            weighted = p * dp
            sets = (lane < 4, (lane >= 4) & (lane < 8), (lane >= 8) & (lane < GATE_COLS))
            a, b, c = (jnp.sum(jnp.where(m, weighted, 0.0), axis=1, keepdims=True) for m in sets)
            dp = weighted - p * jnp.where(sets[0], a, jnp.where(sets[1], b, c))
            st["dlogits"] = dp
        dp_ref[rows_of[s], :] = dp

    def m3(s):
        st = state[s]
        st["dhidden"] = [dot3(st["dnormed"][i], (wouth[i], woutl[i]), NN) for i in range(n)]

    def v3(s):
        st = state[s]
        st["dpre"] = []
        for i, e in enumerate(group):
            sigma, hidden = st["sigma"][i], st["hidden"][i]
            dpre = st["dhidden"][i] * (sigma + hidden * (1.0 - sigma))
            parts = split(dpre)
            dph_ref[rows_of[s], i * H : (i + 1) * H], dpl_ref[rows_of[s], i * H : (i + 1) * H] = parts
            st["dpre"].append(tuple(v[:, :LANES] for v in parts))
            sums[4 * i : 4 * i + 1, :] += jnp.sum(dpre[:, :LANES], axis=0, keepdims=True)

    def m4(s):
        st = state[s]
        for i in range(n):
            halves = tuple(v[:, :LANES] for v in st["dnormed"][i])
            acc[i * LANES : (i + 1) * LANES, D:] += dot3(halves, st["hidden_parts"][i], TN)
        beside = [split(st["dlogits"])] if last else []
        left = tuple(jnp.concatenate([h[k] for h in st["dpre"] + beside], axis=1) for k in range(2))
        both = dot3(left, st["events"], TN)
        acc[:, :D] += both[: n * LANES]
        if last:
            gate_acc[...] += both[n * LANES : n * LANES + 16]

    stages = (m1, v1, m2, v2, m3, v3, m4)
    for turn in range(len(stages) + LAG * (subs - 1)):
        for s in range(subs):
            if 0 <= turn - LAG * s < len(stages):
                stages[turn - LAG * s](s)

    @pl.when(step == steps - 1)
    def _():
        mine = pl.multiple_of(odd * SLICE, SLICE)
        other = pl.multiple_of(SLICE - mine, SLICE)
        for i in range(n):
            for t in range(WIDE // LANES):
                at = slice((t * n + i) * SLICE, (t * n + i + 1) * SLICE)
                lanes = slice(t * LANES, (t + 1) * LANES) if t < D // LANES else tile(D, t - D // LANES)
                own_ref[at, :] = acc[pl.ds(i * LANES + mine, SLICE), lanes]
                part_ref[at, :] = acc[pl.ds(i * LANES + other, SLICE), lanes]
        if last:
            sums_ref[...] = jnp.zeros_like(sums_ref)
            for g, before in enumerate(sums_before):
                sums_ref[8 * g : 8 * g + 8, :] = before[...]
            g = len(GROUPS) - 1
            sums_ref[8 * g : 8 * g + 8, :] = sums[...]
            for t in range(D // LANES):
                sums_ref[64 + 16 * t : 80 + 16 * t, :] = gate_acc[:, t * LANES : (t + 1) * LANES]
        else:
            sums_ref[...] = sums[...]


def experts(group, rows, high, low, cot, p, shards, small, mix, before, deps):
    n = len(group)
    first, last = mix is None, before is not None
    steps = rows // RB
    block = lambda width: pl.BlockSpec((RB, width), lambda i: (i, 0))
    whole = lambda shape: pl.BlockSpec(shape, lambda i: (0,) * len(shape))
    in_specs = [
        block(D),
        block(D),
        block(3 * O),
        block(LANES),
        *[whole(shards[0].shape)] * 4,
    ]
    args = [high, low, cot, p, *shards]
    aliases = {}
    if not first:
        aliases = {len(args) + 1: 0}
        in_specs += [whole((4 * E, H)), block(3 * O)]
        args += [small, mix]
    if last:
        in_specs += [block(LANES)] * len(before[0]) + [whole((8, LANES))] * len(before[1])
        args += [*before[0], *before[1]]
    in_specs += [pl.BlockSpec(memory_space=pl.ANY)] * len(deps)
    args += deps
    payload = WIDE // LANES * n * SLICE
    sums_shape = (2 * LANES // 2, LANES) if last else (8, LANES)
    scratch = [
        pltpu.VMEM((n, O, H), BF16),
        pltpu.VMEM((n, O, H), BF16),
        pltpu.VMEM((n * LANES, WIDE), F32),
        pltpu.VMEM((8, LANES), F32),
    ]
    if last:
        scratch.append(pltpu.VMEM((16, D), F32))
    return pl.pallas_call(
        functools.partial(expert_kernel, group, first, last, len(deps)),
        grid=(steps,),
        in_specs=in_specs,
        out_specs=[
                block(3 * O),
                block(LANES),
                block(n * H),
                block(n * H),
                whole((n * H, D)),
                whole((n * H, D)),
                whole((payload, LANES)),
                whole((payload, LANES)),
                whole(sums_shape),
        ]
        + [whole((4 * E, H))] * first,
        scratch_shapes=scratch,
        out_shape=[
            jax.ShapeDtypeStruct((rows, 3 * O), F32),
            jax.ShapeDtypeStruct((rows, LANES), F32),
            jax.ShapeDtypeStruct((rows, n * H), BF16),
            jax.ShapeDtypeStruct((rows, n * H), BF16),
            jax.ShapeDtypeStruct((n * H, D), BF16),
            jax.ShapeDtypeStruct((n * H, D), BF16),
            jax.ShapeDtypeStruct((payload, LANES), F32),
            jax.ShapeDtypeStruct((payload, LANES), F32),
            jax.ShapeDtypeStruct(sums_shape, F32),
        ]
        + [jax.ShapeDtypeStruct((4 * E, H), F32)] * first,
        input_output_aliases=aliases,
        compiler_params=params(EXPERT_MIB),
        cost_estimate=pl.CostEstimate(flops=n * rows * 6 * 720896, bytes_accessed=rows * 14000, transcendentals=0),
    )(*args)


def event_kernel(n, *refs):
    highs, lows, winh, winl = (refs[k * n : (k + 1) * n] for k in range(4))
    dlogits, gw_ref = refs[4 * n : 4 * n + 2]
    out, token, gw = refs[-3:]
    gw[...] = jnp.zeros_like(gw)
    gw[:GATE_COLS, :] = gw_ref[...]
    total = dot3(split(dlogits[...]), split(gw[...]), NN)
    for g in range(n):
        total = total + dot3((highs[g][...], lows[g][...]), (winh[g][...], winl[g][...]), NN)
    out[...] = total
    token[...] = jnp.zeros_like(token)


def event_grads(rows, highs, lows, winh, winl, dlogits, gate_w, deps):
    block = lambda width: pl.BlockSpec((ROW_BLOCK, width), lambda i: (i, 0))
    whole = lambda shape: pl.BlockSpec(shape, lambda i: (0, 0))
    return pl.pallas_call(
        functools.partial(event_kernel, len(highs)),
        grid=(rows // ROW_BLOCK,),
        in_specs=[block(v.shape[1]) for v in (*highs, *lows)]
        + [whole(v.shape) for v in (*winh, *winl)]
        + [block(LANES), whole((GATE_COLS, D))]
        + [pl.BlockSpec(memory_space=pl.ANY)] * len(deps),
        out_specs=[block(D), whole(TOKEN)],
        scratch_shapes=[pltpu.VMEM((LANES, D), F32)],
        out_shape=[jax.ShapeDtypeStruct((rows, D), F32), jax.ShapeDtypeStruct(TOKEN, F32)],
        compiler_params=params(EVENT_MIB),
        cost_estimate=pl.CostEstimate(flops=6 * rows * D * E * H, bytes_accessed=rows * 10000, transcendentals=0),
    )(*highs, *lows, *winh, *winl, dlogits, gate_w, *deps)


def place_kernel(own, other, *refs):
    out, token, sems = refs[-3:]
    rows = own.shape[0]
    side = lax.axis_index("tp") & 1
    copies = [
        pltpu.make_async_copy(v, out.at[pl.ds(pl.multiple_of(at * rows, ROW_BLOCK), rows), :], sems.at[k])
        for k, (v, at) in enumerate(((own, side), (other, 1 - side)))
    ]
    for copy in copies:
        copy.start()
    token[...] = jnp.zeros_like(token)
    for copy in copies:
        copy.wait()


def place(own, other, deps):
    rows, width = own.shape
    anywhere = pl.BlockSpec(memory_space=pl.ANY)
    return pl.pallas_call(
        place_kernel,
        in_specs=[anywhere] * (2 + len(deps)),
        out_specs=[pl.BlockSpec(memory_space=pltpu.HBM), pl.BlockSpec(memory_space=pltpu.VMEM)],
        scratch_shapes=[pltpu.SemaphoreType.DMA((2,))],
        out_shape=[jax.ShapeDtypeStruct((2 * rows, width), F32), jax.ShapeDtypeStruct(TOKEN, F32)],
        compiler_params=params(SMALL_MIB),
        cost_estimate=pl.CostEstimate(flops=0, bytes_accessed=rows * width * 16, transcendentals=0),
    )(own, other, *deps)


class Job:
    def __init__(self, args, shapes, body, scratch=()):
        self.args, self.body, self.scratch = args, body, list(scratch)
        self.shapes = [jax.ShapeDtypeStruct(shape, F32) for shape in shapes]


def copy_job(*arrays):
    def body(ins, outs, scratch):
        for a, b in zip(ins, outs):
            b[...] = a[...]

    return Job(arrays, [a.shape for a in arrays], body)


def run(jobs, deps=(), through=()):
    args = [a for job in jobs for a in job.args]
    shapes = [o for job in jobs for o in job.shapes]
    scratch = [v for job in jobs for v in job.scratch]

    def kernel(*refs):
        ins, refs = refs[: len(args)], refs[len(args) + len(through) + len(deps) :]
        outs, token, kept = refs[: len(shapes)], refs[len(shapes) + len(through)], refs[len(shapes) + len(through) + 1 :]
        token[...] = jnp.zeros_like(token)
        i = o = k = 0
        for job in jobs:
            ni, no, nk = len(job.args), len(job.shapes), len(job.scratch)
            job.body(ins[i : i + ni], outs[o : o + no], kept[k : k + nk])
            i, o, k = i + ni, o + no, k + nk

    vmem, anywhere = pl.BlockSpec(memory_space=pltpu.VMEM), pl.BlockSpec(memory_space=pl.ANY)
    flat = pl.pallas_call(
        kernel,
        in_specs=[vmem] * len(args) + [anywhere] * (len(through) + len(deps)),
        out_specs=[vmem] * len(shapes) + [anywhere] * len(through) + [vmem],
        out_shape=shapes
        + [jax.ShapeDtypeStruct(v.shape, v.dtype) for v in through]
        + [jax.ShapeDtypeStruct(TOKEN, F32)],
        scratch_shapes=scratch,
        input_output_aliases={len(args) + k: len(shapes) + k for k in range(len(through))},
        compiler_params=params(SMALL_MIB),
        cost_estimate=pl.CostEstimate(flops=0, bytes_accessed=sum(8 * a.size for a in args), transcendentals=0),
    )(*args, *through, *deps)
    result = []
    for job in jobs:
        result.append(list(flat[: len(job.shapes)]))
        flat = flat[len(job.shapes) :]
    return result, list(flat[:-1]), flat[-1]


def part_of(ref, index, rows):
    return ref.at[pl.ds(pl.multiple_of(index * rows, 8), rows), :]


class Reduction:
    def __init__(self, own, got, n_dp):
        self.own, self.got = own, got
        self.bits = n_dp.bit_length() - 1
        unit = 8 << (self.bits - 1)
        self.rows = -(-sum(v.shape[0] for v in own) // unit) * unit
        self.swap = [[(i, i ^ (1 << b)) for i in range(n_dp)] for b in range(self.bits)]
        self.stage = 0

    def over(self, values, bit):
        return [lax.ppermute(v, "dp", self.swap[bit]) for v in values]

    @property
    def finished(self):
        return self.stage == 2 * self.bits

    def job(self):
        stage, bits = self.stage, self.bits
        if stage == 0:
            args = [*self.own, *self.got]
            rows = self.rows
        elif stage <= bits:
            args = [self.keep, *self.got]
            rows = self.keep.shape[0]
        else:
            args = [self.keep, *self.got]
            rows = 2 * self.keep.shape[0]
        n = len(args) // 2
        gather = stage > bits
        bit = stage if stage < bits else 2 * bits - 1 - stage
        halving = stage < bits - 1

        def body(ins, outs, scratch):
            to = scratch[0] if halving else outs[0]
            if gather:
                side = (lax.axis_index("dp") >> bit) & 1
                part_of(to, side, rows // 2)[...] = ins[0][...]
                part_of(to, 1 - side, rows // 2)[...] = ins[1][...]
                return
            at = 0
            for a, b in zip(ins[:n], ins[n:]):
                to[at : at + a.shape[0], :] = a[...] + b[...]
                at += a.shape[0]
            if at < rows:
                to[at:, :] = jnp.zeros((rows - at, LANES), F32)
            if halving:
                side = (lax.axis_index("dp") >> bit) & 1
                outs[0][...] = part_of(to, side, rows // 2)[...]
                outs[1][...] = part_of(to, 1 - side, rows // 2)[...]

        if halving:
            return Job(args, [(rows // 2, LANES)] * 2, body, [pltpu.VMEM((rows, LANES), F32)])
        return Job(args, [(rows, LANES)], body)

    def take(self, outs):
        stage, bits = self.stage, self.bits
        self.keep = outs[0]
        bit = stage if stage < bits else 2 * bits - 2 - stage
        if bit >= 0:
            self.got = self.over([outs[-1]], bit)
        self.stage += 1


def finish_body(ins, outs, both):
    in_grad, in_bias, out_grad, out_bias, gain, shift, gate = outs
    odd = (lax.axis_index("tp") & 1) == 1
    side = lax.axis_index("dp") & 1
    whole = list(ins[:-2])
    half = ins[-1].shape[0]
    part_of(both[0], side, half)[...] = ins[-2][...]
    part_of(both[0], 1 - side, half)[...] = ins[-1][...]
    whole.append(both[0])
    for u, unit in enumerate(UNITS):
        at = 0
        for g in unit:
            group = GROUPS[g]
            for t in range(WIDE // LANES):
                for e in group:
                    tile = whole[u][at : at + SLICE, :]
                    at += SLICE
                    if t < D // LANES:
                        in_grad[e, :, t * LANES : (t + 1) * LANES] = tile
                    else:
                        out_grad[e, :, t * LANES - D : (t + 1) * LANES - D] = tile
    sums = whole[-1][at : at + 8 * len(GROUPS), :]
    sums = jnp.where(odd, sums[:, SLICE:], sums[:, :SLICE])
    for g, group in enumerate(GROUPS):
        for i, e in enumerate(group):
            for k, ref in enumerate((in_bias, out_bias, gain, shift)):
                ref[e : e + 1, :] = sums[8 * g + 4 * i + k : 8 * g + 4 * i + k + 1, :]
    for t in range(D // LANES):
        gate[:, t * LANES : (t + 1) * LANES] = whole[-1][at + 64 + 16 * t : at + 64 + 16 * t + GATE_COLS, :]


def per_device(
    events,
    valid_counts,
    mix_cotangent,
    expert_in,
    expert_in_bias,
    expert_out,
    expert_out_bias,
    norm_gain,
    norm_shift,
    gate_weight,
):
    n_dp = lax.axis_size("dp")
    rows = events.shape[0] // 2
    w_in = jnp.swapaxes(expert_in, 1, 2)
    w_out = jnp.swapaxes(expert_out, 1, 2)
    gate_w = jnp.swapaxes(gate_weight, 0, 1)
    core = [(i, i ^ 1) for i in range(4)]
    across = [(i, i ^ 2) for i in range(4)]
    vectors = [expert_in_bias, expert_out_bias, norm_gain, norm_shift]
    own = list(payload(GROUPS[:1], w_in, w_out, vectors, []))
    far = [lax.ppermute(own[0], "tp", across)]
    beside = [lax.ppermute(own[0], "tp", core)]
    own += payload(GROUPS[1:], w_in, w_out, [], own)
    high, low, p, cot = gates(valid_counts, events, mix_cotangent, gate_w, rows, own[1:2])
    relayed = []
    summing = []
    partial = []

    def between(deps, through=(), sent=()):
        for unit in UNITS[len(summing) :]:
            if unit[-1] < len(partial):
                both = [partial[g] for g in unit]
                summing.append(Reduction([v for b in both for v in b[0]], [v for b in both for v in b[1]], n_dp))
        active = [r for r in summing if not r.finished]
        jobs = [r.job() for r in active] + [copy_job(*sent)]
        fetched = len(relayed)
        fetching = fetched < len(far)
        if fetching:
            jobs.append(copy_job(far[fetched], *own[fetched + 1 : fetched + 2]))
        outs, through, token = run(jobs, deps, through)
        if fetching:
            relayed.append(lax.ppermute(outs[-1][0], "tp", core))
            if len(outs[-1]) > 1:
                far.append(lax.ppermute(outs[-1][1], "tp", across))
                beside.append(lax.ppermute(outs[-1][1], "tp", core))
        for r, o in zip(active, outs):
            r.take(o)
        return [token], through, [lax.ppermute(v, "tp", core) for v in outs[len(active)]]

    deps, _, _ = between([p])
    mix = small = None
    dps, sums, highs, lows, winh, winl = [], [], [], [], [], []
    for g, group in enumerate(GROUPS):
        last = g == len(GROUPS) - 1
        shards = (own[g], beside[g], far[g], relayed[g])
        mix, dp, h, l, wh, wl, mine, part, s, *made = experts(
            group, rows, high, low, cot, p, shards, small, mix, (dps, sums) if last else None, deps
        )
        small = made[0] if made else small
        for held, v in zip((dps, sums, highs, lows, winh, winl), (dp, s, h, l, wh, wl)):
            held.append(v)
        extra = [s] if last else []
        deps, _, got = between([s], sent=[part, *extra])
        partial.append(([mine, *extra], got))
    deps, (mix,), _ = between(deps, [mix])
    other_mix = lax.ppermute(mix, "tp", core)
    x_grad, token = event_grads(rows, highs, lows, winh, winl, dps[-1], gate_w, deps)
    deps, (x_grad,), _ = between([token], [x_grad])
    other_grad = lax.ppermute(x_grad, "tp", core)
    mixtures, token = place(mix, other_mix, deps)
    deps, _, _ = between([token])
    x_grad, token = place(x_grad, other_grad, deps)
    deps = [token]
    while summing[-1].stage < 2 * summing[-1].bits - 1:
        deps, _, _ = between(deps)
    halves = [r.keep for r in summing] + summing[-1].got
    per_expert = (E, SLICE)
    shapes = [(E, SLICE, D), per_expert, (E, SLICE, H), per_expert, per_expert, per_expert, (GATE_COLS, D)]
    scratch = [pltpu.VMEM((summing[-1].rows, LANES), F32)]
    job = Job(halves, shapes, finish_body, scratch)
    (((in_grad, in_bias, out_grad, out_bias, gain, shift, gate),), _, _) = run([job], deps)
    return (
        mixtures,
        x_grad,
        jnp.swapaxes(in_grad, 1, 2),
        in_bias,
        jnp.swapaxes(out_grad, 1, 2),
        out_bias,
        gain,
        shift,
        jnp.swapaxes(gate, 0, 1),
    )


def solution(mesh):
    return jax.shard_map(
        per_device,
        mesh=mesh,
        in_specs=(
            P("dp", None),
            P(),
            P("dp", None),
            P(None, None, "tp"),
            P(None, "tp"),
            P(None, None, "tp"),
            P(None, "tp"),
            P(None, "tp"),
            P(None, "tp"),
            P(),
        ),
        out_specs=(
            P("dp", None),
            P("dp", None),
            P(None, None, "tp"),
            P(None, "tp"),
            P(None, None, "tp"),
            P(None, "tp"),
            P(None, "tp"),
            P(None, "tp"),
            P(),
        ),
        check_vma=False,
    )
```

```python
import functools

import jax
import jax.numpy as jnp
from jax import lax
from jax.experimental import pallas as pl
from jax.experimental.pallas import tpu as pltpu
from jax.sharding import PartitionSpec as P

D = 512
H = 256
O = 256
E = 6
GATE_COLS = 14
SLICE = 64
WIDE = D + H
LANES = 128
TOKEN = (8, LANES)
RB = 512
ROW_BLOCK = 256
SUB = 256
LAG = 1
EPSILON = 1e-05
GROUPS = ((0, 1), (2, 3), (4,), (5,))
UNITS = ((0,), (1,), (2, 3))
WIDTH = (1, 1, 2)
PLAN = (
    ("small", "fetch", ()),
    ("experts", 0, ()),
    ("small", "send", ()),
    ("events", (0,), ()),
    ("small", "fetch", (0,)),
    ("experts", 1, ()),
    ("small", "send fetch", (0,)),
    ("events", (1,), ()),
    ("small", "", (1,)),
    ("experts", 2, ()),
    ("small", "send fetch", (0, 1)),
    ("experts", 3, ()),
    ("small", "send", (0, 1)),
    ("events", (2,), ()),
    ("small", "mix", (2,)),
    ("events", (3,), ()),
    ("small", "grad", (0, 1, 2)),
    ("place", None, ()),
    ("small", "", (0, 1, 2)),
    ("place", None, ()),
)
COLUMN = (
    {0: 0, 1: 1, 4: 2, 5: 3},
    {2: 4, 3: 5, 4: 6, 5: 7},
    {e: 8 + e for e in range(E)},
)
F32 = jnp.float32
BF16 = jnp.bfloat16
NN = (((1,), (0,)), ((), ()))
NT = (((1,), (1,)), ((), ()))
TN = (((0,), (0,)), ((), ()))


def split(v):
    high = v.astype(BF16)
    return high, (v - high.astype(F32)).astype(BF16)


def dot3(a, b, dims):
    def one(u, v):
        return lax.dot_general(u, v, dims, preferred_element_type=F32)

    return one(a[0], b[0]) + (one(a[0], b[1]) + one(a[1], b[0]))


def in_hbm(v):
    return pltpu.with_memory_space_constraint(v, pltpu.HBM)


LARGE = 60
EXPERT_MIB, EVENT_MIB, GATE_MIB, SMALL_MIB = 28, 16, 16, 8


def params(mib):
    return pltpu.CompilerParams(vmem_limit_bytes=mib << 20)


def gate_kernel(n_deps, counts, ev_ref, cot_ref, gw_ref, *refs):
    high_ref, low_ref, p_ref, cot_out, gw, held, sems = refs[n_deps:]
    rows = held.shape[0]
    steps = rows // ROW_BLOCK
    start = pl.multiple_of((lax.axis_index("tp") & 1) * rows, ROW_BLOCK)
    valid = counts[lax.axis_index("dp")]
    blocks = [slice(i * ROW_BLOCK, (i + 1) * ROW_BLOCK) for i in range(steps)]
    copies = [
        pltpu.make_async_copy(ev_ref.at[pl.ds(start + at.start, ROW_BLOCK), :], held.at[at, :], sems.at[i])
        for i, at in enumerate(blocks)
    ]
    copies.append(pltpu.make_async_copy(cot_ref.at[pl.ds(start, rows), :], cot_out, sems.at[steps]))
    for copy in copies:
        copy.start()
    gw[...] = jnp.zeros_like(gw)
    gw[:GATE_COLS, :] = gw_ref[...]
    gate = split(gw[...])
    lane = lax.broadcasted_iota(jnp.int32, (ROW_BLOCK, LANES), 1)
    sets = (lane < 4, (lane >= 4) & (lane < 8), (lane >= 8) & (lane < GATE_COLS))

    def per_set(values, empty, reduce):
        a, b, s = (reduce(jnp.where(m, values, empty), axis=1, keepdims=True) for m in sets)
        return jnp.where(sets[0], a, jnp.where(sets[1], b, s))

    for i, at in enumerate(blocks):
        copies[i].wait()
        events = split(held[at, :])
        high_ref[at, :], low_ref[at, :] = events
        logits = dot3(events, gate, NT)
        top = per_set(logits, -3e38, jnp.max)
        shares = jnp.where(lane < GATE_COLS, jnp.exp(logits - top), 0.0)
        p = shares / per_set(shares, 0.0, jnp.sum)
        row = start + at.start + lax.broadcasted_iota(jnp.int32, logits.shape, 0)
        p_ref[at, :] = jnp.where((row < valid) & (lane < GATE_COLS), p, 0.0)
    copies[-1].wait()


def gates(counts, events, cot, gate_w, rows, deps):
    vmem, hbm = pl.BlockSpec(memory_space=pltpu.VMEM), pl.BlockSpec(memory_space=pltpu.HBM)
    steps = rows // ROW_BLOCK
    return pl.pallas_call(
        functools.partial(gate_kernel, len(deps)),
        in_specs=[pl.BlockSpec(memory_space=pltpu.SMEM), hbm, hbm, vmem]
        + [pl.BlockSpec(memory_space=pl.ANY)] * len(deps),
        out_specs=[vmem] * 4,
        out_shape=[
            pltpu.VMEM((rows, D), BF16),
            pltpu.VMEM((rows, D), BF16),
            pltpu.VMEM((rows, LANES), F32),
            pltpu.VMEM((rows, 3 * O), F32),
        ],
        scratch_shapes=[
            pltpu.VMEM((LANES, D), F32),
            pltpu.VMEM((rows, D), F32),
            pltpu.SemaphoreType.DMA((steps + 1,)),
        ],
        compiler_params=params(GATE_MIB),
        cost_estimate=pl.CostEstimate(flops=6 * rows * D * LANES, bytes_accessed=rows * D * 8, transcendentals=0),
    )(counts, in_hbm(events), in_hbm(cot), in_hbm(gate_w), *deps)


def payload_kernel(groups, vectors, n_deps, w_in, w_out, *refs):
    given = refs[:4] if vectors else ()
    outs, sems = refs[len(given) + n_deps :][: len(groups)], refs[-1]
    copies = []
    for out, group in zip(outs, groups):
        experts_of, rows = pl.ds(group[0], len(group)), slice(0, SLICE)
        for part, lanes in ((w_in, slice(0, D)), (w_out, slice(D, WIDE))):
            copies.append(pltpu.make_async_copy(part.at[experts_of], out.at[:, rows, lanes], sems.at[len(copies)]))
    for copy in copies:
        copy.start()
    if vectors:
        held = refs[-2]
        for k, v in enumerate(given):
            held[k * E : (k + 1) * E, :] = v[...]
        outs[0][:, SLICE:, :] = jnp.zeros((len(groups[0]), 8, WIDE), F32)
        for j in range(4 * E // 8):
            outs[0][0, SLICE:, j * LANES : j * LANES + SLICE] = held[8 * j : 8 * j + 8, :]
    for copy in copies:
        copy.wait()


def payload(groups, w_in, w_out, vectors, deps):
    vmem, hbm = pl.BlockSpec(memory_space=pltpu.VMEM), pl.BlockSpec(memory_space=pltpu.HBM)
    rows = SLICE + 8 if vectors else SLICE
    return pl.pallas_call(
        functools.partial(payload_kernel, groups, bool(vectors), len(deps)),
        in_specs=[hbm, hbm] + [vmem] * len(vectors) + [pl.BlockSpec(memory_space=pl.ANY)] * len(deps),
        out_specs=[vmem] * len(groups),
        out_shape=[pltpu.VMEM((len(group), rows, WIDE), F32) for group in groups],
        scratch_shapes=[pltpu.VMEM((4 * E, SLICE), F32), pltpu.SemaphoreType.DMA((2 * len(groups),))],
        compiler_params=params(SMALL_MIB),
        cost_estimate=pl.CostEstimate(flops=0, bytes_accessed=SLICE * WIDE * 16, transcendentals=0),
    )(in_hbm(w_in), in_hbm(w_out), *[in_hbm(v) for v in vectors], *deps)


def expert_kernel(group, first, last, n_deps, *refs):
    n = len(group)
    refs = list(refs)
    evh_ref, evl_ref, cot_ref, p_ref = refs[:4]
    shards = refs[4:8]
    del refs[:8]
    small = None if first else refs.pop(0)
    mix_in = None if first else refs.pop(0)
    if last:
        dp_before, sums_before = refs[: len(GROUPS) - 1], refs[len(GROUPS) - 1 : 2 * len(GROUPS) - 2]
        del refs[: 2 * len(GROUPS) - 2]
    del refs[:n_deps]
    mix_ref, dp_ref, dph_ref, dpl_ref, winh, winl, own_ref, part_ref, sums_ref = refs[:9]
    del refs[:9]
    if first:
        small = refs.pop(0)
    wouth, woutl, acc, sums = refs[:4]
    gate_acc = refs[4] if last else None
    step, steps = pl.program_id(0), pl.num_programs(0)
    odd = lax.axis_index("tp") & 1
    chip = lax.axis_index("tp") >> 1

    def tile(start, other):
        return pl.ds(pl.multiple_of(start + (chip ^ other) * LANES, LANES), LANES)

    @pl.when(step == 0)
    def _():
        acc[...] = jnp.zeros_like(acc)
        sums[...] = jnp.zeros_like(sums)
        if last:
            gate_acc[...] = jnp.zeros_like(gate_acc)
        for j in range(4 * E // 8 if first else 0):
            vectors = [shard[0, SLICE:, j * LANES : j * LANES + SLICE] for shard in shards]
            even_order, odd_order = (jnp.concatenate([vectors[k ^ c] for k in range(4)], axis=1) for c in range(2))
            small[8 * j : 8 * j + 8, :] = jnp.where(odd == 1, odd_order, even_order)
        if first:
            bias = small[E : 2 * E, :]
            small[E : 2 * E, :] = bias - jnp.mean(bias, axis=1, keepdims=True)
        own_rows = slice(0, SLICE)
        for i, e in enumerate(group):
            parts = [
                (shard[i, own_rows, :D], jnp.concatenate([shard[i, own_rows, tile(D, k)] for k in range(2)], axis=1))
                for shard in shards
            ]
            centre = sum(jnp.sum(out, axis=0, keepdims=True) for _, out in parts) / O
            for k, (into, out) in enumerate(parts):
                at = pl.multiple_of((odd ^ k) * SLICE, SLICE)
                winh[pl.ds(i * H + at, SLICE), :], winl[pl.ds(i * H + at, SLICE), :] = split(into)
                wouth[i, pl.ds(at, SLICE), :], woutl[i, pl.ds(at, SLICE), :] = split(out - centre)

    subs = RB // SUB
    rows_of = [slice(s * SUB, (s + 1) * SUB) for s in range(subs)]
    lane = lax.broadcasted_iota(jnp.int32, (SUB, LANES), 1)
    vector = lambda k, e: small[k * E + e : k * E + e + 1, :]
    state = [dict() for _ in range(subs)]

    def m1(s):
        events = evh_ref[rows_of[s], :], evl_ref[rows_of[s], :]
        state[s]["events"] = events
        pre = dot3(events, (winh[...], winl[...]), NT)
        state[s]["pre"] = [pre[:, i * H : (i + 1) * H] for i in range(n)]

    def v1(s):
        st = state[s]
        st["sigma"], st["hidden"], st["hidden_parts"] = [], [], []
        for i, e in enumerate(group):
            pre = st["pre"][i] + vector(0, e)
            sigma = jax.nn.sigmoid(pre)
            hidden = pre * sigma
            st["sigma"].append(sigma)
            st["hidden"].append(hidden)
            st["hidden_parts"].append(split(hidden))

    def m2(s):
        st = state[s]
        st["centred"] = [dot3(st["hidden_parts"][i], (wouth[i], woutl[i]), NT) for i in range(n)]

    def v2(s):
        st = state[s]
        p = p_ref[rows_of[s], :]
        dp = jnp.zeros_like(p)
        mixed = {}
        cots = [
            jnp.concatenate([cot_ref[rows_of[s], tile(t * O, 0)], cot_ref[rows_of[s], tile(t * O, 1)]], axis=1)
            for t in range(3)
        ]
        st["dnormed"] = []
        for i, e in enumerate(group):
            gain, shift = vector(2, e), vector(3, e)
            centred = st["centred"][i] + vector(1, e)
            rstd = lax.rsqrt(jnp.mean(centred * centred, axis=1, keepdims=True) + EPSILON)
            unit = centred * rstd
            y = unit * gain + shift
            dy = None
            for t in range(3):
                if e not in COLUMN[t]:
                    continue
                column = COLUMN[t][e]
                coef = p[:, column : column + 1]
                mixed[t] = coef * y + mixed[t] if t in mixed else coef * y
                dp = jnp.where(lane == column, jnp.sum(cots[t] * y, axis=1, keepdims=True), dp)
                dy = coef * cots[t] if dy is None else dy + coef * cots[t]
            dunit = dy * gain
            back_first = jnp.mean(dunit, axis=1, keepdims=True)
            back_second = jnp.mean(dunit * unit, axis=1, keepdims=True)
            dnormed = rstd * (dunit - back_first - unit * back_second)
            st["dnormed"].append(split(dnormed))
            dy_half = dy[:, :LANES]
            for k, v in enumerate((dnormed[:, :LANES], dy_half * unit[:, :LANES], dy_half)):
                sums[4 * i + k + 1 : 4 * i + k + 2, :] += jnp.sum(v, axis=0, keepdims=True)
        for t in range(3):
            for other in range(2):
                at = tile(t * O, other)
                if t in mixed:
                    value = mixed[t][:, other * LANES : (other + 1) * LANES]
                    mix_ref[rows_of[s], at] = value if first else mix_in[rows_of[s], at] + value
                elif first:
                    mix_ref[rows_of[s], at] = jnp.zeros((SUB, LANES), F32)
                else:
                    mix_ref[rows_of[s], at] = mix_in[rows_of[s], at]
        if last:
            for other in dp_before:
                dp = dp + other[rows_of[s], :]
            weighted = p * dp
            sets = (lane < 4, (lane >= 4) & (lane < 8), (lane >= 8) & (lane < GATE_COLS))
            a, b, c = (jnp.sum(jnp.where(m, weighted, 0.0), axis=1, keepdims=True) for m in sets)
            dp = weighted - p * jnp.where(sets[0], a, jnp.where(sets[1], b, c))
            st["dlogits"] = dp
        dp_ref[rows_of[s], :] = dp

    def m3(s):
        st = state[s]
        st["dhidden"] = [dot3(st["dnormed"][i], (wouth[i], woutl[i]), NN) for i in range(n)]

    def v3(s):
        st = state[s]
        st["dpre"] = []
        for i, e in enumerate(group):
            sigma, hidden = st["sigma"][i], st["hidden"][i]
            dpre = st["dhidden"][i] * (sigma + hidden * (1.0 - sigma))
            parts = split(dpre)
            dph_ref[rows_of[s], i * H : (i + 1) * H], dpl_ref[rows_of[s], i * H : (i + 1) * H] = parts
            st["dpre"].append(tuple(v[:, :LANES] for v in parts))
            sums[4 * i : 4 * i + 1, :] += jnp.sum(dpre[:, :LANES], axis=0, keepdims=True)

    def m4(s):
        st = state[s]
        for i in range(n):
            halves = tuple(v[:, :LANES] for v in st["dnormed"][i])
            acc[i * LANES : (i + 1) * LANES, D:] += dot3(halves, st["hidden_parts"][i], TN)
        beside = [split(st["dlogits"])] if last else []
        left = tuple(jnp.concatenate([h[k] for h in st["dpre"] + beside], axis=1) for k in range(2))
        both = dot3(left, st["events"], TN)
        acc[:, :D] += both[: n * LANES]
        if last:
            gate_acc[...] += both[n * LANES : n * LANES + 16]

    stages = (m1, v1, m2, v2, m3, v3, m4)
    for turn in range(len(stages) + LAG * (subs - 1)):
        for s in range(subs):
            if 0 <= turn - LAG * s < len(stages):
                stages[turn - LAG * s](s)

    @pl.when(step == steps - 1)
    def _():
        mine = pl.multiple_of(odd * SLICE, SLICE)
        other = pl.multiple_of(SLICE - mine, SLICE)
        for i in range(n):
            for t in range(WIDE // LANES):
                at = slice((t * n + i) * SLICE, (t * n + i + 1) * SLICE)
                lanes = slice(t * LANES, (t + 1) * LANES) if t < D // LANES else tile(D, t - D // LANES)
                own_ref[at, :] = acc[pl.ds(i * LANES + mine, SLICE), lanes]
                part_ref[at, :] = acc[pl.ds(i * LANES + other, SLICE), lanes]
        if last:
            sums_ref[...] = jnp.zeros_like(sums_ref)
            for g, before in enumerate(sums_before):
                sums_ref[8 * g : 8 * g + 8, :] = before[...]
            g = len(GROUPS) - 1
            sums_ref[8 * g : 8 * g + 8, :] = sums[...]
            for t in range(D // LANES):
                sums_ref[64 + 16 * t : 80 + 16 * t, :] = gate_acc[:, t * LANES : (t + 1) * LANES]
        else:
            sums_ref[...] = sums[...]


def experts(group, rows, high, low, cot, p, shards, small, mix, before, deps):
    n = len(group)
    first, last = mix is None, before is not None
    steps = rows // RB
    block = lambda width: pl.BlockSpec((RB, width), lambda i: (i, 0))
    whole = lambda shape: pl.BlockSpec(shape, lambda i: (0,) * len(shape))
    in_specs = [
        block(D),
        block(D),
        block(3 * O),
        block(LANES),
        *[whole(shards[0].shape)] * 4,
    ]
    args = [high, low, cot, p, *shards]
    aliases = {}
    if not first:
        aliases = {len(args) + 1: 0}
        in_specs += [whole((4 * E, H)), block(3 * O)]
        args += [small, mix]
    if last:
        in_specs += [block(LANES)] * len(before[0]) + [whole((8, LANES))] * len(before[1])
        args += [*before[0], *before[1]]
    in_specs += [pl.BlockSpec(memory_space=pl.ANY)] * len(deps)
    args += deps
    payload = WIDE // LANES * n * SLICE
    sums_shape = (2 * LANES // 2, LANES) if last else (8, LANES)
    scratch = [
        pltpu.VMEM((n, O, H), BF16),
        pltpu.VMEM((n, O, H), BF16),
        pltpu.VMEM((n * LANES, WIDE), F32),
        pltpu.VMEM((8, LANES), F32),
    ]
    if last:
        scratch.append(pltpu.VMEM((16, D), F32))
    return pl.pallas_call(
        functools.partial(expert_kernel, group, first, last, len(deps)),
        grid=(steps,),
        in_specs=in_specs,
        out_specs=[
                block(3 * O),
                block(LANES),
                block(n * H),
                block(n * H),
                whole((n * H, D)),
                whole((n * H, D)),
                whole((payload, LANES)),
                whole((payload, LANES)),
                whole(sums_shape),
        ]
        + [whole((4 * E, H))] * first,
        scratch_shapes=scratch,
        out_shape=[
            jax.ShapeDtypeStruct((rows, 3 * O), F32),
            jax.ShapeDtypeStruct((rows, LANES), F32),
            jax.ShapeDtypeStruct((rows, n * H), BF16),
            jax.ShapeDtypeStruct((rows, n * H), BF16),
            jax.ShapeDtypeStruct((n * H, D), BF16),
            jax.ShapeDtypeStruct((n * H, D), BF16),
            jax.ShapeDtypeStruct((payload, LANES), F32),
            jax.ShapeDtypeStruct((payload, LANES), F32),
            jax.ShapeDtypeStruct(sums_shape, F32),
        ]
        + [jax.ShapeDtypeStruct((4 * E, H), F32)] * first,
        input_output_aliases=aliases,
        compiler_params=params(EXPERT_MIB),
        cost_estimate=pl.CostEstimate(flops=n * rows * 6 * 720896, bytes_accessed=rows * 14000, transcendentals=0),
    )(*args)


def event_kernel(n, last, added, n_deps, *refs):
    highs, lows, winh, winl = (refs[k * n : (k + 1) * n] for k in range(4))
    refs = list(refs[4 * n :])
    total = 0.0
    if last:
        dlogits, gw_ref, gw = refs.pop(0), refs.pop(0), refs[-1]
        gw[...] = jnp.zeros_like(gw)
        gw[:GATE_COLS, :] = gw_ref[...]
        total = dot3(split(dlogits[...]), split(gw[...]), NN)
    before = refs.pop(0) if added else None
    out, token = refs[n_deps : n_deps + 2]
    for g in range(n):
        total = total + dot3((highs[g][...], lows[g][...]), (winh[g][...], winl[g][...]), NN)
    out[...] = total + before[...] if added else total
    token[...] = jnp.zeros_like(token)


def event_grads(rows, highs, lows, winh, winl, gating, before, deps):
    block = lambda width: pl.BlockSpec((ROW_BLOCK, width), lambda i: (i, 0))
    whole = lambda shape: pl.BlockSpec(shape, lambda i: (0, 0))
    args = [*highs, *lows, *winh, *winl]
    in_specs = [block(v.shape[1]) for v in (*highs, *lows)] + [whole(v.shape) for v in (*winh, *winl)]
    aliases = {}
    if gating:
        args += gating
        in_specs += [block(LANES), whole((GATE_COLS, D))]
    if before is not None:
        aliases = {len(args): 0}
        args.append(before)
        in_specs.append(block(D))
    return pl.pallas_call(
        functools.partial(event_kernel, len(highs), bool(gating), before is not None, len(deps)),
        grid=(rows // ROW_BLOCK,),
        in_specs=in_specs + [pl.BlockSpec(memory_space=pl.ANY)] * len(deps),
        out_specs=[block(D), whole(TOKEN)],
        scratch_shapes=[pltpu.VMEM((LANES, D), F32)],
        out_shape=[pltpu.VMEM((rows, D), F32), jax.ShapeDtypeStruct(TOKEN, F32)],
        input_output_aliases=aliases,
        compiler_params=params(EVENT_MIB),
        cost_estimate=pl.CostEstimate(
            flops=6 * rows * D * sum(v.shape[1] for v in highs), bytes_accessed=rows * 4000, transcendentals=0
        ),
    )(*args, *deps)


def place_kernel(own, other, *refs):
    out, token, sems = refs[-3:]
    rows = own.shape[0]
    side = lax.axis_index("tp") & 1
    copies = [
        pltpu.make_async_copy(v, out.at[pl.ds(pl.multiple_of(at * rows, ROW_BLOCK), rows), :], sems.at[k])
        for k, (v, at) in enumerate(((own, side), (other, 1 - side)))
    ]
    for copy in copies:
        copy.start()
    token[...] = jnp.zeros_like(token)
    for copy in copies:
        copy.wait()


def place(own, other, deps):
    rows, width = own.shape
    anywhere = pl.BlockSpec(memory_space=pl.ANY)
    return pl.pallas_call(
        place_kernel,
        in_specs=[anywhere] * (2 + len(deps)),
        out_specs=[pl.BlockSpec(memory_space=pltpu.HBM), pl.BlockSpec(memory_space=pltpu.VMEM)],
        scratch_shapes=[pltpu.SemaphoreType.DMA((2,))],
        out_shape=[jax.ShapeDtypeStruct((2 * rows, width), F32), jax.ShapeDtypeStruct(TOKEN, F32)],
        compiler_params=params(SMALL_MIB),
        cost_estimate=pl.CostEstimate(flops=0, bytes_accessed=rows * width * 16, transcendentals=0),
    )(own, other, *deps)


class Job:
    def __init__(self, args, shapes, body, scratch=()):
        self.args, self.body, self.scratch = args, body, list(scratch)
        self.shapes = [jax.ShapeDtypeStruct(shape, F32) for shape in shapes]


def copy_job(*arrays):
    def body(ins, outs, scratch):
        for a, b in zip(ins, outs):
            b[...] = a[...]

    return Job(arrays, [a.shape for a in arrays], body)


def run(jobs, deps=(), through=()):
    args = [a for job in jobs for a in job.args]
    shapes = [o for job in jobs for o in job.shapes]
    scratch = [v for job in jobs for v in job.scratch]

    def kernel(*refs):
        ins, refs = refs[: len(args)], refs[len(args) + len(through) + len(deps) :]
        outs, token, kept = refs[: len(shapes)], refs[len(shapes) + len(through)], refs[len(shapes) + len(through) + 1 :]
        token[...] = jnp.zeros_like(token)
        i = o = k = 0
        for job in jobs:
            ni, no, nk = len(job.args), len(job.shapes), len(job.scratch)
            job.body(ins[i : i + ni], outs[o : o + no], kept[k : k + nk])
            i, o, k = i + ni, o + no, k + nk

    vmem, anywhere = pl.BlockSpec(memory_space=pltpu.VMEM), pl.BlockSpec(memory_space=pl.ANY)
    flat = pl.pallas_call(
        kernel,
        in_specs=[vmem] * len(args) + [anywhere] * (len(through) + len(deps)),
        out_specs=[vmem] * len(shapes) + [anywhere] * len(through) + [vmem],
        out_shape=shapes
        + [jax.ShapeDtypeStruct(v.shape, v.dtype) for v in through]
        + [jax.ShapeDtypeStruct(TOKEN, F32)],
        scratch_shapes=scratch,
        input_output_aliases={len(args) + k: len(shapes) + k for k in range(len(through))},
        compiler_params=params(SMALL_MIB),
        cost_estimate=pl.CostEstimate(flops=0, bytes_accessed=sum(8 * a.size for a in args), transcendentals=0),
    )(*args, *through, *deps)
    result = []
    for job in jobs:
        result.append(list(flat[: len(job.shapes)]))
        flat = flat[len(job.shapes) :]
    return result, list(flat[:-1]), flat[-1]


def part_of(ref, index, rows):
    return ref.at[pl.ds(pl.multiple_of(index * rows, 8), rows), :]


class Reduction:
    def __init__(self, own, got, n_dp, width):
        self.own, self.got = own, got
        left, start = n_dp.bit_length() - 1, 0
        self.groups = []
        while left > width:
            self.groups.append((start, width))
            start, left = start + width, left - width
        self.scattered = len(self.groups)
        self.order = [*self.groups, (start, left), *reversed(self.groups)]
        unit = 8 << start
        self.rows = -(-sum(v.shape[0] for v in own) // unit) * unit
        self.n_dp = n_dp
        self.stage = 0

    @property
    def finished(self):
        return self.stage > len(self.order)

    @property
    def joining(self):
        return self.stage == len(self.order)

    def job(self):
        stage = self.stage
        gather, scatter = stage > self.scattered + 1, stage < self.scattered
        keeps = self.own if stage == 0 else [self.keep]
        args = [*keeps, *self.got]
        came = self.order[stage - 1]
        goes = self.order[stage] if stage < len(self.order) else None
        rows = self.rows if stage == 0 else self.keep.shape[0] * ((1 << came[1]) if gather else 1)
        parts = 1 << goes[1] if scatter else 1

        def body(ins, outs, scratch):
            to = scratch[0] if scatter else outs[0]
            if gather:
                join(ins, to, came)
                return
            at = 0
            for k, a in enumerate(keeps):
                total = ins[k][...]
                for v in ins[k + len(keeps) :: len(keeps)]:
                    total = total + v[...]
                to[at : at + a.shape[0], :] = total
                at += a.shape[0]
            if at < rows:
                to[at:, :] = jnp.zeros((rows - at, LANES), F32)
            if scatter:
                side = side_of(goes)
                for m in range(parts):
                    outs[m][...] = part_of(to, side ^ m, rows // parts)[...]

        if scatter:
            return Job(args, [(rows // parts, LANES)] * parts, body, [pltpu.VMEM((rows, LANES), F32)])
        return Job(args, [(rows, LANES)], body)

    def take(self, outs):
        self.keep = outs[0]
        if self.stage < len(self.order):
            start, bits = self.order[self.stage]
            self.got = []
            for m in range(1, 1 << bits):
                v = outs[m] if self.stage < self.scattered else outs[0]
                self.got.append(lax.ppermute(v, "dp", [(i, i ^ (m << start)) for i in range(self.n_dp)]))
        self.stage += 1


def side_of(bits):
    return (lax.axis_index("dp") >> bits[0]) & ((1 << bits[1]) - 1)


def join(ins, to, bits):
    for m, v in enumerate(ins):
        part_of(to, side_of(bits) ^ m, v.shape[0])[...] = v[...]


def finish_body(joining, ins, outs, both):
    in_grad, in_bias, out_grad, out_bias, gain, shift, gate = outs
    odd = (lax.axis_index("tp") & 1) == 1
    ins, both, summed = list(ins), list(both), []
    for bits in joining:
        if bits:
            n = 1 << bits[1]
            join(ins[:n], both[0], bits)
            summed.append(both.pop(0))
            del ins[:n]
        else:
            summed.append(ins.pop(0))
    for u, unit in enumerate(UNITS):
        at = 0
        for g in unit:
            group = GROUPS[g]
            for t in range(WIDE // LANES):
                for e in group:
                    tile = summed[u][at : at + SLICE, :]
                    at += SLICE
                    if t < D // LANES:
                        in_grad[e, :, t * LANES : (t + 1) * LANES] = tile
                    else:
                        out_grad[e, :, t * LANES - D : (t + 1) * LANES - D] = tile
    sums = summed[-1][at : at + 8 * len(GROUPS), :]
    sums = jnp.where(odd, sums[:, SLICE:], sums[:, :SLICE])
    for g, group in enumerate(GROUPS):
        for i, e in enumerate(group):
            for k, ref in enumerate((in_bias, out_bias, gain, shift)):
                ref[e : e + 1, :] = sums[8 * g + 4 * i + k : 8 * g + 4 * i + k + 1, :]
    for t in range(D // LANES):
        gate[:, t * LANES : (t + 1) * LANES] = summed[-1][at + 64 + 16 * t : at + 64 + 16 * t + GATE_COLS, :]


def per_device(
    events,
    valid_counts,
    mix_cotangent,
    expert_in,
    expert_in_bias,
    expert_out,
    expert_out_bias,
    norm_gain,
    norm_shift,
    gate_weight,
):
    n_dp = lax.axis_size("dp")
    rows = events.shape[0] // 2
    w_in = jnp.swapaxes(expert_in, 1, 2)
    w_out = jnp.swapaxes(expert_out, 1, 2)
    gate_w = jnp.swapaxes(gate_weight, 0, 1)
    core = [(i, i ^ 1) for i in range(4)]
    across = [(i, i ^ 2) for i in range(4)]
    vectors = [expert_in_bias, expert_out_bias, norm_gain, norm_shift]
    own = list(payload(GROUPS[:1], w_in, w_out, vectors, []))
    far = [lax.ppermute(own[0], "tp", across)]
    beside = [lax.ppermute(own[0], "tp", core)]
    own += payload(GROUPS[1:], w_in, w_out, [], own)
    high, low, p, cot = gates(valid_counts, events, mix_cotangent, gate_w, rows, own[1:2])
    relayed = []
    summing = {}
    partial = []
    made = []
    placed, unplaced = [], []
    mix = small = x_grad = None
    deps = [p]
    for kind, what, units in PLAN:
        if kind == "experts":
            last = what == len(GROUPS) - 1
            shards = (own[what], beside[what], far[what], relayed[what])
            before = ([m[1] for m in made], [m[8] for m in made]) if last else None
            made.append(experts(GROUPS[what], rows, high, low, cot, p, shards, small, mix, before, deps))
            mix = made[what][0]
            small = made[0][9]
            deps = [made[what][8]]
        elif kind == "events":
            ours = [[made[g][k] for g in what] for k in (2, 3, 4, 5)]
            gating = [made[-1][1], gate_w] if what[-1] == len(GROUPS) - 1 else []
            x_grad, token = event_grads(rows, *ours, gating, x_grad, deps)
            deps = [token]
        elif kind == "place":
            v, token = place(*unplaced.pop(0), deps)
            placed.append(v)
            deps = [token]
        else:
            jobs = [summing[u].job() for u in units]
            sent, fetched, through = [], [], []
            if "send" in what:
                sent = [made[-1][7]] + ([made[-1][8]] if len(made) == len(GROUPS) else [])
                jobs.append(copy_job(*sent))
            if "fetch" in what:
                group = len(relayed)
                fetched = [far[group], *own[group + 1 : group + 2]]
                jobs.append(copy_job(*fetched))
            if "mix" in what:
                through.append(mix)
            if "grad" in what:
                through.append(x_grad)
            outs, through, token = run(jobs, deps, through)
            deps = [token]
            for u, o in zip(units, outs):
                summing[u].take(o)
            if fetched:
                relayed.append(lax.ppermute(outs[-1][0], "tp", core))
                if len(fetched) > 1:
                    far.append(lax.ppermute(outs[-1][1], "tp", across))
                    beside.append(lax.ppermute(outs[-1][1], "tp", core))
            if sent:
                got = [lax.ppermute(v, "tp", core) for v in outs[len(units)]]
                partial.append(([made[-1][6], *sent[1:]], got))
                for u, (unit, width) in enumerate(zip(UNITS, WIDTH)):
                    if unit[-1] == len(partial) - 1:
                        both = [partial[g] for g in unit]
                        summing[u] = Reduction([v for b in both for v in b[0]], [v for b in both for v in b[1]], n_dp, width)
            unplaced += [(v, lax.ppermute(v, "tp", core)) for v in through]
    mixtures, x_grad = placed
    summing = [summing[u] for u in range(len(UNITS))]
    while not all(u.finished or u.joining for u in summing):
        ours = [u for u in summing if not u.finished and not u.joining]
        outs, _, token = run([u.job() for u in ours], deps)
        deps = [token]
        for u, o in zip(ours, outs):
            u.take(o)
    joining = [u.order[-1] if u.joining else None for u in summing]
    halves = [v for u in summing for v in ([u.keep, *u.got] if u.joining else [u.keep])]
    per_expert = (E, SLICE)
    shapes = [(E, SLICE, D), per_expert, (E, SLICE, H), per_expert, per_expert, per_expert, (GATE_COLS, D)]
    scratch = [pltpu.VMEM((u.rows, LANES), F32) for u in summing if u.joining]
    job = Job(halves, shapes, functools.partial(finish_body, joining), scratch)
    (((in_grad, in_bias, out_grad, out_bias, gain, shift, gate),), _, _) = run([job], deps)
    return (
        mixtures,
        x_grad,
        jnp.swapaxes(in_grad, 1, 2),
        in_bias,
        jnp.swapaxes(out_grad, 1, 2),
        out_bias,
        gain,
        shift,
        jnp.swapaxes(gate, 0, 1),
    )


def solution(mesh):
    return jax.shard_map(
        per_device,
        mesh=mesh,
        in_specs=(
            P("dp", None),
            P(),
            P("dp", None),
            P(None, None, "tp"),
            P(None, "tp"),
            P(None, None, "tp"),
            P(None, "tp"),
            P(None, "tp"),
            P(None, "tp"),
            P(),
        ),
        out_specs=(
            P("dp", None),
            P("dp", None),
            P(None, None, "tp"),
            P(None, "tp"),
            P(None, None, "tp"),
            P(None, "tp"),
            P(None, "tp"),
            P(None, "tp"),
            P(),
        ),
        check_vma=False,
    )
```

```python
import functools

import jax
import jax.numpy as jnp
from jax import lax
from jax.experimental import pallas as pl
from jax.experimental.pallas import tpu as pltpu
from jax.sharding import PartitionSpec as P

D = 512
H = 256
O = 256
E = 6
GATE_COLS = 14
SLICE = 64
WIDE = D + H
LANES = 128
TOKEN = (8, LANES)
RB = 1024
ROW_BLOCK = 256
SUB = 256
LAG = 1
EPSILON = 1e-05
GROUPS = ((0, 1), (2, 3), (4,), (5,))
UNITS = ((0,), (1,), (2, 3))
WAY = ("single", "single", "pair")
PLAN = (
    ("small", "fetch", ()),
    ("experts", 0, ()),
    ("small", "send", ()),
    ("events", (0,), ()),
    ("small", "fetch", (0,)),
    ("experts", 1, ()),
    ("small", "send fetch", (0,)),
    ("events", (1,), ()),
    ("small", "", (0, 1)),
    ("experts", 2, ()),
    ("small", "send fetch", (0, 1)),
    ("experts", 3, ()),
    ("small", "send", (0, 1)),
    ("events", (2,), ()),
    ("small", "", (2,)),
    ("events", (3,), ()),
    ("small", "mix grad", (0, 1, 2)),
    ("small", "", (1, 2)),
    ("place", None, ()),
    ("place", None, ()),
)
COLUMN = (
    {0: 0, 1: 1, 4: 2, 5: 3},
    {2: 4, 3: 5, 4: 6, 5: 7},
    {e: 8 + e for e in range(E)},
)
F32 = jnp.float32
BF16 = jnp.bfloat16
NN = (((1,), (0,)), ((), ()))
NT = (((1,), (1,)), ((), ()))
TN = (((0,), (0,)), ((), ()))


def split(v):
    high = v.astype(BF16)
    return high, (v - high.astype(F32)).astype(BF16)


def dot3(a, b, dims):
    def one(u, v):
        return lax.dot_general(u, v, dims, preferred_element_type=F32)

    return one(a[0], b[0]) + (one(a[0], b[1]) + one(a[1], b[0]))


def in_hbm(v):
    return pltpu.with_memory_space_constraint(v, pltpu.HBM)


LARGE = 60
EXPERT_MIB, EVENT_MIB, GATE_MIB, SMALL_MIB = 28, 16, 16, 8


def params(mib):
    return pltpu.CompilerParams(vmem_limit_bytes=mib << 20)


def gate_kernel(n_deps, counts, ev_ref, cot_ref, gw_ref, *refs):
    high_ref, low_ref, p_ref, cot_out, gw, held, sems = refs[n_deps:]
    rows = held.shape[0]
    steps = rows // ROW_BLOCK
    start = pl.multiple_of((lax.axis_index("tp") & 1) * rows, ROW_BLOCK)
    valid = counts[lax.axis_index("dp")]
    blocks = [slice(i * ROW_BLOCK, (i + 1) * ROW_BLOCK) for i in range(steps)]
    copies = [
        pltpu.make_async_copy(ev_ref.at[pl.ds(start + at.start, ROW_BLOCK), :], held.at[at, :], sems.at[i])
        for i, at in enumerate(blocks)
    ]
    copies.append(pltpu.make_async_copy(cot_ref.at[pl.ds(start, rows), :], cot_out, sems.at[steps]))
    for copy in copies:
        copy.start()
    gw[...] = jnp.zeros_like(gw)
    gw[:GATE_COLS, :] = gw_ref[...]
    gate = split(gw[...])
    lane = lax.broadcasted_iota(jnp.int32, (ROW_BLOCK, LANES), 1)
    sets = (lane < 4, (lane >= 4) & (lane < 8), (lane >= 8) & (lane < GATE_COLS))

    def per_set(values, empty, reduce):
        a, b, s = (reduce(jnp.where(m, values, empty), axis=1, keepdims=True) for m in sets)
        return jnp.where(sets[0], a, jnp.where(sets[1], b, s))

    for i, at in enumerate(blocks):
        copies[i].wait()
        events = split(held[at, :])
        high_ref[at, :], low_ref[at, :] = events
        logits = dot3(events, gate, NT)
        top = per_set(logits, -3e38, jnp.max)
        shares = jnp.where(lane < GATE_COLS, jnp.exp(logits - top), 0.0)
        p = shares / per_set(shares, 0.0, jnp.sum)
        row = start + at.start + lax.broadcasted_iota(jnp.int32, logits.shape, 0)
        p_ref[at, :] = jnp.where((row < valid) & (lane < GATE_COLS), p, 0.0)
    copies[-1].wait()


def gates(counts, events, cot, gate_w, rows, deps):
    vmem, hbm = pl.BlockSpec(memory_space=pltpu.VMEM), pl.BlockSpec(memory_space=pltpu.HBM)
    steps = rows // ROW_BLOCK
    return pl.pallas_call(
        functools.partial(gate_kernel, len(deps)),
        in_specs=[pl.BlockSpec(memory_space=pltpu.SMEM), hbm, hbm, vmem]
        + [pl.BlockSpec(memory_space=pl.ANY)] * len(deps),
        out_specs=[vmem] * 4,
        out_shape=[
            pltpu.VMEM((rows, D), BF16),
            pltpu.VMEM((rows, D), BF16),
            pltpu.VMEM((rows, LANES), F32),
            pltpu.VMEM((rows, 3 * O), F32),
        ],
        scratch_shapes=[
            pltpu.VMEM((LANES, D), F32),
            pltpu.VMEM((rows, D), F32),
            pltpu.SemaphoreType.DMA((steps + 1,)),
        ],
        compiler_params=params(GATE_MIB),
        cost_estimate=pl.CostEstimate(flops=6 * rows * D * LANES, bytes_accessed=rows * D * 8, transcendentals=0),
    )(counts, in_hbm(events), in_hbm(cot), in_hbm(gate_w), *deps)


def payload_kernel(groups, vectors, n_deps, w_in, w_out, *refs):
    given = refs[:4] if vectors else ()
    held = refs[-2]
    outs, sems = refs[len(given) + n_deps :][: len(groups)], refs[-1]
    copies = []
    for out, group in zip(outs, groups):
        experts_of, rows = pl.ds(group[0], len(group)), slice(0, SLICE)
        for part, lanes in ((w_in, slice(0, D)), (w_out, slice(D, WIDE))):
            copies.append(pltpu.make_async_copy(part.at[experts_of], out.at[:, rows, lanes], sems.at[len(copies)]))
    for k, v in enumerate(given):
        copies.append(pltpu.make_async_copy(v, held.at[k, slice(0, E), :], sems.at[len(copies)]))
    for copy in copies:
        copy.start()
    if vectors:
        for copy in copies[-len(given) :]:
            copy.wait()
        copies = copies[: -len(given)]
        rows = jnp.concatenate([held[k, :E, :] for k in range(4)], axis=0)
        outs[0][:, SLICE:, :] = jnp.zeros((len(groups[0]), 8, WIDE), F32)
        for j in range(4 * E // 8):
            outs[0][0, SLICE:, j * LANES : j * LANES + SLICE] = rows[8 * j : 8 * j + 8, :]
    for copy in copies:
        copy.wait()


def payload(groups, w_in, w_out, vectors, deps):
    vmem, hbm = pl.BlockSpec(memory_space=pltpu.VMEM), pl.BlockSpec(memory_space=pltpu.HBM)
    rows = SLICE + 8 if vectors else SLICE
    return pl.pallas_call(
        functools.partial(payload_kernel, groups, bool(vectors), len(deps)),
        in_specs=[hbm, hbm] + [hbm] * len(vectors) + [pl.BlockSpec(memory_space=pl.ANY)] * len(deps),
        out_specs=[vmem] * len(groups),
        out_shape=[pltpu.VMEM((len(group), rows, WIDE), F32) for group in groups],
        scratch_shapes=[pltpu.VMEM((4, 8, SLICE), F32), pltpu.SemaphoreType.DMA((2 * len(groups) + 4,))],
        compiler_params=params(SMALL_MIB),
        cost_estimate=pl.CostEstimate(flops=0, bytes_accessed=SLICE * WIDE * 16, transcendentals=0),
    )(in_hbm(w_in), in_hbm(w_out), *[in_hbm(v) for v in vectors], *deps)


def expert_kernel(group, first, last, n_deps, *refs):
    n = len(group)
    refs = list(refs)
    evh_ref, evl_ref, cot_ref, p_ref = refs[:4]
    shards = refs[4:8]
    del refs[:8]
    small = None if first else refs.pop(0)
    mix_in = None if first else refs.pop(0)
    if last:
        dp_before, sums_before = refs[: len(GROUPS) - 1], refs[len(GROUPS) - 1 : 2 * len(GROUPS) - 2]
        del refs[: 2 * len(GROUPS) - 2]
    del refs[:n_deps]
    mix_ref, dp_ref, dph_ref, dpl_ref, winh, winl, own_ref, part_ref, sums_ref = refs[:9]
    del refs[:9]
    if first:
        small = refs.pop(0)
    wouth, woutl, acc, sums = refs[:4]
    gate_acc = refs[4] if last else None
    step, steps = pl.program_id(0), pl.num_programs(0)
    odd = lax.axis_index("tp") & 1
    chip = lax.axis_index("tp") >> 1

    def tile(start, other):
        return pl.ds(pl.multiple_of(start + (chip ^ other) * LANES, LANES), LANES)

    @pl.when(step == 0)
    def _():
        acc[...] = jnp.zeros_like(acc)
        sums[...] = jnp.zeros_like(sums)
        if last:
            gate_acc[...] = jnp.zeros_like(gate_acc)
        for j in range(4 * E // 8 if first else 0):
            vectors = [shard[0, SLICE:, j * LANES : j * LANES + SLICE] for shard in shards]
            even_order, odd_order = (jnp.concatenate([vectors[k ^ c] for k in range(4)], axis=1) for c in range(2))
            small[8 * j : 8 * j + 8, :] = jnp.where(odd == 1, odd_order, even_order)
        if first:
            bias = small[E : 2 * E, :]
            small[E : 2 * E, :] = bias - jnp.mean(bias, axis=1, keepdims=True)
        own_rows = slice(0, SLICE)
        for i, e in enumerate(group):
            parts = [
                (shard[i, own_rows, :D], jnp.concatenate([shard[i, own_rows, tile(D, k)] for k in range(2)], axis=1))
                for shard in shards
            ]
            centre = sum(jnp.sum(out, axis=0, keepdims=True) for _, out in parts) / O
            for k, (into, out) in enumerate(parts):
                at = pl.multiple_of((odd ^ k) * SLICE, SLICE)
                winh[pl.ds(i * H + at, SLICE), :], winl[pl.ds(i * H + at, SLICE), :] = split(into)
                wouth[i, pl.ds(at, SLICE), :], woutl[i, pl.ds(at, SLICE), :] = split(out - centre)

    subs = RB // SUB
    rows_of = [slice(s * SUB, (s + 1) * SUB) for s in range(subs)]
    lane = lax.broadcasted_iota(jnp.int32, (SUB, LANES), 1)
    vector = lambda k, e: small[k * E + e : k * E + e + 1, :]
    state = [dict() for _ in range(subs)]

    def m1(s):
        events = evh_ref[rows_of[s], :], evl_ref[rows_of[s], :]
        state[s]["events"] = events
        pre = dot3(events, (winh[...], winl[...]), NT)
        state[s]["pre"] = [pre[:, i * H : (i + 1) * H] for i in range(n)]

    def v1(s):
        st = state[s]
        st["sigma"], st["hidden"], st["hidden_parts"] = [], [], []
        for i, e in enumerate(group):
            pre = st["pre"][i] + vector(0, e)
            sigma = jax.nn.sigmoid(pre)
            hidden = pre * sigma
            st["sigma"].append(sigma)
            st["hidden"].append(hidden)
            st["hidden_parts"].append(split(hidden))

    def m2(s):
        st = state[s]
        st["centred"] = [dot3(st["hidden_parts"][i], (wouth[i], woutl[i]), NT) for i in range(n)]

    def v2(s):
        st = state[s]
        p = p_ref[rows_of[s], :]
        dp = jnp.zeros_like(p)
        mixed = {}
        cots = [
            jnp.concatenate([cot_ref[rows_of[s], tile(t * O, 0)], cot_ref[rows_of[s], tile(t * O, 1)]], axis=1)
            for t in range(3)
        ]
        st["dnormed"] = []
        for i, e in enumerate(group):
            gain, shift = vector(2, e), vector(3, e)
            centred = st["centred"][i] + vector(1, e)
            rstd = lax.rsqrt(jnp.mean(centred * centred, axis=1, keepdims=True) + EPSILON)
            unit = centred * rstd
            y = unit * gain + shift
            dy = None
            for t in range(3):
                if e not in COLUMN[t]:
                    continue
                column = COLUMN[t][e]
                coef = p[:, column : column + 1]
                mixed[t] = coef * y + mixed[t] if t in mixed else coef * y
                dp = jnp.where(lane == column, jnp.sum(cots[t] * y, axis=1, keepdims=True), dp)
                dy = coef * cots[t] if dy is None else dy + coef * cots[t]
            dunit = dy * gain
            back_first = jnp.mean(dunit, axis=1, keepdims=True)
            back_second = jnp.mean(dunit * unit, axis=1, keepdims=True)
            dnormed = rstd * (dunit - back_first - unit * back_second)
            st["dnormed"].append(split(dnormed))
            dy_half = dy[:, :LANES]
            for k, v in enumerate((dnormed[:, :LANES], dy_half * unit[:, :LANES], dy_half)):
                sums[4 * i + k + 1 : 4 * i + k + 2, :] += jnp.sum(v, axis=0, keepdims=True)
        for t in range(3):
            for other in range(2):
                at = tile(t * O, other)
                if t in mixed:
                    value = mixed[t][:, other * LANES : (other + 1) * LANES]
                    mix_ref[rows_of[s], at] = value if first else mix_in[rows_of[s], at] + value
                elif first:
                    mix_ref[rows_of[s], at] = jnp.zeros((SUB, LANES), F32)
                else:
                    mix_ref[rows_of[s], at] = mix_in[rows_of[s], at]
        if last:
            for other in dp_before:
                dp = dp + other[rows_of[s], :]
            weighted = p * dp
            sets = (lane < 4, (lane >= 4) & (lane < 8), (lane >= 8) & (lane < GATE_COLS))
            a, b, c = (jnp.sum(jnp.where(m, weighted, 0.0), axis=1, keepdims=True) for m in sets)
            dp = weighted - p * jnp.where(sets[0], a, jnp.where(sets[1], b, c))
            st["dlogits"] = dp
        dp_ref[rows_of[s], :] = dp

    def m3(s):
        st = state[s]
        st["dhidden"] = [dot3(st["dnormed"][i], (wouth[i], woutl[i]), NN) for i in range(n)]

    def v3(s):
        st = state[s]
        st["dpre"] = []
        for i, e in enumerate(group):
            sigma, hidden = st["sigma"][i], st["hidden"][i]
            dpre = st["dhidden"][i] * (sigma + hidden * (1.0 - sigma))
            parts = split(dpre)
            dph_ref[rows_of[s], i * H : (i + 1) * H], dpl_ref[rows_of[s], i * H : (i + 1) * H] = parts
            st["dpre"].append(tuple(v[:, :LANES] for v in parts))
            sums[4 * i : 4 * i + 1, :] += jnp.sum(dpre[:, :LANES], axis=0, keepdims=True)

    def m4(s):
        st = state[s]
        for i in range(n):
            halves = tuple(v[:, :LANES] for v in st["dnormed"][i])
            acc[i * LANES : (i + 1) * LANES, D:] += dot3(halves, st["hidden_parts"][i], TN)
        beside = [split(st["dlogits"])] if last else []
        left = tuple(jnp.concatenate([h[k] for h in st["dpre"] + beside], axis=1) for k in range(2))
        both = dot3(left, st["events"], TN)
        acc[:, :D] += both[: n * LANES]
        if last:
            gate_acc[...] += both[n * LANES : n * LANES + 16]

    stages = (m1, v1, m2, v2, m3, v3, m4)
    for turn in range(len(stages) + LAG * (subs - 1)):
        for s in range(subs):
            if 0 <= turn - LAG * s < len(stages):
                stages[turn - LAG * s](s)

    @pl.when(step == steps - 1)
    def _():
        mine = pl.multiple_of(odd * SLICE, SLICE)
        other = pl.multiple_of(SLICE - mine, SLICE)
        for i in range(n):
            for t in range(WIDE // LANES):
                at = slice((t * n + i) * SLICE, (t * n + i + 1) * SLICE)
                lanes = slice(t * LANES, (t + 1) * LANES) if t < D // LANES else tile(D, t - D // LANES)
                own_ref[at, :] = acc[pl.ds(i * LANES + mine, SLICE), lanes]
                part_ref[at, :] = acc[pl.ds(i * LANES + other, SLICE), lanes]
        if last:
            sums_ref[...] = jnp.zeros_like(sums_ref)
            for g, before in enumerate(sums_before):
                sums_ref[8 * g : 8 * g + 8, :] = before[...]
            g = len(GROUPS) - 1
            sums_ref[8 * g : 8 * g + 8, :] = sums[...]
            for t in range(D // LANES):
                sums_ref[64 + 16 * t : 80 + 16 * t, :] = gate_acc[:, t * LANES : (t + 1) * LANES]
        else:
            sums_ref[...] = sums[...]


def experts(group, rows, high, low, cot, p, shards, small, mix, before, deps):
    n = len(group)
    first, last = mix is None, before is not None
    steps = rows // RB
    block = lambda width: pl.BlockSpec((RB, width), lambda i: (i, 0))
    whole = lambda shape: pl.BlockSpec(shape, lambda i: (0,) * len(shape))
    in_specs = [
        block(D),
        block(D),
        block(3 * O),
        block(LANES),
        *[whole(shards[0].shape)] * 4,
    ]
    args = [high, low, cot, p, *shards]
    aliases = {}
    if not first:
        aliases = {len(args) + 1: 0}
        in_specs += [whole((4 * E, H)), block(3 * O)]
        args += [small, mix]
    if last:
        in_specs += [block(LANES)] * len(before[0]) + [whole((8, LANES))] * len(before[1])
        args += [*before[0], *before[1]]
    in_specs += [pl.BlockSpec(memory_space=pl.ANY)] * len(deps)
    args += deps
    payload = WIDE // LANES * n * SLICE
    sums_shape = (2 * LANES // 2, LANES) if last else (8, LANES)
    scratch = [
        pltpu.VMEM((n, O, H), BF16),
        pltpu.VMEM((n, O, H), BF16),
        pltpu.VMEM((n * LANES, WIDE), F32),
        pltpu.VMEM((8, LANES), F32),
    ]
    if last:
        scratch.append(pltpu.VMEM((16, D), F32))
    return pl.pallas_call(
        functools.partial(expert_kernel, group, first, last, len(deps)),
        grid=(steps,),
        in_specs=in_specs,
        out_specs=[
                block(3 * O),
                block(LANES),
                block(n * H),
                block(n * H),
                whole((n * H, D)),
                whole((n * H, D)),
                whole((payload, LANES)),
                whole((payload, LANES)),
                whole(sums_shape),
        ]
        + [whole((4 * E, H))] * first,
        scratch_shapes=scratch,
        out_shape=[
            jax.ShapeDtypeStruct((rows, 3 * O), F32),
            jax.ShapeDtypeStruct((rows, LANES), F32),
            jax.ShapeDtypeStruct((rows, n * H), BF16),
            jax.ShapeDtypeStruct((rows, n * H), BF16),
            jax.ShapeDtypeStruct((n * H, D), BF16),
            jax.ShapeDtypeStruct((n * H, D), BF16),
            jax.ShapeDtypeStruct((payload, LANES), F32),
            jax.ShapeDtypeStruct((payload, LANES), F32),
            jax.ShapeDtypeStruct(sums_shape, F32),
        ]
        + [jax.ShapeDtypeStruct((4 * E, H), F32)] * first,
        input_output_aliases=aliases,
        compiler_params=params(EXPERT_MIB),
        cost_estimate=pl.CostEstimate(flops=n * rows * 6 * 720896, bytes_accessed=rows * 14000, transcendentals=0),
    )(*args)


def event_kernel(n, last, added, n_deps, *refs):
    highs, lows, winh, winl = (refs[k * n : (k + 1) * n] for k in range(4))
    refs = list(refs[4 * n :])
    total = 0.0
    if last:
        dlogits, gw_ref, gw = refs.pop(0), refs.pop(0), refs[-1]
        gw[...] = jnp.zeros_like(gw)
        gw[:GATE_COLS, :] = gw_ref[...]
        total = dot3(split(dlogits[...]), split(gw[...]), NN)
    before = refs.pop(0) if added else None
    out, token = refs[n_deps : n_deps + 2]
    for g in range(n):
        total = total + dot3((highs[g][...], lows[g][...]), (winh[g][...], winl[g][...]), NN)
    out[...] = total + before[...] if added else total
    token[...] = jnp.zeros_like(token)


def event_grads(rows, highs, lows, winh, winl, gating, before, deps):
    block = lambda width: pl.BlockSpec((ROW_BLOCK, width), lambda i: (i, 0))
    whole = lambda shape: pl.BlockSpec(shape, lambda i: (0, 0))
    args = [*highs, *lows, *winh, *winl]
    in_specs = [block(v.shape[1]) for v in (*highs, *lows)] + [whole(v.shape) for v in (*winh, *winl)]
    aliases = {}
    if gating:
        args += gating
        in_specs += [block(LANES), whole((GATE_COLS, D))]
    if before is not None:
        aliases = {len(args): 0}
        args.append(before)
        in_specs.append(block(D))
    return pl.pallas_call(
        functools.partial(event_kernel, len(highs), bool(gating), before is not None, len(deps)),
        grid=(rows // ROW_BLOCK,),
        in_specs=in_specs + [pl.BlockSpec(memory_space=pl.ANY)] * len(deps),
        out_specs=[block(D), whole(TOKEN)],
        scratch_shapes=[pltpu.VMEM((LANES, D), F32)],
        out_shape=[pltpu.VMEM((rows, D), F32), jax.ShapeDtypeStruct(TOKEN, F32)],
        input_output_aliases=aliases,
        compiler_params=params(EVENT_MIB),
        cost_estimate=pl.CostEstimate(
            flops=6 * rows * D * sum(v.shape[1] for v in highs), bytes_accessed=rows * 4000, transcendentals=0
        ),
    )(*args, *deps)


def place_kernel(own, other, *refs):
    out, token, sems = refs[-3:]
    rows = own.shape[0]
    side = lax.axis_index("tp") & 1
    copies = [
        pltpu.make_async_copy(v, out.at[pl.ds(pl.multiple_of(at * rows, ROW_BLOCK), rows), :], sems.at[k])
        for k, (v, at) in enumerate(((own, side), (other, 1 - side)))
    ]
    for copy in copies:
        copy.start()
    token[...] = jnp.zeros_like(token)
    for copy in copies:
        copy.wait()


def place(own, other, deps):
    rows, width = own.shape
    anywhere = pl.BlockSpec(memory_space=pl.ANY)
    return pl.pallas_call(
        place_kernel,
        in_specs=[anywhere] * (2 + len(deps)),
        out_specs=[pl.BlockSpec(memory_space=pltpu.HBM), pl.BlockSpec(memory_space=pltpu.VMEM)],
        scratch_shapes=[pltpu.SemaphoreType.DMA((2,))],
        out_shape=[jax.ShapeDtypeStruct((2 * rows, width), F32), jax.ShapeDtypeStruct(TOKEN, F32)],
        compiler_params=params(SMALL_MIB),
        cost_estimate=pl.CostEstimate(flops=0, bytes_accessed=rows * width * 16, transcendentals=0),
    )(own, other, *deps)


class Job:
    def __init__(self, args, shapes, body, scratch=()):
        self.args, self.body, self.scratch = args, body, list(scratch)
        self.shapes = [jax.ShapeDtypeStruct(shape, F32) for shape in shapes]


def copy_job(*arrays):
    def body(ins, outs, scratch):
        for a, b in zip(ins, outs):
            b[...] = a[...]

    return Job(arrays, [a.shape for a in arrays], body)


def run(jobs, deps=(), through=()):
    args = [a for job in jobs for a in job.args]
    shapes = [o for job in jobs for o in job.shapes]
    scratch = [v for job in jobs for v in job.scratch]

    def kernel(*refs):
        ins, refs = refs[: len(args)], refs[len(args) + len(through) + len(deps) :]
        outs, token, kept = refs[: len(shapes)], refs[len(shapes) + len(through)], refs[len(shapes) + len(through) + 1 :]
        token[...] = jnp.zeros_like(token)
        i = o = k = 0
        for job in jobs:
            ni, no, nk = len(job.args), len(job.shapes), len(job.scratch)
            job.body(ins[i : i + ni], outs[o : o + no], kept[k : k + nk])
            i, o, k = i + ni, o + no, k + nk

    vmem, anywhere = pl.BlockSpec(memory_space=pltpu.VMEM), pl.BlockSpec(memory_space=pl.ANY)
    flat = pl.pallas_call(
        kernel,
        in_specs=[vmem] * len(args) + [anywhere] * (len(through) + len(deps)),
        out_specs=[vmem] * len(shapes) + [anywhere] * len(through) + [vmem],
        out_shape=shapes
        + [jax.ShapeDtypeStruct(v.shape, v.dtype) for v in through]
        + [jax.ShapeDtypeStruct(TOKEN, F32)],
        scratch_shapes=scratch,
        input_output_aliases={len(args) + k: len(shapes) + k for k in range(len(through))},
        compiler_params=params(SMALL_MIB),
        cost_estimate=pl.CostEstimate(flops=0, bytes_accessed=sum(8 * a.size for a in args), transcendentals=0),
    )(*args, *through, *deps)
    result = []
    for job in jobs:
        result.append(list(flat[: len(job.shapes)]))
        flat = flat[len(job.shapes) :]
    return result, list(flat[:-1]), flat[-1]


def part_of(ref, index, rows):
    return ref.at[pl.ds(pl.multiple_of(index * rows, 8), rows), :]


class Piece:
    def __init__(self, array, at=0, rows=None):
        self.array, self.at = array, at
        self.rows = array.shape[0] if rows is None else rows

    def of(self, ref):
        return ref.at[pl.ds(self.at, self.rows), :]


def bit_groups(bits, width):
    groups, start = [], 0
    while bits - start > width:
        groups.append((start, width))
        start += width
    return groups, (start, bits - start)


class Reduction:
    def __init__(self, own, got, n_dp, kind):
        self.keep, self.got = [Piece(v) for v in own], [Piece(v) for v in got]
        pairs, last = bit_groups(n_dp.bit_length() - 1, 2)
        singles, lone = bit_groups(n_dp.bit_length() - 1, 1)
        if kind == "single":
            scatter, last, gather = singles, lone, singles
        elif kind == "pair":
            scatter, gather = pairs, pairs
        else:
            scatter, gather = [(b + k, 1) for b, n in pairs for k in reversed(range(n))], pairs
        self.order = [*scatter, last, *reversed(gather)]
        self.scattered = len(scatter)
        unit = 8 << sum(n for _, n in scatter)
        self.rows = -(-sum(p.rows for p in self.keep) // unit) * unit
        self.n_dp = n_dp
        self.stage = 0

    @property
    def finished(self):
        return self.stage > len(self.order)

    @property
    def joining(self):
        return self.stage == len(self.order)

    def job(self):
        stage = self.stage
        gather, scatter = stage > self.scattered + 1, stage < self.scattered
        n = len(self.keep)
        pieces = [*self.keep, *self.got]
        came = self.order[stage - 1]
        goes = self.order[stage] if stage < len(self.order) else None
        rows = self.rows if stage == 0 else self.keep[0].rows * ((1 << came[1]) if gather else 1)
        parts = 1 << goes[1] if scatter else 1

        def body(ins, outs, scratch):
            ins = [p.of(ref) for p, ref in zip(pieces, ins)]
            to = scratch[0] if scatter else outs[0]
            if gather:
                join(ins, to, came)
                return
            at = 0
            for k, piece in enumerate(pieces[:n]):
                total = ins[k][...]
                for v in ins[k + n :: n]:
                    total = total + v[...]
                to[at : at + piece.rows, :] = total
                at += piece.rows
            if at < rows:
                to[at:rows, :] = jnp.zeros((rows - at, LANES), F32)
            if scatter:
                side = side_of(goes)
                for m in range(parts):
                    outs[m][...] = part_of(to, side ^ m, rows // parts)[...]

        arrays = [p.array for p in pieces]
        if scatter:
            return Job(arrays, [(rows // parts, LANES)] * parts, body, [pltpu.VMEM((rows, LANES), F32)])
        return Job(arrays, [(rows, LANES)], body)

    def take(self, outs):
        self.stage += 1
        self.keep = [Piece(outs[0])]
        if self.stage <= len(self.order):
            sent = outs[1:] if self.stage <= self.scattered else None
            self.got = [Piece(v) for v in exchange(outs[0], sent, self.order[self.stage - 1], self.n_dp)]

    @staticmethod
    def take_together(units, out, rows):
        at = 0
        came = exchange(out, None, units[0].order[units[0].stage], units[0].n_dp)
        for unit, n in zip(units, rows):
            unit.stage += 1
            unit.keep, unit.got = [Piece(out, at, n)], [Piece(v, at, n) for v in came]
            at += n


def exchange(whole, parts, bits, n_dp):
    start, n = bits
    return [
        lax.ppermute(whole if parts is None else parts[m - 1], "dp", [(i, i ^ (m << start)) for i in range(n_dp)])
        for m in range(1, 1 << n)
    ]


def side_of(bits):
    return (lax.axis_index("dp") >> bits[0]) & ((1 << bits[1]) - 1)


def join(ins, to, bits):
    for m, v in enumerate(ins):
        part_of(to, side_of(bits) ^ m, v.shape[0])[...] = v[...]


def together(jobs):
    rows = [job.shapes[0].shape[0] for job in jobs]

    def body(ins, outs, scratch):
        at = i = 0
        for job, n in zip(jobs, rows):
            job.body(ins[i : i + len(job.args)], [outs[0].at[pl.ds(at, n), :]], [])
            i, at = i + len(job.args), at + n

    return Job([a for job in jobs for a in job.args], [(sum(rows), LANES)], body), rows


def finish_body(joining, ins, outs, both):
    in_grad, in_bias, out_grad, out_bias, gain, shift, gate = outs
    odd = (lax.axis_index("tp") & 1) == 1
    ins, both, summed = list(ins), list(both), []
    for bits, pieces in joining:
        parts = [piece.of(ins.pop(0)) for piece in pieces]
        if bits:
            join(parts, both[0], bits)
            summed.append(both.pop(0))
        else:
            summed.append(parts[0])
    for u, unit in enumerate(UNITS):
        at = 0
        for g in unit:
            group = GROUPS[g]
            for t in range(WIDE // LANES):
                for e in group:
                    tile = summed[u][at : at + SLICE, :]
                    at += SLICE
                    if t < D // LANES:
                        in_grad[e, :, t * LANES : (t + 1) * LANES] = tile
                    else:
                        out_grad[e, :, t * LANES - D : (t + 1) * LANES - D] = tile
    sums = summed[-1][at : at + 8 * len(GROUPS), :]
    sums = jnp.where(odd, sums[:, SLICE:], sums[:, :SLICE])
    for g, group in enumerate(GROUPS):
        for i, e in enumerate(group):
            for k, ref in enumerate((in_bias, out_bias, gain, shift)):
                ref[e : e + 1, :] = sums[8 * g + 4 * i + k : 8 * g + 4 * i + k + 1, :]
    for t in range(D // LANES):
        gate[:, t * LANES : (t + 1) * LANES] = summed[-1][at + 64 + 16 * t : at + 64 + 16 * t + GATE_COLS, :]


def per_device(
    events,
    valid_counts,
    mix_cotangent,
    expert_in,
    expert_in_bias,
    expert_out,
    expert_out_bias,
    norm_gain,
    norm_shift,
    gate_weight,
):
    n_dp = lax.axis_size("dp")
    rows = events.shape[0] // 2
    w_in = jnp.swapaxes(expert_in, 1, 2)
    w_out = jnp.swapaxes(expert_out, 1, 2)
    gate_w = jnp.swapaxes(gate_weight, 0, 1)
    core = [(i, i ^ 1) for i in range(4)]
    across = [(i, i ^ 2) for i in range(4)]
    vectors = [expert_in_bias, expert_out_bias, norm_gain, norm_shift]
    own = list(payload(GROUPS[:1], w_in, w_out, vectors, []))
    far = [lax.ppermute(own[0], "tp", across)]
    beside = [lax.ppermute(own[0], "tp", core)]
    own += payload(GROUPS[1:], w_in, w_out, [], own)
    high, low, p, cot = gates(valid_counts, events, mix_cotangent, gate_w, rows, own[1:2])
    relayed = []
    summing = {}
    partial = []
    made = []
    placed, unplaced = [], []
    mix = small = x_grad = None
    deps = [p]
    for kind, what, units in PLAN:
        if kind == "experts":
            last = what == len(GROUPS) - 1
            shards = (own[what], beside[what], far[what], relayed[what])
            before = ([m[1] for m in made], [m[8] for m in made]) if last else None
            made.append(experts(GROUPS[what], rows, high, low, cot, p, shards, small, mix, before, deps))
            mix = made[what][0]
            small = made[0][9]
            deps = [made[what][8]]
        elif kind == "events":
            ours = [[made[g][k] for g in what] for k in (2, 3, 4, 5)]
            gating = [made[-1][1], gate_w] if what[-1] == len(GROUPS) - 1 else []
            x_grad, token = event_grads(rows, *ours, gating, x_grad, deps)
            deps = [token]
        elif kind == "place":
            v, token = place(*unplaced.pop(0), deps)
            placed.append(v)
            deps = [token]
        else:
            joint = units if "joint" in what else ()
            alone = () if joint else units
            jobs = [summing[u].job() for u in alone]
            sent, fetched, through = [], [], []
            if "send" in what:
                sent = [made[-1][7]] + ([made[-1][8]] if len(made) == len(GROUPS) else [])
                jobs.append(copy_job(*sent))
            if "fetch" in what:
                group = len(relayed)
                fetched = [far[group], *own[group + 1 : group + 2]]
                jobs.append(copy_job(*fetched))
            if "mix" in what:
                through.append(mix)
            if "grad" in what:
                through.append(x_grad)
            if joint:
                job, rows_of = together([summing[u].job() for u in joint])
                jobs.append(job)
            outs, through, token = run(jobs, deps, through)
            deps = [token]
            if joint:
                Reduction.take_together([summing[u] for u in joint], outs.pop()[0], rows_of)
            for u, o in zip(alone, outs):
                summing[u].take(o)
            if fetched:
                relayed.append(lax.ppermute(outs[-1][0], "tp", core))
                if len(fetched) > 1:
                    far.append(lax.ppermute(outs[-1][1], "tp", across))
                    beside.append(lax.ppermute(outs[-1][1], "tp", core))
            if sent:
                got = [lax.ppermute(v, "tp", core) for v in outs[len(alone)]]
                partial.append(([made[-1][6], *sent[1:]], got))
                for u, (unit, way) in enumerate(zip(UNITS, WAY)):
                    if unit[-1] == len(partial) - 1:
                        both = [partial[g] for g in unit]
                        summing[u] = Reduction([v for b in both for v in b[0]], [v for b in both for v in b[1]], n_dp, way)
            unplaced += [(v, lax.ppermute(v, "tp", core)) for v in through]
    mixtures, x_grad = placed
    summing = [summing[u] for u in range(len(UNITS))]
    while not all(u.finished or u.joining for u in summing):
        ours = [u for u in summing if not u.finished and not u.joining]
        outs, _, token = run([u.job() for u in ours], deps)
        deps = [token]
        for u, o in zip(ours, outs):
            u.take(o)
    joining = [(u.order[-1], [*u.keep, *u.got]) if u.joining else (None, u.keep) for u in summing]
    halves = [p.array for _, pieces in joining for p in pieces]
    per_expert = (E, SLICE)
    shapes = [(E, SLICE, D), per_expert, (E, SLICE, H), per_expert, per_expert, per_expert, (GATE_COLS, D)]
    scratch = [pltpu.VMEM((u.rows, LANES), F32) for u in summing if u.joining]
    job = Job(halves, shapes, functools.partial(finish_body, joining), scratch)
    (((in_grad, in_bias, out_grad, out_bias, gain, shift, gate),), _, _) = run([job], deps)
    return (
        mixtures,
        x_grad,
        jnp.swapaxes(in_grad, 1, 2),
        in_bias,
        jnp.swapaxes(out_grad, 1, 2),
        out_bias,
        gain,
        shift,
        jnp.swapaxes(gate, 0, 1),
    )


def solution(mesh):
    return jax.shard_map(
        per_device,
        mesh=mesh,
        in_specs=(
            P("dp", None),
            P(),
            P("dp", None),
            P(None, None, "tp"),
            P(None, "tp"),
            P(None, None, "tp"),
            P(None, "tp"),
            P(None, "tp"),
            P(None, "tp"),
            P(),
        ),
        out_specs=(
            P("dp", None),
            P("dp", None),
            P(None, None, "tp"),
            P(None, "tp"),
            P(None, None, "tp"),
            P(None, "tp"),
            P(None, "tp"),
            P(None, "tp"),
            P(),
        ),
        check_vma=False,
    )
```

```python
import functools

import jax
import jax.numpy as jnp
from jax import lax
from jax.experimental import pallas as pl
from jax.experimental.pallas import tpu as pltpu
from jax.sharding import PartitionSpec as P

D = 512
H = 256
O = 256
E = 6
GATE_COLS = 14
SLICE = 64
WIDE = D + H
LANES = 128
TOKEN = (8, LANES)
RB = 1024
ROW_BLOCK = 256
SUB = 256
LAG = 1
EPSILON = 1e-05
GROUPS = ((0, 1), (2, 3), (4,), (5,))
UNITS = ((0,), (1,), (2, 3))
WAY = ("single", "single", "pair")
SPARE = (0, 0, 0)
PLAN = (
    ("small", "fetch", ()),
    ("experts", 0, ()),
    ("small", "send", ()),
    ("events", (0,), ()),
    ("small", "fetch", (0,)),
    ("experts", 1, ()),
    ("small", "send fetch", (0,)),
    ("small", "", (1,)),
    ("experts", 2, ()),
    ("small", "send fetch", (0, 1)),
    ("experts", 3, ()),
    ("small", "send", (0, 1)),
    ("events", (2,), ()),
    ("small", "", (2,)),
    ("events", (1, 3), ()),
    ("small", "mix grad", (0, 1, 2)),
    ("small", "", (0, 1, 2)),
    ("place", None, ()),
    ("place", None, ()),
)
COLUMN = (
    {0: 0, 1: 1, 4: 2, 5: 3},
    {2: 4, 3: 5, 4: 6, 5: 7},
    {e: 8 + e for e in range(E)},
)
F32 = jnp.float32
BF16 = jnp.bfloat16
NN = (((1,), (0,)), ((), ()))
NT = (((1,), (1,)), ((), ()))
TN = (((0,), (0,)), ((), ()))


def split(v):
    high = v.astype(BF16)
    return high, (v - high.astype(F32)).astype(BF16)


def dot3(a, b, dims):
    def one(u, v):
        return lax.dot_general(u, v, dims, preferred_element_type=F32)

    return one(a[0], b[0]) + (one(a[0], b[1]) + one(a[1], b[0]))


def in_hbm(v):
    return pltpu.with_memory_space_constraint(v, pltpu.HBM)


LARGE = 60
EXPERT_MIB, EVENT_MIB, GATE_MIB, SMALL_MIB = 28, 16, 16, 8


def params(mib):
    return pltpu.CompilerParams(vmem_limit_bytes=mib << 20)


def gate_kernel(n_deps, counts, ev_ref, cot_ref, gw_ref, *refs):
    high_ref, low_ref, p_ref, cot_out, gw, held, sems = refs[n_deps:]
    rows = held.shape[0]
    steps = rows // ROW_BLOCK
    start = pl.multiple_of((lax.axis_index("tp") & 1) * rows, ROW_BLOCK)
    valid = counts[lax.axis_index("dp")]
    blocks = [slice(i * ROW_BLOCK, (i + 1) * ROW_BLOCK) for i in range(steps)]
    copies = [
        pltpu.make_async_copy(ev_ref.at[pl.ds(start + at.start, ROW_BLOCK), :], held.at[at, :], sems.at[i])
        for i, at in enumerate(blocks)
    ]
    copies.append(pltpu.make_async_copy(cot_ref.at[pl.ds(start, rows), :], cot_out, sems.at[steps]))
    for copy in copies:
        copy.start()
    gw[...] = jnp.zeros_like(gw)
    gw[:GATE_COLS, :] = gw_ref[...]
    gate = split(gw[...])
    lane = lax.broadcasted_iota(jnp.int32, (ROW_BLOCK, LANES), 1)
    sets = (lane < 4, (lane >= 4) & (lane < 8), (lane >= 8) & (lane < GATE_COLS))

    def per_set(values, empty, reduce):
        a, b, s = (reduce(jnp.where(m, values, empty), axis=1, keepdims=True) for m in sets)
        return jnp.where(sets[0], a, jnp.where(sets[1], b, s))

    for i, at in enumerate(blocks):
        copies[i].wait()
        events = split(held[at, :])
        high_ref[at, :], low_ref[at, :] = events
        logits = dot3(events, gate, NT)
        top = per_set(logits, -3e38, jnp.max)
        shares = jnp.where(lane < GATE_COLS, jnp.exp(logits - top), 0.0)
        p = shares / per_set(shares, 0.0, jnp.sum)
        row = start + at.start + lax.broadcasted_iota(jnp.int32, logits.shape, 0)
        p_ref[at, :] = jnp.where((row < valid) & (lane < GATE_COLS), p, 0.0)
    copies[-1].wait()


def gates(counts, events, cot, gate_w, rows, deps):
    vmem, hbm = pl.BlockSpec(memory_space=pltpu.VMEM), pl.BlockSpec(memory_space=pltpu.HBM)
    steps = rows // ROW_BLOCK
    return pl.pallas_call(
        functools.partial(gate_kernel, len(deps)),
        in_specs=[pl.BlockSpec(memory_space=pltpu.SMEM), hbm, hbm, vmem]
        + [pl.BlockSpec(memory_space=pl.ANY)] * len(deps),
        out_specs=[vmem] * 4,
        out_shape=[
            pltpu.VMEM((rows, D), BF16),
            pltpu.VMEM((rows, D), BF16),
            pltpu.VMEM((rows, LANES), F32),
            pltpu.VMEM((rows, 3 * O), F32),
        ],
        scratch_shapes=[
            pltpu.VMEM((LANES, D), F32),
            pltpu.VMEM((rows, D), F32),
            pltpu.SemaphoreType.DMA((steps + 1,)),
        ],
        compiler_params=params(GATE_MIB),
        cost_estimate=pl.CostEstimate(flops=6 * rows * D * LANES, bytes_accessed=rows * D * 8, transcendentals=0),
    )(counts, in_hbm(events), in_hbm(cot), in_hbm(gate_w), *deps)


def payload_kernel(groups, vectors, n_deps, w_in, w_out, *refs):
    given = refs[:4] if vectors else ()
    held = refs[-2]
    outs, sems = refs[len(given) + n_deps :][: len(groups)], refs[-1]
    copies = []
    for out, group in zip(outs, groups):
        experts_of, rows = pl.ds(group[0], len(group)), slice(0, SLICE)
        for part, lanes in ((w_in, slice(0, D)), (w_out, slice(D, WIDE))):
            copies.append(pltpu.make_async_copy(part.at[experts_of], out.at[:, rows, lanes], sems.at[len(copies)]))
    for k, v in enumerate(given):
        copies.append(pltpu.make_async_copy(v, held.at[k, slice(0, E), :], sems.at[len(copies)]))
    for copy in copies:
        copy.start()
    if vectors:
        for copy in copies[-len(given) :]:
            copy.wait()
        copies = copies[: -len(given)]
        rows = jnp.concatenate([held[k, :E, :] for k in range(4)], axis=0)
        outs[0][:, SLICE:, :] = jnp.zeros((len(groups[0]), 8, WIDE), F32)
        for j in range(4 * E // 8):
            outs[0][0, SLICE:, j * LANES : j * LANES + SLICE] = rows[8 * j : 8 * j + 8, :]
    for copy in copies:
        copy.wait()


def payload(groups, w_in, w_out, vectors, deps):
    vmem, hbm = pl.BlockSpec(memory_space=pltpu.VMEM), pl.BlockSpec(memory_space=pltpu.HBM)
    rows = SLICE + 8 if vectors else SLICE
    return pl.pallas_call(
        functools.partial(payload_kernel, groups, bool(vectors), len(deps)),
        in_specs=[hbm, hbm] + [hbm] * len(vectors) + [pl.BlockSpec(memory_space=pl.ANY)] * len(deps),
        out_specs=[vmem] * len(groups),
        out_shape=[pltpu.VMEM((len(group), rows, WIDE), F32) for group in groups],
        scratch_shapes=[pltpu.VMEM((4, 8, SLICE), F32), pltpu.SemaphoreType.DMA((2 * len(groups) + 4,))],
        compiler_params=params(SMALL_MIB),
        cost_estimate=pl.CostEstimate(flops=0, bytes_accessed=SLICE * WIDE * 16, transcendentals=0),
    )(in_hbm(w_in), in_hbm(w_out), *[in_hbm(v) for v in vectors], *deps)


def expert_kernel(group, first, last, n_deps, *refs):
    n = len(group)
    refs = list(refs)
    evh_ref, evl_ref, cot_ref, p_ref = refs[:4]
    shards = refs[4:8]
    del refs[:8]
    small = None if first else refs.pop(0)
    mix_in = None if first else refs.pop(0)
    if last:
        dp_before, sums_before = refs[: len(GROUPS) - 1], refs[len(GROUPS) - 1 : 2 * len(GROUPS) - 2]
        del refs[: 2 * len(GROUPS) - 2]
    del refs[:n_deps]
    mix_ref, dp_ref, dph_ref, dpl_ref, winh, winl, own_ref, part_ref, sums_ref = refs[:9]
    del refs[:9]
    if first:
        small = refs.pop(0)
    wouth, woutl, acc, sums = refs[:4]
    gate_acc = refs[4] if last else None
    step, steps = pl.program_id(0), pl.num_programs(0)
    odd = lax.axis_index("tp") & 1
    chip = lax.axis_index("tp") >> 1

    def tile(start, other):
        return pl.ds(pl.multiple_of(start + (chip ^ other) * LANES, LANES), LANES)

    @pl.when(step == 0)
    def _():
        acc[...] = jnp.zeros_like(acc)
        sums[...] = jnp.zeros_like(sums)
        if last:
            gate_acc[...] = jnp.zeros_like(gate_acc)
        for j in range(4 * E // 8 if first else 0):
            vectors = [shard[0, SLICE:, j * LANES : j * LANES + SLICE] for shard in shards]
            even_order, odd_order = (jnp.concatenate([vectors[k ^ c] for k in range(4)], axis=1) for c in range(2))
            small[8 * j : 8 * j + 8, :] = jnp.where(odd == 1, odd_order, even_order)
        if first:
            bias = small[E : 2 * E, :]
            small[E : 2 * E, :] = bias - jnp.mean(bias, axis=1, keepdims=True)
        own_rows = slice(0, SLICE)
        for i, e in enumerate(group):
            parts = [
                (shard[i, own_rows, :D], jnp.concatenate([shard[i, own_rows, tile(D, k)] for k in range(2)], axis=1))
                for shard in shards
            ]
            centre = sum(jnp.sum(out, axis=0, keepdims=True) for _, out in parts) / O
            for k, (into, out) in enumerate(parts):
                at = pl.multiple_of((odd ^ k) * SLICE, SLICE)
                winh[pl.ds(i * H + at, SLICE), :], winl[pl.ds(i * H + at, SLICE), :] = split(into)
                wouth[i, pl.ds(at, SLICE), :], woutl[i, pl.ds(at, SLICE), :] = split(out - centre)

    subs = RB // SUB
    rows_of = [slice(s * SUB, (s + 1) * SUB) for s in range(subs)]
    lane = lax.broadcasted_iota(jnp.int32, (SUB, LANES), 1)
    vector = lambda k, e: small[k * E + e : k * E + e + 1, :]
    state = [dict() for _ in range(subs)]

    def m1(s):
        events = evh_ref[rows_of[s], :], evl_ref[rows_of[s], :]
        state[s]["events"] = events
        pre = dot3(events, (winh[...], winl[...]), NT)
        state[s]["pre"] = [pre[:, i * H : (i + 1) * H] for i in range(n)]

    def v1(s):
        st = state[s]
        st["sigma"], st["hidden"], st["hidden_parts"] = [], [], []
        for i, e in enumerate(group):
            pre = st["pre"][i] + vector(0, e)
            sigma = jax.nn.sigmoid(pre)
            hidden = pre * sigma
            st["sigma"].append(sigma)
            st["hidden"].append(hidden)
            st["hidden_parts"].append(split(hidden))

    def m2(s):
        st = state[s]
        st["centred"] = [dot3(st["hidden_parts"][i], (wouth[i], woutl[i]), NT) for i in range(n)]

    def v2(s):
        st = state[s]
        p = p_ref[rows_of[s], :]
        dp = jnp.zeros_like(p)
        mixed = {}
        cots = [
            jnp.concatenate([cot_ref[rows_of[s], tile(t * O, 0)], cot_ref[rows_of[s], tile(t * O, 1)]], axis=1)
            for t in range(3)
        ]
        st["dnormed"] = []
        for i, e in enumerate(group):
            gain, shift = vector(2, e), vector(3, e)
            centred = st["centred"][i] + vector(1, e)
            rstd = lax.rsqrt(jnp.mean(centred * centred, axis=1, keepdims=True) + EPSILON)
            unit = centred * rstd
            y = unit * gain + shift
            dy = None
            for t in range(3):
                if e not in COLUMN[t]:
                    continue
                column = COLUMN[t][e]
                coef = p[:, column : column + 1]
                mixed[t] = coef * y + mixed[t] if t in mixed else coef * y
                dp = jnp.where(lane == column, jnp.sum(cots[t] * y, axis=1, keepdims=True), dp)
                dy = coef * cots[t] if dy is None else dy + coef * cots[t]
            dunit = dy * gain
            back_first = jnp.mean(dunit, axis=1, keepdims=True)
            back_second = jnp.mean(dunit * unit, axis=1, keepdims=True)
            dnormed = rstd * (dunit - back_first - unit * back_second)
            st["dnormed"].append(split(dnormed))
            dy_half = dy[:, :LANES]
            for k, v in enumerate((dnormed[:, :LANES], dy_half * unit[:, :LANES], dy_half)):
                sums[4 * i + k + 1 : 4 * i + k + 2, :] += jnp.sum(v, axis=0, keepdims=True)
        for t in range(3):
            for other in range(2):
                at = tile(t * O, other)
                if t in mixed:
                    value = mixed[t][:, other * LANES : (other + 1) * LANES]
                    mix_ref[rows_of[s], at] = value if first else mix_in[rows_of[s], at] + value
                elif first:
                    mix_ref[rows_of[s], at] = jnp.zeros((SUB, LANES), F32)
                else:
                    mix_ref[rows_of[s], at] = mix_in[rows_of[s], at]
        if last:
            for other in dp_before:
                dp = dp + other[rows_of[s], :]
            weighted = p * dp
            sets = (lane < 4, (lane >= 4) & (lane < 8), (lane >= 8) & (lane < GATE_COLS))
            a, b, c = (jnp.sum(jnp.where(m, weighted, 0.0), axis=1, keepdims=True) for m in sets)
            dp = weighted - p * jnp.where(sets[0], a, jnp.where(sets[1], b, c))
            st["dlogits"] = dp
        dp_ref[rows_of[s], :] = dp

    def m3(s):
        st = state[s]
        st["dhidden"] = [dot3(st["dnormed"][i], (wouth[i], woutl[i]), NN) for i in range(n)]

    def v3(s):
        st = state[s]
        st["dpre"] = []
        for i, e in enumerate(group):
            sigma, hidden = st["sigma"][i], st["hidden"][i]
            dpre = st["dhidden"][i] * (sigma + hidden * (1.0 - sigma))
            parts = split(dpre)
            dph_ref[rows_of[s], i * H : (i + 1) * H], dpl_ref[rows_of[s], i * H : (i + 1) * H] = parts
            st["dpre"].append(tuple(v[:, :LANES] for v in parts))
            sums[4 * i : 4 * i + 1, :] += jnp.sum(dpre[:, :LANES], axis=0, keepdims=True)

    def m4(s):
        st = state[s]
        for i in range(n):
            halves = tuple(v[:, :LANES] for v in st["dnormed"][i])
            acc[i * LANES : (i + 1) * LANES, D:] += dot3(halves, st["hidden_parts"][i], TN)
        beside = [split(st["dlogits"][:, :16])] if last else []
        left = tuple(jnp.concatenate([h[k] for h in st["dpre"] + beside], axis=1) for k in range(2))
        both = dot3(left, st["events"], TN)
        acc[:, :D] += both[: n * LANES]
        if last:
            gate_acc[...] += both[n * LANES : n * LANES + 16]

    stages = (m1, v1, m2, v2, m3, v3, m4)
    for turn in range(len(stages) + LAG * (subs - 1)):
        for s in range(subs):
            if 0 <= turn - LAG * s < len(stages):
                stages[turn - LAG * s](s)

    @pl.when(step == steps - 1)
    def _():
        mine = pl.multiple_of(odd * SLICE, SLICE)
        other = pl.multiple_of(SLICE - mine, SLICE)
        for i in range(n):
            for t in range(WIDE // LANES):
                at = slice((t * n + i) * SLICE, (t * n + i + 1) * SLICE)
                lanes = slice(t * LANES, (t + 1) * LANES) if t < D // LANES else tile(D, t - D // LANES)
                own_ref[at, :] = acc[pl.ds(i * LANES + mine, SLICE), lanes]
                part_ref[at, :] = acc[pl.ds(i * LANES + other, SLICE), lanes]
        if last:
            for g, before in enumerate(sums_before):
                sums_ref[8 * g : 8 * g + 8, :] = before[...]
            g = len(GROUPS) - 1
            sums_ref[8 * g : 8 * g + 8, :] = sums[...]
            for t in range(D // LANES):
                sums_ref[8 * g + 8 + 16 * t : 8 * g + 24 + 16 * t, :] = gate_acc[:, t * LANES : (t + 1) * LANES]
        else:
            sums_ref[...] = sums[...]


def experts(group, rows, high, low, cot, p, shards, small, mix, before, deps):
    n = len(group)
    first, last = mix is None, before is not None
    steps = rows // RB
    block = lambda width: pl.BlockSpec((RB, width), lambda i: (i, 0))
    whole = lambda shape: pl.BlockSpec(shape, lambda i: (0,) * len(shape))
    in_specs = [
        block(D),
        block(D),
        block(3 * O),
        block(LANES),
        *[whole(shards[0].shape)] * 4,
    ]
    args = [high, low, cot, p, *shards]
    aliases = {}
    if not first:
        aliases = {len(args) + 1: 0}
        in_specs += [whole((4 * E, H)), block(3 * O)]
        args += [small, mix]
    if last:
        in_specs += [block(LANES)] * len(before[0]) + [whole((8, LANES))] * len(before[1])
        args += [*before[0], *before[1]]
    in_specs += [pl.BlockSpec(memory_space=pl.ANY)] * len(deps)
    args += deps
    payload = WIDE // LANES * n * SLICE
    sums_shape = (8 * len(GROUPS) + 16 * (D // LANES), LANES) if last else (8, LANES)
    scratch = [
        pltpu.VMEM((n, O, H), BF16),
        pltpu.VMEM((n, O, H), BF16),
        pltpu.VMEM((n * LANES, WIDE), F32),
        pltpu.VMEM((8, LANES), F32),
    ]
    if last:
        scratch.append(pltpu.VMEM((16, D), F32))
    return pl.pallas_call(
        functools.partial(expert_kernel, group, first, last, len(deps)),
        grid=(steps,),
        in_specs=in_specs,
        out_specs=[
                block(3 * O),
                block(LANES),
                block(n * H),
                block(n * H),
                whole((n * H, D)),
                whole((n * H, D)),
                whole((payload, LANES)),
                whole((payload, LANES)),
                whole(sums_shape),
        ]
        + [whole((4 * E, H))] * first,
        scratch_shapes=scratch,
        out_shape=[
            jax.ShapeDtypeStruct((rows, 3 * O), F32),
            jax.ShapeDtypeStruct((rows, LANES), F32),
            jax.ShapeDtypeStruct((rows, n * H), BF16),
            jax.ShapeDtypeStruct((rows, n * H), BF16),
            jax.ShapeDtypeStruct((n * H, D), BF16),
            jax.ShapeDtypeStruct((n * H, D), BF16),
            jax.ShapeDtypeStruct((payload, LANES), F32),
            jax.ShapeDtypeStruct((payload, LANES), F32),
            jax.ShapeDtypeStruct(sums_shape, F32),
        ]
        + [jax.ShapeDtypeStruct((4 * E, H), F32)] * first,
        input_output_aliases=aliases,
        compiler_params=params(EXPERT_MIB),
        cost_estimate=pl.CostEstimate(flops=n * rows * 6 * 720896, bytes_accessed=rows * 14000, transcendentals=0),
    )(*args)


def event_kernel(n, last, added, n_deps, *refs):
    highs, lows, winh, winl = (refs[k * n : (k + 1) * n] for k in range(4))
    refs = list(refs[4 * n :])
    total = 0.0
    if last:
        dlogits, gw_ref, gw = refs.pop(0), refs.pop(0), refs[-1]
        gw[...] = jnp.zeros_like(gw)
        gw[:GATE_COLS, :] = gw_ref[...]
        total = dot3(split(dlogits[...]), split(gw[...]), NN)
    before = refs.pop(0) if added else None
    out, token = refs[n_deps : n_deps + 2]
    for g in range(n):
        total = total + dot3((highs[g][...], lows[g][...]), (winh[g][...], winl[g][...]), NN)
    out[...] = total + before[...] if added else total
    token[...] = jnp.zeros_like(token)


def event_grads(rows, highs, lows, winh, winl, gating, before, deps):
    block = lambda width: pl.BlockSpec((ROW_BLOCK, width), lambda i: (i, 0))
    whole = lambda shape: pl.BlockSpec(shape, lambda i: (0, 0))
    args = [*highs, *lows, *winh, *winl]
    in_specs = [block(v.shape[1]) for v in (*highs, *lows)] + [whole(v.shape) for v in (*winh, *winl)]
    aliases = {}
    if gating:
        args += gating
        in_specs += [block(LANES), whole((GATE_COLS, D))]
    if before is not None:
        aliases = {len(args): 0}
        args.append(before)
        in_specs.append(block(D))
    return pl.pallas_call(
        functools.partial(event_kernel, len(highs), bool(gating), before is not None, len(deps)),
        grid=(rows // ROW_BLOCK,),
        in_specs=in_specs + [pl.BlockSpec(memory_space=pl.ANY)] * len(deps),
        out_specs=[block(D), whole(TOKEN)],
        scratch_shapes=[pltpu.VMEM((LANES, D), F32)],
        out_shape=[pltpu.VMEM((rows, D), F32), jax.ShapeDtypeStruct(TOKEN, F32)],
        input_output_aliases=aliases,
        compiler_params=params(EVENT_MIB),
        cost_estimate=pl.CostEstimate(
            flops=6 * rows * D * sum(v.shape[1] for v in highs), bytes_accessed=rows * 4000, transcendentals=0
        ),
    )(*args, *deps)


def place_kernel(own, other, *refs):
    out, token, sems = refs[-3:]
    rows = own.shape[0]
    side = lax.axis_index("tp") & 1
    copies = [
        pltpu.make_async_copy(v, out.at[pl.ds(pl.multiple_of(at * rows, ROW_BLOCK), rows), :], sems.at[k])
        for k, (v, at) in enumerate(((own, side), (other, 1 - side)))
    ]
    for copy in copies:
        copy.start()
    token[...] = jnp.zeros_like(token)
    for copy in copies:
        copy.wait()


def place(own, other, deps):
    rows, width = own.shape
    anywhere = pl.BlockSpec(memory_space=pl.ANY)
    return pl.pallas_call(
        place_kernel,
        in_specs=[anywhere] * (2 + len(deps)),
        out_specs=[pl.BlockSpec(memory_space=pltpu.HBM), pl.BlockSpec(memory_space=pltpu.VMEM)],
        scratch_shapes=[pltpu.SemaphoreType.DMA((2,))],
        out_shape=[jax.ShapeDtypeStruct((2 * rows, width), F32), jax.ShapeDtypeStruct(TOKEN, F32)],
        compiler_params=params(SMALL_MIB),
        cost_estimate=pl.CostEstimate(flops=0, bytes_accessed=rows * width * 16, transcendentals=0),
    )(own, other, *deps)


class Job:
    def __init__(self, args, shapes, body, scratch=()):
        self.args, self.body, self.scratch = args, body, list(scratch)
        self.shapes = [jax.ShapeDtypeStruct(shape, F32) for shape in shapes]


def copy_job(*arrays):
    def body(ins, outs, scratch):
        for a, b in zip(ins, outs):
            b[...] = a[...]

    return Job(arrays, [a.shape for a in arrays], body)


def run(jobs, deps=(), through=()):
    args = [a for job in jobs for a in job.args]
    shapes = [o for job in jobs for o in job.shapes]
    scratch = [v for job in jobs for v in job.scratch]

    def kernel(*refs):
        ins, refs = refs[: len(args)], refs[len(args) + len(through) + len(deps) :]
        outs, token, kept = refs[: len(shapes)], refs[len(shapes) + len(through)], refs[len(shapes) + len(through) + 1 :]
        token[...] = jnp.zeros_like(token)
        i = o = k = 0
        for job in jobs:
            ni, no, nk = len(job.args), len(job.shapes), len(job.scratch)
            job.body(ins[i : i + ni], outs[o : o + no], kept[k : k + nk])
            i, o, k = i + ni, o + no, k + nk

    vmem, anywhere = pl.BlockSpec(memory_space=pltpu.VMEM), pl.BlockSpec(memory_space=pl.ANY)
    flat = pl.pallas_call(
        kernel,
        in_specs=[vmem] * len(args) + [anywhere] * (len(through) + len(deps)),
        out_specs=[vmem] * len(shapes) + [anywhere] * len(through) + [vmem],
        out_shape=shapes
        + [jax.ShapeDtypeStruct(v.shape, v.dtype) for v in through]
        + [jax.ShapeDtypeStruct(TOKEN, F32)],
        scratch_shapes=scratch,
        input_output_aliases={len(args) + k: len(shapes) + k for k in range(len(through))},
        compiler_params=params(SMALL_MIB),
        cost_estimate=pl.CostEstimate(flops=0, bytes_accessed=sum(8 * a.size for a in args), transcendentals=0),
    )(*args, *through, *deps)
    result = []
    for job in jobs:
        result.append(list(flat[: len(job.shapes)]))
        flat = flat[len(job.shapes) :]
    return result, list(flat[:-1]), flat[-1]


def part_of(ref, index, rows):
    return ref.at[pl.ds(pl.multiple_of(index * rows, 8), rows), :]


class Piece:
    def __init__(self, array, at=0, rows=None):
        self.array, self.at = array, at
        self.rows = array.shape[0] if rows is None else rows

    def of(self, ref):
        return ref.at[pl.ds(self.at, self.rows), :]


def bit_groups(bits, width):
    groups, start = [], 0
    while bits - start > width:
        groups.append((start, width))
        start += width
    return groups, (start, bits - start)


class Reduction:
    def __init__(self, own, got, n_dp, kind, spare):
        self.spare = spare
        self.keep, self.got = [Piece(v) for v in own], [Piece(v) for v in got]
        pairs, last = bit_groups(n_dp.bit_length() - 1, 2)
        singles, lone = bit_groups(n_dp.bit_length() - 1, 1)
        if kind == "single":
            scatter, last, gather = singles, lone, singles
        elif kind == "pair":
            scatter, gather = pairs, pairs
        else:
            scatter, gather = [(b + k, 1) for b, n in pairs for k in reversed(range(n))], pairs
        self.order = [*scatter, last, *reversed(gather)]
        self.scattered = len(scatter)
        unit = 8 << sum(n for _, n in scatter)
        self.rows = -(-sum(p.rows for p in self.keep) // unit) * unit
        self.n_dp = n_dp
        self.stage = 0

    @property
    def finished(self):
        return self.stage > len(self.order)

    @property
    def joining(self):
        return self.stage == len(self.order)

    def job(self):
        stage = self.stage
        gather, scatter = stage > self.scattered + 1, stage < self.scattered
        n = len(self.keep)
        pieces = [*self.keep, *self.got]
        came = self.order[stage - 1]
        goes = self.order[stage] if stage < len(self.order) else None
        rows = self.rows if stage == 0 else self.keep[0].rows * ((1 << came[1]) if gather else 1)
        parts = 1 << goes[1] if scatter else 1

        def body(ins, outs, scratch):
            ins = [p.of(ref) for p, ref in zip(pieces, ins)]
            to = scratch[0] if scatter else outs[0]
            if gather:
                join(ins, to, came)
                return
            at = 0
            for k, piece in enumerate(pieces[:n]):
                total = ins[k][...]
                for v in ins[k + n :: n]:
                    total = total + v[...]
                to[at : at + piece.rows, :] = total
                at += piece.rows
            if at < to.shape[0]:
                to[at:, :] = jnp.zeros((to.shape[0] - at, LANES), F32)
            if scatter:
                side = side_of(goes)
                for m in range(parts):
                    outs[m][...] = part_of(to, side ^ m, rows // parts)[...]

        arrays = [p.array for p in pieces]
        if scatter:
            return Job(arrays, [(rows // parts, LANES)] * parts, body, [pltpu.VMEM((rows, LANES), F32)])
        self.used = rows
        return Job(arrays, [(rows + (self.spare if stage == self.scattered else 0), LANES)], body)

    def take(self, outs):
        self.stage += 1
        scatters = self.stage <= self.scattered
        rows = None if scatters else self.used
        self.keep = [Piece(outs[0], 0, rows)]
        if self.stage <= len(self.order):
            sent = outs[1:] if scatters else None
            self.got = [Piece(v, 0, rows) for v in exchange(outs[0], sent, self.order[self.stage - 1], self.n_dp)]

    @staticmethod
    def take_together(units, out, rows):
        at = 0
        came = exchange(out, None, units[0].order[units[0].stage], units[0].n_dp)
        for unit, n in zip(units, rows):
            unit.stage += 1
            unit.keep, unit.got = [Piece(out, at, n)], [Piece(v, at, n) for v in came]
            at += n


def exchange(whole, parts, bits, n_dp):
    start, n = bits
    return [
        lax.ppermute(whole if parts is None else parts[m - 1], "dp", [(i, i ^ (m << start)) for i in range(n_dp)])
        for m in range(1, 1 << n)
    ]


def side_of(bits):
    return (lax.axis_index("dp") >> bits[0]) & ((1 << bits[1]) - 1)


def join(ins, to, bits):
    for m, v in enumerate(ins):
        part_of(to, side_of(bits) ^ m, v.shape[0])[...] = v[...]


def together(jobs):
    rows = [job.shapes[0].shape[0] for job in jobs]

    def body(ins, outs, scratch):
        at = i = 0
        for job, n in zip(jobs, rows):
            job.body(ins[i : i + len(job.args)], [outs[0].at[pl.ds(at, n), :]], [])
            i, at = i + len(job.args), at + n

    return Job([a for job in jobs for a in job.args], [(sum(rows), LANES)], body), rows


def finish_body(joining, ins, outs, both):
    in_grad, in_bias, out_grad, out_bias, gain, shift, gate = outs
    odd = (lax.axis_index("tp") & 1) == 1
    ins, both, summed = list(ins), list(both), []
    for bits, pieces in joining:
        parts = [piece.of(ins.pop(0)) for piece in pieces]
        if bits:
            join(parts, both[0], bits)
            summed.append(both.pop(0))
        else:
            summed.append(parts[0])
    for u, unit in enumerate(UNITS):
        at = 0
        for g in unit:
            group = GROUPS[g]
            for t in range(WIDE // LANES):
                for e in group:
                    tile = summed[u][at : at + SLICE, :]
                    at += SLICE
                    if t < D // LANES:
                        in_grad[e, :, t * LANES : (t + 1) * LANES] = tile
                    else:
                        out_grad[e, :, t * LANES - D : (t + 1) * LANES - D] = tile
    sums = summed[-1][at : at + 8 * len(GROUPS), :]
    sums = jnp.where(odd, sums[:, SLICE:], sums[:, :SLICE])
    start = at + 8 * len(GROUPS)
    for g, group in enumerate(GROUPS):
        for i, e in enumerate(group):
            for k, ref in enumerate((in_bias, out_bias, gain, shift)):
                ref[e : e + 1, :] = sums[8 * g + 4 * i + k : 8 * g + 4 * i + k + 1, :]
    for t in range(D // LANES):
        gate[:, t * LANES : (t + 1) * LANES] = summed[-1][start + 16 * t : start + 16 * t + GATE_COLS, :]


def per_device(
    events,
    valid_counts,
    mix_cotangent,
    expert_in,
    expert_in_bias,
    expert_out,
    expert_out_bias,
    norm_gain,
    norm_shift,
    gate_weight,
):
    n_dp = lax.axis_size("dp")
    rows = events.shape[0] // 2
    w_in = jnp.swapaxes(expert_in, 1, 2)
    w_out = jnp.swapaxes(expert_out, 1, 2)
    gate_w = jnp.swapaxes(gate_weight, 0, 1)
    core = [(i, i ^ 1) for i in range(4)]
    across = [(i, i ^ 2) for i in range(4)]
    vectors = [expert_in_bias, expert_out_bias, norm_gain, norm_shift]
    own = list(payload(GROUPS[:1], w_in, w_out, vectors, []))
    far = [lax.ppermute(own[0], "tp", across)]
    beside = [lax.ppermute(own[0], "tp", core)]
    own += payload(GROUPS[1:], w_in, w_out, [], own)
    high, low, p, cot = gates(valid_counts, events, mix_cotangent, gate_w, rows, own[1:2])
    relayed = []
    summing = {}
    partial = []
    made = []
    placed, unplaced = [], []
    mix = small = x_grad = None
    deps = [p]
    for kind, what, units, *holding in PLAN:
        if kind == "experts":
            last = what == len(GROUPS) - 1
            shards = (own[what], beside[what], far[what], relayed[what])
            before = ([m[1] for m in made], [m[8] for m in made]) if last else None
            made.append(experts(GROUPS[what], rows, high, low, cot, p, shards, small, mix, before, deps))
            mix = made[what][0]
            small = made[0][9]
            deps = [made[what][8]]
        elif kind == "events":
            ours = [[made[g][k] for g in what] for k in (2, 3, 4, 5)]
            gating = [made[-1][1], gate_w] if what[-1] == len(GROUPS) - 1 else []
            x_grad, token = event_grads(rows, *ours, gating, x_grad, deps)
            deps = [token]
        elif kind == "place":
            v, token = place(*unplaced.pop(0), deps)
            placed.append(v)
            deps = [token]
        else:
            joint = units if "joint" in what else ()
            alone = () if joint else units
            held = holding[0] if holding else ()
            jobs = [summing[u].job() for u in (*alone, *held)]
            sent, fetched, through = [], [], []
            if "send" in what:
                sent = [made[-1][7]] + ([made[-1][8]] if len(made) == len(GROUPS) else [])
                jobs.append(copy_job(*sent))
            if "fetch" in what:
                group = len(relayed)
                fetched = [far[group], *own[group + 1 : group + 2]]
                jobs.append(copy_job(*fetched))
            if "mix" in what:
                through.append(mix)
            if "grad" in what:
                through.append(x_grad)
            if joint:
                job, rows_of = together([summing[u].job() for u in joint])
                jobs.append(job)
            outs, through, token = run(jobs, deps, through)
            deps = [token]
            if joint:
                Reduction.take_together([summing[u] for u in joint], outs.pop()[0], rows_of)
            for u, o in zip(alone, outs):
                summing[u].take(o)
            for u, o in zip(held, outs[len(alone) :]):
                summing[u].keep, summing[u].got = [Piece(o[0])], []
            if fetched:
                relayed.append(lax.ppermute(outs[-1][0], "tp", core))
                if len(fetched) > 1:
                    far.append(lax.ppermute(outs[-1][1], "tp", across))
                    beside.append(lax.ppermute(outs[-1][1], "tp", core))
            if sent:
                got = [lax.ppermute(v, "tp", core) for v in outs[len(alone) + len(held)]]
                partial.append(([made[-1][6], *sent[1:]], got))
                for u, (unit, way, spare) in enumerate(zip(UNITS, WAY, SPARE)):
                    if unit[-1] == len(partial) - 1:
                        both = [partial[g] for g in unit]
                        summing[u] = Reduction([v for b in both for v in b[0]], [v for b in both for v in b[1]], n_dp, way, spare)
            unplaced += [(v, lax.ppermute(v, "tp", core)) for v in through]
    mixtures, x_grad = placed
    summing = [summing[u] for u in range(len(UNITS))]
    while not all(u.finished or u.joining for u in summing):
        ours = [u for u in summing if not u.finished and not u.joining]
        outs, _, token = run([u.job() for u in ours], deps)
        deps = [token]
        for u, o in zip(ours, outs):
            u.take(o)
    joining = [(u.order[-1], [*u.keep, *u.got]) if u.joining else (None, u.keep) for u in summing]
    halves = [p.array for _, pieces in joining for p in pieces]
    per_expert = (E, SLICE)
    shapes = [(E, SLICE, D), per_expert, (E, SLICE, H), per_expert, per_expert, per_expert, (GATE_COLS, D)]
    scratch = [pltpu.VMEM((u.rows, LANES), F32) for u in summing if u.joining]
    job = Job(halves, shapes, functools.partial(finish_body, joining), scratch)
    (((in_grad, in_bias, out_grad, out_bias, gain, shift, gate),), _, _) = run([job], deps)
    return (
        mixtures,
        x_grad,
        jnp.swapaxes(in_grad, 1, 2),
        in_bias,
        jnp.swapaxes(out_grad, 1, 2),
        out_bias,
        gain,
        shift,
        jnp.swapaxes(gate, 0, 1),
    )


def solution(mesh):
    return jax.shard_map(
        per_device,
        mesh=mesh,
        in_specs=(
            P("dp", None),
            P(),
            P("dp", None),
            P(None, None, "tp"),
            P(None, "tp"),
            P(None, None, "tp"),
            P(None, "tp"),
            P(None, "tp"),
            P(None, "tp"),
            P(),
        ),
        out_specs=(
            P("dp", None),
            P("dp", None),
            P(None, None, "tp"),
            P(None, "tp"),
            P(None, None, "tp"),
            P(None, "tp"),
            P(None, "tp"),
            P(None, "tp"),
            P(),
        ),
        check_vma=False,
    )
```

```python
import functools

import jax
import jax.numpy as jnp
from jax import lax
from jax.experimental import pallas as pl
from jax.experimental.pallas import tpu as pltpu
from jax.sharding import PartitionSpec as P

D = 512
H = 256
O = 256
E = 6
GATE_COLS = 14
SLICE = 64
WIDE = D + H
LANES = 128
TOKEN = (8, LANES)
RB = 1024
ROW_BLOCK = 512
SUB = 256
LAG = 1
EPSILON = 1e-05
GROUPS = ((0, 1), (2, 3), (4,), (5,))
UNITS = ((0,), (1,), (2, 3))
WAY = ("single", "single", "pair")
SPARE = (0, 0, 0)
PLAN = (
    ("small", "fetch", ()),
    ("experts", 0, ()),
    ("small", "send", ()),
    ("events", (0,), ()),
    ("small", "fetch", (0,)),
    ("experts", 1, ()),
    ("small", "send fetch", (0,)),
    ("small", "", (1,)),
    ("experts", 2, ()),
    ("small", "send fetch", (0, 1)),
    ("experts", 3, ()),
    ("small", "send", (0, 1)),
    ("events", (2,), ()),
    ("small", "", (2,)),
    ("events", (1, 3), ()),
    ("small", "mix grad", (0, 1, 2)),
    ("small", "", (0, 1, 2)),
    ("place", None, ()),
    ("place", None, ()),
)
COLUMN = (
    {0: 0, 1: 1, 4: 2, 5: 3},
    {2: 4, 3: 5, 4: 6, 5: 7},
    {e: 8 + e for e in range(E)},
)
F32 = jnp.float32
BF16 = jnp.bfloat16
NN = (((1,), (0,)), ((), ()))
NT = (((1,), (1,)), ((), ()))
TN = (((0,), (0,)), ((), ()))


def split(v):
    high = v.astype(BF16)
    return high, (v - high.astype(F32)).astype(BF16)


def dot3(a, b, dims):
    def one(u, v):
        return lax.dot_general(u, v, dims, preferred_element_type=F32)

    return one(a[0], b[0]) + (one(a[0], b[1]) + one(a[1], b[0]))


def in_hbm(v):
    return pltpu.with_memory_space_constraint(v, pltpu.HBM)


LARGE = 60
EXPERT_MIB, EVENT_MIB, GATE_MIB, SMALL_MIB = 28, 16, 16, 8


def params(mib):
    return pltpu.CompilerParams(vmem_limit_bytes=mib << 20)


def gate_kernel(n_deps, counts, ev_ref, cot_ref, gw_ref, *refs):
    high_ref, low_ref, p_ref, cot_out, gw, held, sems = refs[n_deps:]
    rows = held.shape[0]
    steps = rows // ROW_BLOCK
    start = pl.multiple_of((lax.axis_index("tp") & 1) * rows, ROW_BLOCK)
    valid = counts[lax.axis_index("dp")]
    blocks = [slice(i * ROW_BLOCK, (i + 1) * ROW_BLOCK) for i in range(steps)]
    copies = [
        pltpu.make_async_copy(ev_ref.at[pl.ds(start + at.start, ROW_BLOCK), :], held.at[at, :], sems.at[i])
        for i, at in enumerate(blocks)
    ]
    copies.append(pltpu.make_async_copy(cot_ref.at[pl.ds(start, rows), :], cot_out, sems.at[steps]))
    for copy in copies:
        copy.start()
    gw[...] = jnp.zeros_like(gw)
    gw[:GATE_COLS, :] = gw_ref[...]
    gate = split(gw[...])
    lane = lax.broadcasted_iota(jnp.int32, (ROW_BLOCK, LANES), 1)
    sets = (lane < 4, (lane >= 4) & (lane < 8), (lane >= 8) & (lane < GATE_COLS))

    def per_set(values, empty, reduce):
        a, b, s = (reduce(jnp.where(m, values, empty), axis=1, keepdims=True) for m in sets)
        return jnp.where(sets[0], a, jnp.where(sets[1], b, s))

    for i, at in enumerate(blocks):
        copies[i].wait()
        events = split(held[at, :])
        high_ref[at, :], low_ref[at, :] = events
        logits = dot3(events, gate, NT)
        top = per_set(logits, -3e38, jnp.max)
        shares = jnp.where(lane < GATE_COLS, jnp.exp(logits - top), 0.0)
        p = shares / per_set(shares, 0.0, jnp.sum)
        row = start + at.start + lax.broadcasted_iota(jnp.int32, logits.shape, 0)
        p_ref[at, :] = jnp.where((row < valid) & (lane < GATE_COLS), p, 0.0)
    copies[-1].wait()


def gates(counts, events, cot, gate_w, rows, deps):
    vmem, hbm = pl.BlockSpec(memory_space=pltpu.VMEM), pl.BlockSpec(memory_space=pltpu.HBM)
    steps = rows // ROW_BLOCK
    return pl.pallas_call(
        functools.partial(gate_kernel, len(deps)),
        in_specs=[pl.BlockSpec(memory_space=pltpu.SMEM), hbm, hbm, vmem]
        + [pl.BlockSpec(memory_space=pl.ANY)] * len(deps),
        out_specs=[vmem] * 4,
        out_shape=[
            pltpu.VMEM((rows, D), BF16),
            pltpu.VMEM((rows, D), BF16),
            pltpu.VMEM((rows, LANES), F32),
            pltpu.VMEM((rows, 3 * O), F32),
        ],
        scratch_shapes=[
            pltpu.VMEM((LANES, D), F32),
            pltpu.VMEM((rows, D), F32),
            pltpu.SemaphoreType.DMA((steps + 1,)),
        ],
        compiler_params=params(GATE_MIB),
        cost_estimate=pl.CostEstimate(flops=6 * rows * D * LANES, bytes_accessed=rows * D * 8, transcendentals=0),
    )(counts, in_hbm(events), in_hbm(cot), in_hbm(gate_w), *deps)


def payload_kernel(groups, vectors, n_deps, w_in, w_out, *refs):
    given = refs[:4] if vectors else ()
    held = refs[-2]
    outs, sems = refs[len(given) + n_deps :][: len(groups)], refs[-1]
    copies = []
    for out, group in zip(outs, groups):
        experts_of, rows = pl.ds(group[0], len(group)), slice(0, SLICE)
        for part, lanes in ((w_in, slice(0, D)), (w_out, slice(D, WIDE))):
            copies.append(pltpu.make_async_copy(part.at[experts_of], out.at[:, rows, lanes], sems.at[len(copies)]))
    for k, v in enumerate(given):
        copies.append(pltpu.make_async_copy(v, held.at[k, slice(0, E), :], sems.at[len(copies)]))
    for copy in copies:
        copy.start()
    if vectors:
        for copy in copies[-len(given) :]:
            copy.wait()
        copies = copies[: -len(given)]
        rows = jnp.concatenate([held[k, :E, :] for k in range(4)], axis=0)
        outs[0][:, SLICE:, :] = jnp.zeros((len(groups[0]), 8, WIDE), F32)
        for j in range(4 * E // 8):
            outs[0][0, SLICE:, j * LANES : j * LANES + SLICE] = rows[8 * j : 8 * j + 8, :]
    for copy in copies:
        copy.wait()


def payload(groups, w_in, w_out, vectors, deps):
    vmem, hbm = pl.BlockSpec(memory_space=pltpu.VMEM), pl.BlockSpec(memory_space=pltpu.HBM)
    rows = SLICE + 8 if vectors else SLICE
    return pl.pallas_call(
        functools.partial(payload_kernel, groups, bool(vectors), len(deps)),
        in_specs=[hbm, hbm] + [hbm] * len(vectors) + [pl.BlockSpec(memory_space=pl.ANY)] * len(deps),
        out_specs=[vmem] * len(groups),
        out_shape=[pltpu.VMEM((len(group), rows, WIDE), F32) for group in groups],
        scratch_shapes=[pltpu.VMEM((4, 8, SLICE), F32), pltpu.SemaphoreType.DMA((2 * len(groups) + 4,))],
        compiler_params=params(SMALL_MIB),
        cost_estimate=pl.CostEstimate(flops=0, bytes_accessed=SLICE * WIDE * 16, transcendentals=0),
    )(in_hbm(w_in), in_hbm(w_out), *[in_hbm(v) for v in vectors], *deps)


def expert_kernel(group, first, last, n_deps, *refs):
    n = len(group)
    sub = SUB * n
    refs = list(refs)
    evh_ref, evl_ref, cot_ref, p_ref = refs[:4]
    shards = refs[4:8]
    del refs[:8]
    small = None if first else refs.pop(0)
    mix_in = None if first else refs.pop(0)
    if last:
        dp_before, sums_before = refs[: len(GROUPS) - 1], refs[len(GROUPS) - 1 : 2 * len(GROUPS) - 2]
        del refs[: 2 * len(GROUPS) - 2]
    del refs[:n_deps]
    mix_ref, dp_ref, dph_ref, dpl_ref, winh, winl, own_ref, part_ref, sums_ref = refs[:9]
    del refs[:9]
    if first:
        small = refs.pop(0)
    wouth, woutl, acc, sums = refs[:4]
    gate_acc = refs[4] if last else None
    step, steps = pl.program_id(0), pl.num_programs(0)
    odd = lax.axis_index("tp") & 1
    chip = lax.axis_index("tp") >> 1

    def tile(start, other):
        return pl.ds(pl.multiple_of(start + (chip ^ other) * LANES, LANES), LANES)

    @pl.when(step == 0)
    def _():
        acc[...] = jnp.zeros_like(acc)
        sums[...] = jnp.zeros_like(sums)
        if last:
            gate_acc[...] = jnp.zeros_like(gate_acc)
        for j in range(4 * E // 8 if first else 0):
            vectors = [shard[0, SLICE:, j * LANES : j * LANES + SLICE] for shard in shards]
            even_order, odd_order = (jnp.concatenate([vectors[k ^ c] for k in range(4)], axis=1) for c in range(2))
            small[8 * j : 8 * j + 8, :] = jnp.where(odd == 1, odd_order, even_order)
        if first:
            bias = small[E : 2 * E, :]
            small[E : 2 * E, :] = bias - jnp.mean(bias, axis=1, keepdims=True)
        own_rows = slice(0, SLICE)
        for i, e in enumerate(group):
            parts = [
                (shard[i, own_rows, :D], jnp.concatenate([shard[i, own_rows, tile(D, k)] for k in range(2)], axis=1))
                for shard in shards
            ]
            centre = sum(jnp.sum(out, axis=0, keepdims=True) for _, out in parts) / O
            for k, (into, out) in enumerate(parts):
                at = pl.multiple_of((odd ^ k) * SLICE, SLICE)
                winh[pl.ds(i * H + at, SLICE), :], winl[pl.ds(i * H + at, SLICE), :] = split(into)
                wouth[i, pl.ds(at, SLICE), :], woutl[i, pl.ds(at, SLICE), :] = split(out - centre)

    subs = RB // sub
    rows_of = [slice(s * sub, (s + 1) * sub) for s in range(subs)]
    lane = lax.broadcasted_iota(jnp.int32, (sub, LANES), 1)
    vector = lambda k, e: small[k * E + e : k * E + e + 1, :]
    state = [dict() for _ in range(subs)]

    def m1(s):
        events = evh_ref[rows_of[s], :], evl_ref[rows_of[s], :]
        state[s]["events"] = events
        pre = dot3(events, (winh[...], winl[...]), NT)
        state[s]["pre"] = [pre[:, i * H : (i + 1) * H] for i in range(n)]

    def v1(s):
        st = state[s]
        st["sigma"], st["hidden"], st["hidden_parts"] = [], [], []
        for i, e in enumerate(group):
            pre = st["pre"][i] + vector(0, e)
            sigma = jax.nn.sigmoid(pre)
            hidden = pre * sigma
            st["sigma"].append(sigma)
            st["hidden"].append(hidden)
            st["hidden_parts"].append(split(hidden))

    def m2(s):
        st = state[s]
        st["centred"] = [dot3(st["hidden_parts"][i], (wouth[i], woutl[i]), NT) for i in range(n)]

    def v2(s):
        st = state[s]
        p = p_ref[rows_of[s], :]
        dp = jnp.zeros_like(p)
        mixed = {}
        cots = [
            jnp.concatenate([cot_ref[rows_of[s], tile(t * O, 0)], cot_ref[rows_of[s], tile(t * O, 1)]], axis=1)
            for t in range(3)
        ]
        st["dnormed"] = []
        for i, e in enumerate(group):
            gain, shift = vector(2, e), vector(3, e)
            centred = st["centred"][i] + vector(1, e)
            rstd = lax.rsqrt(jnp.mean(centred * centred, axis=1, keepdims=True) + EPSILON)
            unit = centred * rstd
            y = unit * gain + shift
            dy = None
            for t in range(3):
                if e not in COLUMN[t]:
                    continue
                column = COLUMN[t][e]
                coef = p[:, column : column + 1]
                mixed[t] = coef * y + mixed[t] if t in mixed else coef * y
                dp = jnp.where(lane == column, jnp.sum(cots[t] * y, axis=1, keepdims=True), dp)
                dy = coef * cots[t] if dy is None else dy + coef * cots[t]
            dunit = dy * gain
            back_first = jnp.mean(dunit, axis=1, keepdims=True)
            back_second = jnp.mean(dunit * unit, axis=1, keepdims=True)
            dnormed = rstd * (dunit - back_first - unit * back_second)
            st["dnormed"].append(split(dnormed))
            dy_half = dy[:, :LANES]
            for k, v in enumerate((dnormed[:, :LANES], dy_half * unit[:, :LANES], dy_half)):
                sums[4 * i + k + 1 : 4 * i + k + 2, :] += jnp.sum(v, axis=0, keepdims=True)
        for t in range(3):
            for other in range(2):
                at = tile(t * O, other)
                if t in mixed:
                    value = mixed[t][:, other * LANES : (other + 1) * LANES]
                    mix_ref[rows_of[s], at] = value if first else mix_in[rows_of[s], at] + value
                elif first:
                    mix_ref[rows_of[s], at] = jnp.zeros((sub, LANES), F32)
                else:
                    mix_ref[rows_of[s], at] = mix_in[rows_of[s], at]
        if last:
            for other in dp_before:
                dp = dp + other[rows_of[s], :]
            weighted = p * dp
            sets = (lane < 4, (lane >= 4) & (lane < 8), (lane >= 8) & (lane < GATE_COLS))
            a, b, c = (jnp.sum(jnp.where(m, weighted, 0.0), axis=1, keepdims=True) for m in sets)
            dp = weighted - p * jnp.where(sets[0], a, jnp.where(sets[1], b, c))
            st["dlogits"] = dp
        dp_ref[rows_of[s], :] = dp

    def m3(s):
        st = state[s]
        st["dhidden"] = [dot3(st["dnormed"][i], (wouth[i], woutl[i]), NN) for i in range(n)]

    def v3(s):
        st = state[s]
        st["dpre"] = []
        for i, e in enumerate(group):
            sigma, hidden = st["sigma"][i], st["hidden"][i]
            dpre = st["dhidden"][i] * (sigma + hidden * (1.0 - sigma))
            parts = split(dpre)
            dph_ref[rows_of[s], i * H : (i + 1) * H], dpl_ref[rows_of[s], i * H : (i + 1) * H] = parts
            st["dpre"].append(tuple(v[:, :LANES] for v in parts))
            sums[4 * i : 4 * i + 1, :] += jnp.sum(dpre[:, :LANES], axis=0, keepdims=True)

    def m4(s):
        st = state[s]
        for i in range(n):
            halves = tuple(v[:, :LANES] for v in st["dnormed"][i])
            acc[i * LANES : (i + 1) * LANES, D:] += dot3(halves, st["hidden_parts"][i], TN)
        beside = [split(st["dlogits"][:, :16])] if last else []
        left = tuple(jnp.concatenate([h[k] for h in st["dpre"] + beside], axis=1) for k in range(2))
        both = dot3(left, st["events"], TN)
        acc[:, :D] += both[: n * LANES]
        if last:
            gate_acc[...] += both[n * LANES : n * LANES + 16]

    stages = (m1, v1, m2, v2, m3, v3, m4)
    for turn in range(len(stages) + LAG * (subs - 1)):
        for s in range(subs):
            if 0 <= turn - LAG * s < len(stages):
                stages[turn - LAG * s](s)

    @pl.when(step == steps - 1)
    def _():
        mine = pl.multiple_of(odd * SLICE, SLICE)
        other = pl.multiple_of(SLICE - mine, SLICE)
        for i in range(n):
            for t in range(WIDE // LANES):
                at = slice((t * n + i) * SLICE, (t * n + i + 1) * SLICE)
                lanes = slice(t * LANES, (t + 1) * LANES) if t < D // LANES else tile(D, t - D // LANES)
                own_ref[at, :] = acc[pl.ds(i * LANES + mine, SLICE), lanes]
                part_ref[at, :] = acc[pl.ds(i * LANES + other, SLICE), lanes]
        if last:
            for g, before in enumerate(sums_before):
                sums_ref[8 * g : 8 * g + 8, :] = before[...]
            g = len(GROUPS) - 1
            sums_ref[8 * g : 8 * g + 8, :] = sums[...]
            for t in range(D // LANES):
                sums_ref[8 * g + 8 + 16 * t : 8 * g + 24 + 16 * t, :] = gate_acc[:, t * LANES : (t + 1) * LANES]
        else:
            sums_ref[...] = sums[...]


def experts(group, rows, high, low, cot, p, shards, small, mix, before, deps):
    n = len(group)
    first, last = mix is None, before is not None
    steps = rows // RB
    block = lambda width: pl.BlockSpec((RB, width), lambda i: (i, 0))
    whole = lambda shape: pl.BlockSpec(shape, lambda i: (0,) * len(shape))
    in_specs = [
        block(D),
        block(D),
        block(3 * O),
        block(LANES),
        *[whole(shards[0].shape)] * 4,
    ]
    args = [high, low, cot, p, *shards]
    aliases = {}
    if not first:
        aliases = {len(args) + 1: 0}
        in_specs += [whole((4 * E, H)), block(3 * O)]
        args += [small, mix]
    if last:
        in_specs += [block(LANES)] * len(before[0]) + [whole((8, LANES))] * len(before[1])
        args += [*before[0], *before[1]]
    in_specs += [pl.BlockSpec(memory_space=pl.ANY)] * len(deps)
    args += deps
    payload = WIDE // LANES * n * SLICE
    sums_shape = (8 * len(GROUPS) + 16 * (D // LANES), LANES) if last else (8, LANES)
    scratch = [
        pltpu.VMEM((n, O, H), BF16),
        pltpu.VMEM((n, O, H), BF16),
        pltpu.VMEM((n * LANES, WIDE), F32),
        pltpu.VMEM((8, LANES), F32),
    ]
    if last:
        scratch.append(pltpu.VMEM((16, D), F32))
    return pl.pallas_call(
        functools.partial(expert_kernel, group, first, last, len(deps)),
        grid=(steps,),
        in_specs=in_specs,
        out_specs=[
                block(3 * O),
                block(LANES),
                block(n * H),
                block(n * H),
                whole((n * H, D)),
                whole((n * H, D)),
                whole((payload, LANES)),
                whole((payload, LANES)),
                whole(sums_shape),
        ]
        + [whole((4 * E, H))] * first,
        scratch_shapes=scratch,
        out_shape=[
            jax.ShapeDtypeStruct((rows, 3 * O), F32),
            jax.ShapeDtypeStruct((rows, LANES), F32),
            jax.ShapeDtypeStruct((rows, n * H), BF16),
            jax.ShapeDtypeStruct((rows, n * H), BF16),
            jax.ShapeDtypeStruct((n * H, D), BF16),
            jax.ShapeDtypeStruct((n * H, D), BF16),
            jax.ShapeDtypeStruct((payload, LANES), F32),
            jax.ShapeDtypeStruct((payload, LANES), F32),
            jax.ShapeDtypeStruct(sums_shape, F32),
        ]
        + [jax.ShapeDtypeStruct((4 * E, H), F32)] * first,
        input_output_aliases=aliases,
        compiler_params=params(EXPERT_MIB),
        cost_estimate=pl.CostEstimate(flops=n * rows * 6 * 720896, bytes_accessed=rows * 14000, transcendentals=0),
    )(*args)


def event_kernel(n, last, added, n_deps, *refs):
    highs, lows, winh, winl = (refs[k * n : (k + 1) * n] for k in range(4))
    refs = list(refs[4 * n :])
    total = 0.0
    if last:
        dlogits, gw_ref, gw = refs.pop(0), refs.pop(0), refs[-1]
        gw[...] = jnp.zeros_like(gw)
        gw[:GATE_COLS, :] = gw_ref[...]
        total = dot3(split(dlogits[...]), split(gw[...]), NN)
    before = refs.pop(0) if added else None
    out, token = refs[n_deps : n_deps + 2]
    for g in range(n):
        total = total + dot3((highs[g][...], lows[g][...]), (winh[g][...], winl[g][...]), NN)
    out[...] = total + before[...] if added else total
    token[...] = jnp.zeros_like(token)


def event_grads(rows, highs, lows, winh, winl, gating, before, deps):
    block = lambda width: pl.BlockSpec((ROW_BLOCK, width), lambda i: (i, 0))
    whole = lambda shape: pl.BlockSpec(shape, lambda i: (0, 0))
    args = [*highs, *lows, *winh, *winl]
    in_specs = [block(v.shape[1]) for v in (*highs, *lows)] + [whole(v.shape) for v in (*winh, *winl)]
    aliases = {}
    if gating:
        args += gating
        in_specs += [block(LANES), whole((GATE_COLS, D))]
    if before is not None:
        aliases = {len(args): 0}
        args.append(before)
        in_specs.append(block(D))
    return pl.pallas_call(
        functools.partial(event_kernel, len(highs), bool(gating), before is not None, len(deps)),
        grid=(rows // ROW_BLOCK,),
        in_specs=in_specs + [pl.BlockSpec(memory_space=pl.ANY)] * len(deps),
        out_specs=[block(D), whole(TOKEN)],
        scratch_shapes=[pltpu.VMEM((LANES, D), F32)],
        out_shape=[pltpu.VMEM((rows, D), F32), jax.ShapeDtypeStruct(TOKEN, F32)],
        input_output_aliases=aliases,
        compiler_params=params(EVENT_MIB),
        cost_estimate=pl.CostEstimate(
            flops=6 * rows * D * sum(v.shape[1] for v in highs), bytes_accessed=rows * 4000, transcendentals=0
        ),
    )(*args, *deps)


def place_kernel(own, other, *refs):
    out, token, sems = refs[-3:]
    rows = own.shape[0]
    side = lax.axis_index("tp") & 1
    copies = [
        pltpu.make_async_copy(v, out.at[pl.ds(pl.multiple_of(at * rows, ROW_BLOCK), rows), :], sems.at[k])
        for k, (v, at) in enumerate(((own, side), (other, 1 - side)))
    ]
    for copy in copies:
        copy.start()
    token[...] = jnp.zeros_like(token)
    for copy in copies:
        copy.wait()


def place(own, other, deps):
    rows, width = own.shape
    anywhere = pl.BlockSpec(memory_space=pl.ANY)
    return pl.pallas_call(
        place_kernel,
        in_specs=[anywhere] * (2 + len(deps)),
        out_specs=[pl.BlockSpec(memory_space=pltpu.HBM), pl.BlockSpec(memory_space=pltpu.VMEM)],
        scratch_shapes=[pltpu.SemaphoreType.DMA((2,))],
        out_shape=[jax.ShapeDtypeStruct((2 * rows, width), F32), jax.ShapeDtypeStruct(TOKEN, F32)],
        compiler_params=params(SMALL_MIB),
        cost_estimate=pl.CostEstimate(flops=0, bytes_accessed=rows * width * 16, transcendentals=0),
    )(own, other, *deps)


class Job:
    def __init__(self, args, shapes, body, scratch=()):
        self.args, self.body, self.scratch = args, body, list(scratch)
        self.shapes = [jax.ShapeDtypeStruct(shape, F32) for shape in shapes]


def copy_job(*arrays):
    def body(ins, outs, scratch):
        for a, b in zip(ins, outs):
            b[...] = a[...]

    return Job(arrays, [a.shape for a in arrays], body)


def run(jobs, deps=(), through=()):
    args = [a for job in jobs for a in job.args]
    shapes = [o for job in jobs for o in job.shapes]
    scratch = [v for job in jobs for v in job.scratch]

    def kernel(*refs):
        ins, refs = refs[: len(args)], refs[len(args) + len(through) + len(deps) :]
        outs, token, kept = refs[: len(shapes)], refs[len(shapes) + len(through)], refs[len(shapes) + len(through) + 1 :]
        token[...] = jnp.zeros_like(token)
        i = o = k = 0
        for job in jobs:
            ni, no, nk = len(job.args), len(job.shapes), len(job.scratch)
            job.body(ins[i : i + ni], outs[o : o + no], kept[k : k + nk])
            i, o, k = i + ni, o + no, k + nk

    vmem, anywhere = pl.BlockSpec(memory_space=pltpu.VMEM), pl.BlockSpec(memory_space=pl.ANY)
    flat = pl.pallas_call(
        kernel,
        in_specs=[vmem] * len(args) + [anywhere] * (len(through) + len(deps)),
        out_specs=[vmem] * len(shapes) + [anywhere] * len(through) + [vmem],
        out_shape=shapes
        + [jax.ShapeDtypeStruct(v.shape, v.dtype) for v in through]
        + [jax.ShapeDtypeStruct(TOKEN, F32)],
        scratch_shapes=scratch,
        input_output_aliases={len(args) + k: len(shapes) + k for k in range(len(through))},
        compiler_params=params(SMALL_MIB),
        cost_estimate=pl.CostEstimate(flops=0, bytes_accessed=sum(8 * a.size for a in args), transcendentals=0),
    )(*args, *through, *deps)
    result = []
    for job in jobs:
        result.append(list(flat[: len(job.shapes)]))
        flat = flat[len(job.shapes) :]
    return result, list(flat[:-1]), flat[-1]


def part_of(ref, index, rows):
    return ref.at[pl.ds(pl.multiple_of(index * rows, 8), rows), :]


class Piece:
    def __init__(self, array, at=0, rows=None):
        self.array, self.at = array, at
        self.rows = array.shape[0] if rows is None else rows

    def of(self, ref):
        return ref.at[pl.ds(self.at, self.rows), :]


def bit_groups(bits, width):
    groups, start = [], 0
    while bits - start > width:
        groups.append((start, width))
        start += width
    return groups, (start, bits - start)


class Reduction:
    def __init__(self, own, got, n_dp, kind, spare):
        self.spare = spare
        self.keep, self.got = [Piece(v) for v in own], [Piece(v) for v in got]
        pairs, last = bit_groups(n_dp.bit_length() - 1, 2)
        singles, lone = bit_groups(n_dp.bit_length() - 1, 1)
        if kind == "single":
            scatter, last, gather = singles, lone, singles
        elif kind == "pair":
            scatter, gather = pairs, pairs
        else:
            scatter, gather = [(b + k, 1) for b, n in pairs for k in reversed(range(n))], pairs
        self.order = [*scatter, last, *reversed(gather)]
        self.scattered = len(scatter)
        unit = 8 << sum(n for _, n in scatter)
        self.rows = -(-sum(p.rows for p in self.keep) // unit) * unit
        self.n_dp = n_dp
        self.stage = 0

    @property
    def finished(self):
        return self.stage > len(self.order)

    @property
    def joining(self):
        return self.stage == len(self.order)

    def job(self):
        stage = self.stage
        gather, scatter = stage > self.scattered + 1, stage < self.scattered
        n = len(self.keep)
        pieces = [*self.keep, *self.got]
        came = self.order[stage - 1]
        goes = self.order[stage] if stage < len(self.order) else None
        rows = self.rows if stage == 0 else self.keep[0].rows * ((1 << came[1]) if gather else 1)
        parts = 1 << goes[1] if scatter else 1

        def body(ins, outs, scratch):
            ins = [p.of(ref) for p, ref in zip(pieces, ins)]
            to = scratch[0] if scatter else outs[0]
            if gather:
                join(ins, to, came)
                return
            at = 0
            for k, piece in enumerate(pieces[:n]):
                total = ins[k][...]
                for v in ins[k + n :: n]:
                    total = total + v[...]
                to[at : at + piece.rows, :] = total
                at += piece.rows
            if at < to.shape[0]:
                to[at:, :] = jnp.zeros((to.shape[0] - at, LANES), F32)
            if scatter:
                side = side_of(goes)
                for m in range(parts):
                    outs[m][...] = part_of(to, side ^ m, rows // parts)[...]

        arrays = [p.array for p in pieces]
        if scatter:
            return Job(arrays, [(rows // parts, LANES)] * parts, body, [pltpu.VMEM((rows, LANES), F32)])
        self.used = rows
        return Job(arrays, [(rows + (self.spare if stage == self.scattered else 0), LANES)], body)

    def take(self, outs):
        self.stage += 1
        scatters = self.stage <= self.scattered
        rows = None if scatters else self.used
        self.keep = [Piece(outs[0], 0, rows)]
        if self.stage <= len(self.order):
            sent = outs[1:] if scatters else None
            self.got = [Piece(v, 0, rows) for v in exchange(outs[0], sent, self.order[self.stage - 1], self.n_dp)]

    @staticmethod
    def take_together(units, out, rows):
        at = 0
        came = exchange(out, None, units[0].order[units[0].stage], units[0].n_dp)
        for unit, n in zip(units, rows):
            unit.stage += 1
            unit.keep, unit.got = [Piece(out, at, n)], [Piece(v, at, n) for v in came]
            at += n


def exchange(whole, parts, bits, n_dp):
    start, n = bits
    return [
        lax.ppermute(whole if parts is None else parts[m - 1], "dp", [(i, i ^ (m << start)) for i in range(n_dp)])
        for m in range(1, 1 << n)
    ]


def side_of(bits):
    return (lax.axis_index("dp") >> bits[0]) & ((1 << bits[1]) - 1)


def join(ins, to, bits):
    for m, v in enumerate(ins):
        part_of(to, side_of(bits) ^ m, v.shape[0])[...] = v[...]


def together(jobs):
    rows = [job.shapes[0].shape[0] for job in jobs]

    def body(ins, outs, scratch):
        at = i = 0
        for job, n in zip(jobs, rows):
            job.body(ins[i : i + len(job.args)], [outs[0].at[pl.ds(at, n), :]], [])
            i, at = i + len(job.args), at + n

    return Job([a for job in jobs for a in job.args], [(sum(rows), LANES)], body), rows


def finish_body(joining, ins, outs, both):
    in_grad, in_bias, out_grad, out_bias, gain, shift, gate = outs
    odd = (lax.axis_index("tp") & 1) == 1
    ins, both, summed = list(ins), list(both), []
    for bits, pieces in joining:
        parts = [piece.of(ins.pop(0)) for piece in pieces]
        if bits:
            join(parts, both[0], bits)
            summed.append(both.pop(0))
        else:
            summed.append(parts[0])
    for u, unit in enumerate(UNITS):
        at = 0
        for g in unit:
            group = GROUPS[g]
            for t in range(WIDE // LANES):
                for e in group:
                    tile = summed[u][at : at + SLICE, :]
                    at += SLICE
                    if t < D // LANES:
                        in_grad[e, :, t * LANES : (t + 1) * LANES] = tile
                    else:
                        out_grad[e, :, t * LANES - D : (t + 1) * LANES - D] = tile
    sums = summed[-1][at : at + 8 * len(GROUPS), :]
    sums = jnp.where(odd, sums[:, SLICE:], sums[:, :SLICE])
    start = at + 8 * len(GROUPS)
    for g, group in enumerate(GROUPS):
        for i, e in enumerate(group):
            for k, ref in enumerate((in_bias, out_bias, gain, shift)):
                ref[e : e + 1, :] = sums[8 * g + 4 * i + k : 8 * g + 4 * i + k + 1, :]
    for t in range(D // LANES):
        gate[:, t * LANES : (t + 1) * LANES] = summed[-1][start + 16 * t : start + 16 * t + GATE_COLS, :]


def per_device(
    events,
    valid_counts,
    mix_cotangent,
    expert_in,
    expert_in_bias,
    expert_out,
    expert_out_bias,
    norm_gain,
    norm_shift,
    gate_weight,
):
    n_dp = lax.axis_size("dp")
    rows = events.shape[0] // 2
    w_in = jnp.swapaxes(expert_in, 1, 2)
    w_out = jnp.swapaxes(expert_out, 1, 2)
    gate_w = jnp.swapaxes(gate_weight, 0, 1)
    core = [(i, i ^ 1) for i in range(4)]
    across = [(i, i ^ 2) for i in range(4)]
    vectors = [expert_in_bias, expert_out_bias, norm_gain, norm_shift]
    own = list(payload(GROUPS[:1], w_in, w_out, vectors, []))
    far = [lax.ppermute(own[0], "tp", across)]
    beside = [lax.ppermute(own[0], "tp", core)]
    own += payload(GROUPS[1:], w_in, w_out, [], own)
    high, low, p, cot = gates(valid_counts, events, mix_cotangent, gate_w, rows, own[1:2])
    relayed = []
    summing = {}
    partial = []
    made = []
    placed, unplaced = [], []
    mix = small = x_grad = None
    deps = [p]
    for kind, what, units, *holding in PLAN:
        if kind == "experts":
            last = what == len(GROUPS) - 1
            shards = (own[what], beside[what], far[what], relayed[what])
            before = ([m[1] for m in made], [m[8] for m in made]) if last else None
            made.append(experts(GROUPS[what], rows, high, low, cot, p, shards, small, mix, before, deps))
            mix = made[what][0]
            small = made[0][9]
            deps = [made[what][8]]
        elif kind == "events":
            ours = [[made[g][k] for g in what] for k in (2, 3, 4, 5)]
            gating = [made[-1][1], gate_w] if what[-1] == len(GROUPS) - 1 else []
            x_grad, token = event_grads(rows, *ours, gating, x_grad, deps)
            deps = [token]
        elif kind == "place":
            v, token = place(*unplaced.pop(0), deps)
            placed.append(v)
            deps = [token]
        else:
            joint = units if "joint" in what else ()
            alone = () if joint else units
            held = holding[0] if holding else ()
            jobs = [summing[u].job() for u in (*alone, *held)]
            sent, fetched, through = [], [], []
            if "send" in what:
                sent = [made[-1][7]] + ([made[-1][8]] if len(made) == len(GROUPS) else [])
                jobs.append(copy_job(*sent))
            if "fetch" in what:
                group = len(relayed)
                fetched = [far[group], *own[group + 1 : group + 2]]
                jobs.append(copy_job(*fetched))
            if "mix" in what:
                through.append(mix)
            if "grad" in what:
                through.append(x_grad)
            if joint:
                job, rows_of = together([summing[u].job() for u in joint])
                jobs.append(job)
            outs, through, token = run(jobs, deps, through)
            deps = [token]
            if joint:
                Reduction.take_together([summing[u] for u in joint], outs.pop()[0], rows_of)
            for u, o in zip(alone, outs):
                summing[u].take(o)
            for u, o in zip(held, outs[len(alone) :]):
                summing[u].keep, summing[u].got = [Piece(o[0])], []
            if fetched:
                relayed.append(lax.ppermute(outs[-1][0], "tp", core))
                if len(fetched) > 1:
                    far.append(lax.ppermute(outs[-1][1], "tp", across))
                    beside.append(lax.ppermute(outs[-1][1], "tp", core))
            if sent:
                got = [lax.ppermute(v, "tp", core) for v in outs[len(alone) + len(held)]]
                partial.append(([made[-1][6], *sent[1:]], got))
                for u, (unit, way, spare) in enumerate(zip(UNITS, WAY, SPARE)):
                    if unit[-1] == len(partial) - 1:
                        both = [partial[g] for g in unit]
                        summing[u] = Reduction([v for b in both for v in b[0]], [v for b in both for v in b[1]], n_dp, way, spare)
            unplaced += [(v, lax.ppermute(v, "tp", core)) for v in through]
    mixtures, x_grad = placed
    summing = [summing[u] for u in range(len(UNITS))]
    while not all(u.finished or u.joining for u in summing):
        ours = [u for u in summing if not u.finished and not u.joining]
        outs, _, token = run([u.job() for u in ours], deps)
        deps = [token]
        for u, o in zip(ours, outs):
            u.take(o)
    joining = [(u.order[-1], [*u.keep, *u.got]) if u.joining else (None, u.keep) for u in summing]
    halves = [p.array for _, pieces in joining for p in pieces]
    per_expert = (E, SLICE)
    shapes = [(E, SLICE, D), per_expert, (E, SLICE, H), per_expert, per_expert, per_expert, (GATE_COLS, D)]
    scratch = [pltpu.VMEM((u.rows, LANES), F32) for u in summing if u.joining]
    job = Job(halves, shapes, functools.partial(finish_body, joining), scratch)
    (((in_grad, in_bias, out_grad, out_bias, gain, shift, gate),), _, _) = run([job], deps)
    return (
        mixtures,
        x_grad,
        jnp.swapaxes(in_grad, 1, 2),
        in_bias,
        jnp.swapaxes(out_grad, 1, 2),
        out_bias,
        gain,
        shift,
        jnp.swapaxes(gate, 0, 1),
    )


def solution(mesh):
    return jax.shard_map(
        per_device,
        mesh=mesh,
        in_specs=(
            P("dp", None),
            P(),
            P("dp", None),
            P(None, None, "tp"),
            P(None, "tp"),
            P(None, None, "tp"),
            P(None, "tp"),
            P(None, "tp"),
            P(None, "tp"),
            P(),
        ),
        out_specs=(
            P("dp", None),
            P("dp", None),
            P(None, None, "tp"),
            P(None, "tp"),
            P(None, None, "tp"),
            P(None, "tp"),
            P(None, "tp"),
            P(None, "tp"),
            P(),
        ),
        check_vma=False,
    )
```

```python
import functools

import jax
import jax.numpy as jnp
from jax import lax
from jax.experimental import pallas as pl
from jax.experimental.pallas import tpu as pltpu
from jax.sharding import PartitionSpec as P

D = 512
H = 256
O = 256
E = 6
GATE_COLS = 14
SLICE = 64
WIDE = D + H
LANES = 128
TOKEN = (8, LANES)
RB = 1024
ROW_BLOCK = 512
SUB = 256
LAG = 1
EPSILON = 1e-05
GROUPS = ((0, 1), (2, 3), (4,), (5,))
UNITS = ((0,), (1,), (2, 3))
WAY = ("single", "single", "pair")
SPARE = (0, 0, 0)
PLAN = (
    ("small", "fetch", ()),
    ("experts", 0, ()),
    ("small", "send", ()),
    ("events", (0,), ()),
    ("small", "fetch", (0,)),
    ("experts", 1, ()),
    ("small", "send fetch", (0,)),
    ("small", "", (1,)),
    ("experts", 2, ()),
    ("small", "send fetch", (0, 1)),
    ("experts", 3, ()),
    ("small", "send", (0, 1)),
    ("events", (2,), ()),
    ("small", "", (2,)),
    ("events", (1, 3), ()),
    ("small", "mix grad", (0, 1, 2)),
    ("small", "", (0, 1, 2)),
    ("place", None, ()),
    ("place", None, ()),
)
COLUMN = (
    {0: 0, 1: 1, 4: 2, 5: 3},
    {2: 4, 3: 5, 4: 6, 5: 7},
    {e: 8 + e for e in range(E)},
)
F32 = jnp.float32
BF16 = jnp.bfloat16
NN = (((1,), (0,)), ((), ()))
NT = (((1,), (1,)), ((), ()))
TN = (((0,), (0,)), ((), ()))


def split(v):
    high = v.astype(BF16)
    return high, (v - high.astype(F32)).astype(BF16)


def dot3(a, b, dims):
    def one(u, v):
        return lax.dot_general(u, v, dims, preferred_element_type=F32)

    return one(a[0], b[0]) + (one(a[0], b[1]) + one(a[1], b[0]))


def in_hbm(v):
    return pltpu.with_memory_space_constraint(v, pltpu.HBM)


LARGE = 60
EXPERT_MIB, EVENT_MIB, GATE_MIB, SMALL_MIB = 28, 16, 16, 8


def params(mib):
    return pltpu.CompilerParams(vmem_limit_bytes=mib << 20)


def gate_kernel(n_deps, counts, ev_ref, cot_ref, gw_ref, *refs):
    high_ref, low_ref, p_ref, cot_out, gw, held, sems = refs[n_deps:]
    rows = held.shape[0]
    steps = rows // ROW_BLOCK
    start = pl.multiple_of((lax.axis_index("tp") & 1) * rows, ROW_BLOCK)
    valid = counts[lax.axis_index("dp")]
    blocks = [slice(i * ROW_BLOCK, (i + 1) * ROW_BLOCK) for i in range(steps)]
    copies = [
        pltpu.make_async_copy(ev_ref.at[pl.ds(start + at.start, ROW_BLOCK), :], held.at[at, :], sems.at[i])
        for i, at in enumerate(blocks)
    ]
    copies.append(pltpu.make_async_copy(cot_ref.at[pl.ds(start, rows), :], cot_out, sems.at[steps]))
    for copy in copies:
        copy.start()
    gw[...] = jnp.zeros_like(gw)
    gw[:GATE_COLS, :] = gw_ref[...]
    gate = split(gw[...])
    lane = lax.broadcasted_iota(jnp.int32, (ROW_BLOCK, LANES), 1)
    sets = (lane < 4, (lane >= 4) & (lane < 8), (lane >= 8) & (lane < GATE_COLS))

    def per_set(values, empty, reduce):
        a, b, s = (reduce(jnp.where(m, values, empty), axis=1, keepdims=True) for m in sets)
        return jnp.where(sets[0], a, jnp.where(sets[1], b, s))

    for i, at in enumerate(blocks):
        copies[i].wait()
        events = split(held[at, :])
        high_ref[at, :], low_ref[at, :] = events
        logits = dot3(events, gate, NT)
        top = per_set(logits, -3e38, jnp.max)
        shares = jnp.where(lane < GATE_COLS, jnp.exp(logits - top), 0.0)
        p = shares / per_set(shares, 0.0, jnp.sum)
        row = start + at.start + lax.broadcasted_iota(jnp.int32, logits.shape, 0)
        p_ref[at, :] = jnp.where((row < valid) & (lane < GATE_COLS), p, 0.0)
    copies[-1].wait()


def gates(counts, events, cot, gate_w, rows, deps):
    vmem, hbm = pl.BlockSpec(memory_space=pltpu.VMEM), pl.BlockSpec(memory_space=pltpu.HBM)
    steps = rows // ROW_BLOCK
    return pl.pallas_call(
        functools.partial(gate_kernel, len(deps)),
        in_specs=[pl.BlockSpec(memory_space=pltpu.SMEM), hbm, hbm, vmem]
        + [pl.BlockSpec(memory_space=pl.ANY)] * len(deps),
        out_specs=[vmem] * 4,
        out_shape=[
            pltpu.VMEM((rows, D), BF16),
            pltpu.VMEM((rows, D), BF16),
            pltpu.VMEM((rows, LANES), F32),
            pltpu.VMEM((rows, 3 * O), F32),
        ],
        scratch_shapes=[
            pltpu.VMEM((LANES, D), F32),
            pltpu.VMEM((rows, D), F32),
            pltpu.SemaphoreType.DMA((steps + 1,)),
        ],
        compiler_params=params(GATE_MIB),
        cost_estimate=pl.CostEstimate(flops=6 * rows * D * LANES, bytes_accessed=rows * D * 8, transcendentals=0),
    )(counts, in_hbm(events), in_hbm(cot), in_hbm(gate_w), *deps)


def payload_kernel(groups, vectors, n_deps, w_in, w_out, *refs):
    given = refs[:4] if vectors else ()
    held = refs[-2]
    outs, sems = refs[len(given) + n_deps :][: len(groups)], refs[-1]
    copies = []
    for out, group in zip(outs, groups):
        for part, lanes in ((w_in, slice(0, D)), (w_out, slice(D, WIDE))):
            for i, e in enumerate(group):
                to = out.at[pl.ds(i * SLICE, SLICE), lanes] if vectors else out.at[i, :, lanes]
                copies.append(pltpu.make_async_copy(part.at[e], to, sems.at[len(copies)]))
    for k, v in enumerate(given):
        copies.append(pltpu.make_async_copy(v, held.at[k, slice(0, E), :], sems.at[len(copies)]))
    for copy in copies:
        copy.start()
    if vectors:
        for copy in copies[-len(given) :]:
            copy.wait()
        copies = copies[: -len(given)]
        rows = jnp.concatenate([held[k, :E, :] for k in range(4)], axis=0)
        end = len(groups[0]) * SLICE
        outs[0][end:, :] = jnp.zeros((8, WIDE), F32)
        for j in range(4 * E // 8):
            outs[0][end:, j * LANES : j * LANES + SLICE] = rows[8 * j : 8 * j + 8, :]
    for copy in copies:
        copy.wait()


def payload(groups, w_in, w_out, vectors, deps):
    vmem, hbm = pl.BlockSpec(memory_space=pltpu.VMEM), pl.BlockSpec(memory_space=pltpu.HBM)
    shapes = [(len(group) * SLICE + 8, WIDE) if vectors else (len(group), SLICE, WIDE) for group in groups]
    return pl.pallas_call(
        functools.partial(payload_kernel, groups, bool(vectors), len(deps)),
        in_specs=[hbm, hbm] + [hbm] * len(vectors) + [pl.BlockSpec(memory_space=pl.ANY)] * len(deps),
        out_specs=[vmem] * len(groups),
        out_shape=[pltpu.VMEM(shape, F32) for shape in shapes],
        scratch_shapes=[pltpu.VMEM((4, 8, SLICE), F32), pltpu.SemaphoreType.DMA((2 * E + 4,))],
        compiler_params=params(SMALL_MIB),
        cost_estimate=pl.CostEstimate(flops=0, bytes_accessed=SLICE * WIDE * 16, transcendentals=0),
    )(in_hbm(w_in), in_hbm(w_out), *[in_hbm(v) for v in vectors], *deps)


def expert_kernel(group, first, last, n_deps, *refs):
    n = len(group)
    sub = SUB * n
    refs = list(refs)
    evh_ref, evl_ref, cot_ref, p_ref = refs[:4]
    shards = refs[4:8]
    del refs[:8]
    small = None if first else refs.pop(0)
    mix_in = None if first else refs.pop(0)
    if last:
        dp_before, sums_before = refs[: len(GROUPS) - 1], refs[len(GROUPS) - 1 : 2 * len(GROUPS) - 2]
        del refs[: 2 * len(GROUPS) - 2]
    del refs[:n_deps]
    mix_ref, dp_ref, dph_ref, dpl_ref, winh, winl, own_ref, part_ref, sums_ref = refs[:9]
    del refs[:9]
    if first:
        small = refs.pop(0)
    wouth, woutl, acc, sums = refs[:4]
    gate_acc = refs[4] if last else None
    step, steps = pl.program_id(0), pl.num_programs(0)
    odd = lax.axis_index("tp") & 1
    chip = lax.axis_index("tp") >> 1

    def tile(start, other):
        return pl.ds(pl.multiple_of(start + (chip ^ other) * LANES, LANES), LANES)

    @pl.when(step == 0)
    def _():
        acc[...] = jnp.zeros_like(acc)
        sums[...] = jnp.zeros_like(sums)
        if last:
            gate_acc[...] = jnp.zeros_like(gate_acc)
        for j in range(4 * E // 8 if first else 0):
            vectors = [shard[n * SLICE :, j * LANES : j * LANES + SLICE] for shard in shards]
            even_order, odd_order = (jnp.concatenate([vectors[k ^ c] for k in range(4)], axis=1) for c in range(2))
            small[8 * j : 8 * j + 8, :] = jnp.where(odd == 1, odd_order, even_order)
        if first:
            bias = small[E : 2 * E, :]
            small[E : 2 * E, :] = bias - jnp.mean(bias, axis=1, keepdims=True)
        for i, e in enumerate(group):
            at = (slice(i * SLICE, (i + 1) * SLICE),) if first else (i, slice(0, SLICE))
            parts = [
                (shard[*at, slice(0, D)], jnp.concatenate([shard[*at, tile(D, k)] for k in range(2)], axis=1))
                for shard in shards
            ]
            centre = sum(jnp.sum(out, axis=0, keepdims=True) for _, out in parts) / O
            for k, (into, out) in enumerate(parts):
                at = pl.multiple_of((odd ^ k) * SLICE, SLICE)
                winh[pl.ds(i * H + at, SLICE), :], winl[pl.ds(i * H + at, SLICE), :] = split(into)
                wouth[i, pl.ds(at, SLICE), :], woutl[i, pl.ds(at, SLICE), :] = split(out - centre)

    subs = RB // sub
    rows_of = [slice(s * sub, (s + 1) * sub) for s in range(subs)]
    lane = lax.broadcasted_iota(jnp.int32, (sub, LANES), 1)
    vector = lambda k, e: small[k * E + e : k * E + e + 1, :]
    state = [dict() for _ in range(subs)]

    def m1(s):
        events = evh_ref[rows_of[s], :], evl_ref[rows_of[s], :]
        state[s]["events"] = events
        pre = dot3(events, (winh[...], winl[...]), NT)
        state[s]["pre"] = [pre[:, i * H : (i + 1) * H] for i in range(n)]

    def v1(s):
        st = state[s]
        st["sigma"], st["hidden"], st["hidden_parts"] = [], [], []
        for i, e in enumerate(group):
            pre = st["pre"][i] + vector(0, e)
            sigma = jax.nn.sigmoid(pre)
            hidden = pre * sigma
            st["sigma"].append(sigma)
            st["hidden"].append(hidden)
            st["hidden_parts"].append(split(hidden))

    def m2(s):
        st = state[s]
        st["centred"] = [dot3(st["hidden_parts"][i], (wouth[i], woutl[i]), NT) for i in range(n)]

    def v2(s):
        st = state[s]
        p = p_ref[rows_of[s], :]
        dp = jnp.zeros_like(p)
        mixed = {}
        cots = [
            jnp.concatenate([cot_ref[rows_of[s], tile(t * O, 0)], cot_ref[rows_of[s], tile(t * O, 1)]], axis=1)
            for t in range(3)
        ]
        st["dnormed"] = []
        for i, e in enumerate(group):
            gain, shift = vector(2, e), vector(3, e)
            centred = st["centred"][i] + vector(1, e)
            rstd = lax.rsqrt(jnp.mean(centred * centred, axis=1, keepdims=True) + EPSILON)
            unit = centred * rstd
            y = unit * gain + shift
            dy = None
            for t in range(3):
                if e not in COLUMN[t]:
                    continue
                column = COLUMN[t][e]
                coef = p[:, column : column + 1]
                mixed[t] = coef * y + mixed[t] if t in mixed else coef * y
                dp = jnp.where(lane == column, jnp.sum(cots[t] * y, axis=1, keepdims=True), dp)
                dy = coef * cots[t] if dy is None else dy + coef * cots[t]
            dunit = dy * gain
            back_first = jnp.mean(dunit, axis=1, keepdims=True)
            back_second = jnp.mean(dunit * unit, axis=1, keepdims=True)
            dnormed = rstd * (dunit - back_first - unit * back_second)
            st["dnormed"].append(split(dnormed))
            dy_half = dy[:, :LANES]
            for k, v in enumerate((dnormed[:, :LANES], dy_half * unit[:, :LANES], dy_half)):
                sums[4 * i + k + 1 : 4 * i + k + 2, :] += jnp.sum(v, axis=0, keepdims=True)
        for t in range(3):
            for other in range(2):
                at = tile(t * O, other)
                if t in mixed:
                    value = mixed[t][:, other * LANES : (other + 1) * LANES]
                    mix_ref[rows_of[s], at] = value if first else mix_in[rows_of[s], at] + value
                elif first:
                    mix_ref[rows_of[s], at] = jnp.zeros((sub, LANES), F32)
                else:
                    mix_ref[rows_of[s], at] = mix_in[rows_of[s], at]
        if last:
            for other in dp_before:
                dp = dp + other[rows_of[s], :]
            weighted = p * dp
            sets = (lane < 4, (lane >= 4) & (lane < 8), (lane >= 8) & (lane < GATE_COLS))
            a, b, c = (jnp.sum(jnp.where(m, weighted, 0.0), axis=1, keepdims=True) for m in sets)
            dp = weighted - p * jnp.where(sets[0], a, jnp.where(sets[1], b, c))
            st["dlogits"] = dp
        dp_ref[rows_of[s], :] = dp

    def m3(s):
        st = state[s]
        st["dhidden"] = [dot3(st["dnormed"][i], (wouth[i], woutl[i]), NN) for i in range(n)]

    def v3(s):
        st = state[s]
        st["dpre"] = []
        for i, e in enumerate(group):
            sigma, hidden = st["sigma"][i], st["hidden"][i]
            dpre = st["dhidden"][i] * (sigma + hidden * (1.0 - sigma))
            parts = split(dpre)
            dph_ref[rows_of[s], i * H : (i + 1) * H], dpl_ref[rows_of[s], i * H : (i + 1) * H] = parts
            st["dpre"].append(tuple(v[:, :LANES] for v in parts))
            sums[4 * i : 4 * i + 1, :] += jnp.sum(dpre[:, :LANES], axis=0, keepdims=True)

    def m4(s):
        st = state[s]
        for i in range(n):
            halves = tuple(v[:, :LANES] for v in st["dnormed"][i])
            acc[i * LANES : (i + 1) * LANES, D:] += dot3(halves, st["hidden_parts"][i], TN)
        beside = [split(st["dlogits"][:, :16])] if last else []
        left = tuple(jnp.concatenate([h[k] for h in st["dpre"] + beside], axis=1) for k in range(2))
        both = dot3(left, st["events"], TN)
        acc[:, :D] += both[: n * LANES]
        if last:
            gate_acc[...] += both[n * LANES : n * LANES + 16]

    stages = (m1, v1, m2, v2, m3, v3, m4)
    for turn in range(len(stages) + LAG * (subs - 1)):
        for s in range(subs):
            if 0 <= turn - LAG * s < len(stages):
                stages[turn - LAG * s](s)

    @pl.when(step == steps - 1)
    def _():
        mine = pl.multiple_of(odd * SLICE, SLICE)
        other = pl.multiple_of(SLICE - mine, SLICE)
        for i in range(n):
            for t in range(WIDE // LANES):
                at = slice((t * n + i) * SLICE, (t * n + i + 1) * SLICE)
                lanes = slice(t * LANES, (t + 1) * LANES) if t < D // LANES else tile(D, t - D // LANES)
                own_ref[at, :] = acc[pl.ds(i * LANES + mine, SLICE), lanes]
                part_ref[at, :] = acc[pl.ds(i * LANES + other, SLICE), lanes]
        if last:
            for g, before in enumerate(sums_before):
                sums_ref[8 * g : 8 * g + 8, :] = before[...]
            g = len(GROUPS) - 1
            sums_ref[8 * g : 8 * g + 8, :] = sums[...]
            for t in range(D // LANES):
                sums_ref[8 * g + 8 + 16 * t : 8 * g + 24 + 16 * t, :] = gate_acc[:, t * LANES : (t + 1) * LANES]
        else:
            sums_ref[...] = sums[...]


def experts(group, rows, high, low, cot, p, shards, small, mix, before, deps):
    n = len(group)
    first, last = mix is None, before is not None
    steps = rows // RB
    block = lambda width: pl.BlockSpec((RB, width), lambda i: (i, 0))
    whole = lambda shape: pl.BlockSpec(shape, lambda i: (0,) * len(shape))
    in_specs = [
        block(D),
        block(D),
        block(3 * O),
        block(LANES),
        *[whole(shards[0].shape)] * 4,
    ]
    args = [high, low, cot, p, *shards]
    aliases = {}
    if not first:
        aliases = {len(args) + 1: 0}
        in_specs += [whole((4 * E, H)), block(3 * O)]
        args += [small, mix]
    if last:
        in_specs += [block(LANES)] * len(before[0]) + [whole((8, LANES))] * len(before[1])
        args += [*before[0], *before[1]]
    in_specs += [pl.BlockSpec(memory_space=pl.ANY)] * len(deps)
    args += deps
    payload = WIDE // LANES * n * SLICE
    sums_shape = (8 * len(GROUPS) + 16 * (D // LANES), LANES) if last else (8, LANES)
    scratch = [
        pltpu.VMEM((n, O, H), BF16),
        pltpu.VMEM((n, O, H), BF16),
        pltpu.VMEM((n * LANES, WIDE), F32),
        pltpu.VMEM((8, LANES), F32),
    ]
    if last:
        scratch.append(pltpu.VMEM((16, D), F32))
    return pl.pallas_call(
        functools.partial(expert_kernel, group, first, last, len(deps)),
        grid=(steps,),
        in_specs=in_specs,
        out_specs=[
                block(3 * O),
                block(LANES),
                block(n * H),
                block(n * H),
                whole((n * H, D)),
                whole((n * H, D)),
                whole((payload, LANES)),
                whole((payload, LANES)),
                whole(sums_shape),
        ]
        + [whole((4 * E, H))] * first,
        scratch_shapes=scratch,
        out_shape=[
            jax.ShapeDtypeStruct((rows, 3 * O), F32),
            jax.ShapeDtypeStruct((rows, LANES), F32),
            jax.ShapeDtypeStruct((rows, n * H), BF16),
            jax.ShapeDtypeStruct((rows, n * H), BF16),
            jax.ShapeDtypeStruct((n * H, D), BF16),
            jax.ShapeDtypeStruct((n * H, D), BF16),
            jax.ShapeDtypeStruct((payload, LANES), F32),
            jax.ShapeDtypeStruct((payload, LANES), F32),
            jax.ShapeDtypeStruct(sums_shape, F32),
        ]
        + [jax.ShapeDtypeStruct((4 * E, H), F32)] * first,
        input_output_aliases=aliases,
        compiler_params=params(EXPERT_MIB),
        cost_estimate=pl.CostEstimate(flops=n * rows * 6 * 720896, bytes_accessed=rows * 14000, transcendentals=0),
    )(*args)


def event_kernel(n, last, added, n_deps, *refs):
    highs, lows, winh, winl = (refs[k * n : (k + 1) * n] for k in range(4))
    refs = list(refs[4 * n :])
    total = 0.0
    if last:
        dlogits, gw_ref, gw = refs.pop(0), refs.pop(0), refs[-1]
        gw[...] = jnp.zeros_like(gw)
        gw[:GATE_COLS, :] = gw_ref[...]
        total = dot3(split(dlogits[...]), split(gw[...]), NN)
    before = refs.pop(0) if added else None
    out, token = refs[n_deps : n_deps + 2]
    for g in range(n):
        total = total + dot3((highs[g][...], lows[g][...]), (winh[g][...], winl[g][...]), NN)
    out[...] = total + before[...] if added else total
    token[...] = jnp.zeros_like(token)


def event_grads(rows, highs, lows, winh, winl, gating, before, deps):
    block = lambda width: pl.BlockSpec((ROW_BLOCK, width), lambda i: (i, 0))
    whole = lambda shape: pl.BlockSpec(shape, lambda i: (0, 0))
    args = [*highs, *lows, *winh, *winl]
    in_specs = [block(v.shape[1]) for v in (*highs, *lows)] + [whole(v.shape) for v in (*winh, *winl)]
    aliases = {}
    if gating:
        args += gating
        in_specs += [block(LANES), whole((GATE_COLS, D))]
    if before is not None:
        aliases = {len(args): 0}
        args.append(before)
        in_specs.append(block(D))
    return pl.pallas_call(
        functools.partial(event_kernel, len(highs), bool(gating), before is not None, len(deps)),
        grid=(rows // ROW_BLOCK,),
        in_specs=in_specs + [pl.BlockSpec(memory_space=pl.ANY)] * len(deps),
        out_specs=[block(D), whole(TOKEN)],
        scratch_shapes=[pltpu.VMEM((LANES, D), F32)],
        out_shape=[pltpu.VMEM((rows, D), F32), jax.ShapeDtypeStruct(TOKEN, F32)],
        input_output_aliases=aliases,
        compiler_params=params(EVENT_MIB),
        cost_estimate=pl.CostEstimate(
            flops=6 * rows * D * sum(v.shape[1] for v in highs), bytes_accessed=rows * 4000, transcendentals=0
        ),
    )(*args, *deps)


def place_kernel(own, other, *refs):
    out, token, sems = refs[-3:]
    rows = own.shape[0]
    side = lax.axis_index("tp") & 1
    copies = [
        pltpu.make_async_copy(v, out.at[pl.ds(pl.multiple_of(at * rows, ROW_BLOCK), rows), :], sems.at[k])
        for k, (v, at) in enumerate(((own, side), (other, 1 - side)))
    ]
    for copy in copies:
        copy.start()
    token[...] = jnp.zeros_like(token)
    for copy in copies:
        copy.wait()


def place(own, other, deps):
    rows, width = own.shape
    anywhere = pl.BlockSpec(memory_space=pl.ANY)
    return pl.pallas_call(
        place_kernel,
        in_specs=[anywhere] * (2 + len(deps)),
        out_specs=[pl.BlockSpec(memory_space=pltpu.HBM), pl.BlockSpec(memory_space=pltpu.VMEM)],
        scratch_shapes=[pltpu.SemaphoreType.DMA((2,))],
        out_shape=[jax.ShapeDtypeStruct((2 * rows, width), F32), jax.ShapeDtypeStruct(TOKEN, F32)],
        compiler_params=params(SMALL_MIB),
        cost_estimate=pl.CostEstimate(flops=0, bytes_accessed=rows * width * 16, transcendentals=0),
    )(own, other, *deps)


class Job:
    def __init__(self, args, shapes, body, scratch=()):
        self.args, self.body, self.scratch = args, body, list(scratch)
        self.shapes = [jax.ShapeDtypeStruct(shape, F32) for shape in shapes]


def copy_job(*arrays):
    def body(ins, outs, scratch):
        for a, b in zip(ins, outs):
            b[...] = a[...]

    return Job(arrays, [a.shape for a in arrays], body)


def run(jobs, deps=(), through=()):
    args = [a for job in jobs for a in job.args]
    shapes = [o for job in jobs for o in job.shapes]
    scratch = [v for job in jobs for v in job.scratch]

    def kernel(*refs):
        ins, refs = refs[: len(args)], refs[len(args) + len(through) + len(deps) :]
        outs, token, kept = refs[: len(shapes)], refs[len(shapes) + len(through)], refs[len(shapes) + len(through) + 1 :]
        token[...] = jnp.zeros_like(token)
        i = o = k = 0
        for job in jobs:
            ni, no, nk = len(job.args), len(job.shapes), len(job.scratch)
            job.body(ins[i : i + ni], outs[o : o + no], kept[k : k + nk])
            i, o, k = i + ni, o + no, k + nk

    vmem, anywhere = pl.BlockSpec(memory_space=pltpu.VMEM), pl.BlockSpec(memory_space=pl.ANY)
    flat = pl.pallas_call(
        kernel,
        in_specs=[vmem] * len(args) + [anywhere] * (len(through) + len(deps)),
        out_specs=[vmem] * len(shapes) + [anywhere] * len(through) + [vmem],
        out_shape=shapes
        + [jax.ShapeDtypeStruct(v.shape, v.dtype) for v in through]
        + [jax.ShapeDtypeStruct(TOKEN, F32)],
        scratch_shapes=scratch,
        input_output_aliases={len(args) + k: len(shapes) + k for k in range(len(through))},
        compiler_params=params(SMALL_MIB),
        cost_estimate=pl.CostEstimate(flops=0, bytes_accessed=sum(8 * a.size for a in args), transcendentals=0),
    )(*args, *through, *deps)
    result = []
    for job in jobs:
        result.append(list(flat[: len(job.shapes)]))
        flat = flat[len(job.shapes) :]
    return result, list(flat[:-1]), flat[-1]


def part_of(ref, index, rows):
    return ref.at[pl.ds(pl.multiple_of(index * rows, 8), rows), :]


class Piece:
    def __init__(self, array, at=0, rows=None):
        self.array, self.at = array, at
        self.rows = array.shape[0] if rows is None else rows

    def of(self, ref):
        return ref.at[pl.ds(self.at, self.rows), :]


def bit_groups(bits, width):
    groups, start = [], 0
    while bits - start > width:
        groups.append((start, width))
        start += width
    return groups, (start, bits - start)


class Reduction:
    def __init__(self, own, got, n_dp, kind, spare):
        self.spare = spare
        self.keep, self.got = [Piece(v) for v in own], [Piece(v) for v in got]
        pairs, last = bit_groups(n_dp.bit_length() - 1, 2)
        singles, lone = bit_groups(n_dp.bit_length() - 1, 1)
        if kind == "single":
            scatter, last, gather = singles, lone, singles
        elif kind == "pair":
            scatter, gather = pairs, pairs
        else:
            scatter, gather = [(b + k, 1) for b, n in pairs for k in reversed(range(n))], pairs
        self.order = [*scatter, last, *reversed(gather)]
        self.scattered = len(scatter)
        unit = 8 << sum(n for _, n in scatter)
        self.rows = -(-sum(p.rows for p in self.keep) // unit) * unit
        self.n_dp = n_dp
        self.stage = 0

    @property
    def finished(self):
        return self.stage > len(self.order)

    @property
    def joining(self):
        return self.stage == len(self.order)

    def job(self):
        stage = self.stage
        gather, scatter = stage > self.scattered + 1, stage < self.scattered
        n = len(self.keep)
        pieces = [*self.keep, *self.got]
        came = self.order[stage - 1]
        goes = self.order[stage] if stage < len(self.order) else None
        rows = self.rows if stage == 0 else self.keep[0].rows * ((1 << came[1]) if gather else 1)
        parts = 1 << goes[1] if scatter else 1

        def body(ins, outs, scratch):
            ins = [p.of(ref) for p, ref in zip(pieces, ins)]
            to = scratch[0] if scatter else outs[0]
            if gather:
                join(ins, to, came)
                return
            at = 0
            for k, piece in enumerate(pieces[:n]):
                total = ins[k][...]
                for v in ins[k + n :: n]:
                    total = total + v[...]
                to[at : at + piece.rows, :] = total
                at += piece.rows
            if at < to.shape[0]:
                to[at:, :] = jnp.zeros((to.shape[0] - at, LANES), F32)
            if scatter:
                side = side_of(goes)
                for m in range(parts):
                    outs[m][...] = part_of(to, side ^ m, rows // parts)[...]

        arrays = [p.array for p in pieces]
        if scatter:
            return Job(arrays, [(rows // parts, LANES)] * parts, body, [pltpu.VMEM((rows, LANES), F32)])
        self.used = rows
        return Job(arrays, [(rows + (self.spare if stage == self.scattered else 0), LANES)], body)

    def take(self, outs):
        self.stage += 1
        scatters = self.stage <= self.scattered
        rows = None if scatters else self.used
        self.keep = [Piece(outs[0], 0, rows)]
        if self.stage <= len(self.order):
            sent = outs[1:] if scatters else None
            self.got = [Piece(v, 0, rows) for v in exchange(outs[0], sent, self.order[self.stage - 1], self.n_dp)]

    @staticmethod
    def take_together(units, out, rows):
        at = 0
        came = exchange(out, None, units[0].order[units[0].stage], units[0].n_dp)
        for unit, n in zip(units, rows):
            unit.stage += 1
            unit.keep, unit.got = [Piece(out, at, n)], [Piece(v, at, n) for v in came]
            at += n


def exchange(whole, parts, bits, n_dp):
    start, n = bits
    return [
        lax.ppermute(whole if parts is None else parts[m - 1], "dp", [(i, i ^ (m << start)) for i in range(n_dp)])
        for m in range(1, 1 << n)
    ]


def side_of(bits):
    return (lax.axis_index("dp") >> bits[0]) & ((1 << bits[1]) - 1)


def join(ins, to, bits):
    for m, v in enumerate(ins):
        part_of(to, side_of(bits) ^ m, v.shape[0])[...] = v[...]


def together(jobs):
    rows = [job.shapes[0].shape[0] for job in jobs]

    def body(ins, outs, scratch):
        at = i = 0
        for job, n in zip(jobs, rows):
            job.body(ins[i : i + len(job.args)], [outs[0].at[pl.ds(at, n), :]], [])
            i, at = i + len(job.args), at + n

    return Job([a for job in jobs for a in job.args], [(sum(rows), LANES)], body), rows


def finish_body(joining, ins, outs, both):
    in_grad, in_bias, out_grad, out_bias, gain, shift, gate = outs
    odd = (lax.axis_index("tp") & 1) == 1
    ins, both, summed = list(ins), list(both), []
    for bits, pieces in joining:
        parts = [piece.of(ins.pop(0)) for piece in pieces]
        if bits:
            join(parts, both[0], bits)
            summed.append(both.pop(0))
        else:
            summed.append(parts[0])
    for u, unit in enumerate(UNITS):
        at = 0
        for g in unit:
            group = GROUPS[g]
            for t in range(WIDE // LANES):
                for e in group:
                    tile = summed[u][at : at + SLICE, :]
                    at += SLICE
                    if t < D // LANES:
                        in_grad[e, :, t * LANES : (t + 1) * LANES] = tile
                    else:
                        out_grad[e, :, t * LANES - D : (t + 1) * LANES - D] = tile
    sums = summed[-1][at : at + 8 * len(GROUPS), :]
    sums = jnp.where(odd, sums[:, SLICE:], sums[:, :SLICE])
    start = at + 8 * len(GROUPS)
    for g, group in enumerate(GROUPS):
        for i, e in enumerate(group):
            for k, ref in enumerate((in_bias, out_bias, gain, shift)):
                ref[e : e + 1, :] = sums[8 * g + 4 * i + k : 8 * g + 4 * i + k + 1, :]
    for t in range(D // LANES):
        gate[:, t * LANES : (t + 1) * LANES] = summed[-1][start + 16 * t : start + 16 * t + GATE_COLS, :]


def per_device(
    events,
    valid_counts,
    mix_cotangent,
    expert_in,
    expert_in_bias,
    expert_out,
    expert_out_bias,
    norm_gain,
    norm_shift,
    gate_weight,
):
    n_dp = lax.axis_size("dp")
    rows = events.shape[0] // 2
    w_in = jnp.swapaxes(expert_in, 1, 2)
    w_out = jnp.swapaxes(expert_out, 1, 2)
    gate_w = jnp.swapaxes(gate_weight, 0, 1)
    core = [(i, i ^ 1) for i in range(4)]
    across = [(i, i ^ 2) for i in range(4)]
    vectors = [expert_in_bias, expert_out_bias, norm_gain, norm_shift]
    own = list(payload(GROUPS[:1], w_in, w_out, vectors, []))
    far = [lax.ppermute(own[0], "tp", across)]
    beside = [lax.ppermute(own[0], "tp", core)]
    own += payload(GROUPS[1:], w_in, w_out, [], own)
    high, low, p, cot = gates(valid_counts, events, mix_cotangent, gate_w, rows, own[1:2])
    relayed = []
    summing = {}
    partial = []
    made = []
    placed, unplaced = [], []
    mix = small = x_grad = None
    deps = [p]
    for kind, what, units, *holding in PLAN:
        if kind == "experts":
            last = what == len(GROUPS) - 1
            shards = (own[what], beside[what], far[what], relayed[what])
            before = ([m[1] for m in made], [m[8] for m in made]) if last else None
            made.append(experts(GROUPS[what], rows, high, low, cot, p, shards, small, mix, before, deps))
            mix = made[what][0]
            small = made[0][9]
            deps = [made[what][8]]
        elif kind == "events":
            ours = [[made[g][k] for g in what] for k in (2, 3, 4, 5)]
            gating = [made[-1][1], gate_w] if what[-1] == len(GROUPS) - 1 else []
            x_grad, token = event_grads(rows, *ours, gating, x_grad, deps)
            deps = [token]
        elif kind == "place":
            v, token = place(*unplaced.pop(0), deps)
            placed.append(v)
            deps = [token]
        else:
            joint = units if "joint" in what else ()
            alone = () if joint else units
            held = holding[0] if holding else ()
            jobs = [summing[u].job() for u in (*alone, *held)]
            sent, fetched, through = [], [], []
            if "send" in what:
                sent = [made[-1][7]] + ([made[-1][8]] if len(made) == len(GROUPS) else [])
                jobs.append(copy_job(*sent))
            if "fetch" in what:
                group = len(relayed)
                fetched = [far[group], *own[group + 1 : group + 2]]
                jobs.append(copy_job(*fetched))
            if "mix" in what:
                through.append(mix)
            if "grad" in what:
                through.append(x_grad)
            if joint:
                job, rows_of = together([summing[u].job() for u in joint])
                jobs.append(job)
            outs, through, token = run(jobs, deps, through)
            deps = [token]
            if joint:
                Reduction.take_together([summing[u] for u in joint], outs.pop()[0], rows_of)
            for u, o in zip(alone, outs):
                summing[u].take(o)
            for u, o in zip(held, outs[len(alone) :]):
                summing[u].keep, summing[u].got = [Piece(o[0])], []
            if fetched:
                relayed.append(lax.ppermute(outs[-1][0], "tp", core))
                if len(fetched) > 1:
                    far.append(lax.ppermute(outs[-1][1], "tp", across))
                    beside.append(lax.ppermute(outs[-1][1], "tp", core))
            if sent:
                got = [lax.ppermute(v, "tp", core) for v in outs[len(alone) + len(held)]]
                partial.append(([made[-1][6], *sent[1:]], got))
                for u, (unit, way, spare) in enumerate(zip(UNITS, WAY, SPARE)):
                    if unit[-1] == len(partial) - 1:
                        both = [partial[g] for g in unit]
                        summing[u] = Reduction([v for b in both for v in b[0]], [v for b in both for v in b[1]], n_dp, way, spare)
            unplaced += [(v, lax.ppermute(v, "tp", core)) for v in through]
    mixtures, x_grad = placed
    summing = [summing[u] for u in range(len(UNITS))]
    while not all(u.finished or u.joining for u in summing):
        ours = [u for u in summing if not u.finished and not u.joining]
        outs, _, token = run([u.job() for u in ours], deps)
        deps = [token]
        for u, o in zip(ours, outs):
            u.take(o)
    joining = [(u.order[-1], [*u.keep, *u.got]) if u.joining else (None, u.keep) for u in summing]
    halves = [p.array for _, pieces in joining for p in pieces]
    per_expert = (E, SLICE)
    shapes = [(E, SLICE, D), per_expert, (E, SLICE, H), per_expert, per_expert, per_expert, (GATE_COLS, D)]
    scratch = [pltpu.VMEM((u.rows, LANES), F32) for u in summing if u.joining]
    job = Job(halves, shapes, functools.partial(finish_body, joining), scratch)
    (((in_grad, in_bias, out_grad, out_bias, gain, shift, gate),), _, _) = run([job], deps)
    return (
        mixtures,
        x_grad,
        jnp.swapaxes(in_grad, 1, 2),
        in_bias,
        jnp.swapaxes(out_grad, 1, 2),
        out_bias,
        gain,
        shift,
        jnp.swapaxes(gate, 0, 1),
    )


def solution(mesh):
    return jax.shard_map(
        per_device,
        mesh=mesh,
        in_specs=(
            P("dp", None),
            P(),
            P("dp", None),
            P(None, None, "tp"),
            P(None, "tp"),
            P(None, None, "tp"),
            P(None, "tp"),
            P(None, "tp"),
            P(None, "tp"),
            P(),
        ),
        out_specs=(
            P("dp", None),
            P("dp", None),
            P(None, None, "tp"),
            P(None, "tp"),
            P(None, None, "tp"),
            P(None, "tp"),
            P(None, "tp"),
            P(None, "tp"),
            P(),
        ),
        check_vma=False,
    )
```

```python
import functools

import jax
import jax.numpy as jnp
from jax import lax
from jax.experimental import pallas as pl
from jax.experimental.pallas import tpu as pltpu
from jax.sharding import PartitionSpec as P

D = 512
H = 256
O = 256
E = 6
GATE_COLS = 14
SLICE = 64
WIDE = D + H
LANES = 128
TOKEN = (8, LANES)
RB = 1024
ROW_BLOCK = 512
SUB = 256
LAG = 1
EPSILON = 1e-05
GROUPS = ((0, 1), (2, 3), (4,), (5,))
UNITS = ((0,), (1,), (2, 3))
WAY = ("single", "single", "pair")
SPARE = (0, 0, 0)
PLAN = (
    ("small", "fetch", ()),
    ("experts", 0, ()),
    ("small", "send", ()),
    ("events", (0,), ()),
    ("small", "fetch", (0,)),
    ("experts", 1, ()),
    ("small", "send fetch", (0,)),
    ("small", "", (1,)),
    ("experts", 2, ()),
    ("small", "send fetch", (0, 1)),
    ("experts", 3, ()),
    ("small", "send", (0, 1)),
    ("small", "", (2,)),
    ("events", (1, 2, 3), ()),
    ("small", "mix grad", (0, 1, 2)),
    ("small", "", (0, 1, 2)),
    ("place", None, ()),
    ("place", None, ()),
)
COLUMN = (
    {0: 0, 1: 1, 4: 2, 5: 3},
    {2: 4, 3: 5, 4: 6, 5: 7},
    {e: 8 + e for e in range(E)},
)
F32 = jnp.float32
BF16 = jnp.bfloat16
NN = (((1,), (0,)), ((), ()))
NT = (((1,), (1,)), ((), ()))
TN = (((0,), (0,)), ((), ()))


def split(v):
    high = v.astype(BF16)
    return high, (v - high.astype(F32)).astype(BF16)


def dot3(a, b, dims):
    def one(u, v):
        return lax.dot_general(u, v, dims, preferred_element_type=F32)

    return one(a[0], b[0]) + (one(a[0], b[1]) + one(a[1], b[0]))


def in_hbm(v):
    return pltpu.with_memory_space_constraint(v, pltpu.HBM)


LARGE = 60
EXPERT_MIB, EVENT_MIB, GATE_MIB, SMALL_MIB = 28, 16, 16, 8


def params(mib):
    return pltpu.CompilerParams(vmem_limit_bytes=mib << 20)


def gate_kernel(n_deps, counts, ev_ref, cot_ref, gw_ref, *refs):
    high_ref, low_ref, p_ref, cot_out, gw, held, sems = refs[n_deps:]
    rows = held.shape[0]
    steps = rows // ROW_BLOCK
    start = pl.multiple_of((lax.axis_index("tp") & 1) * rows, ROW_BLOCK)
    valid = counts[lax.axis_index("dp")]
    blocks = [slice(i * ROW_BLOCK, (i + 1) * ROW_BLOCK) for i in range(steps)]
    copies = [
        pltpu.make_async_copy(ev_ref.at[pl.ds(start + at.start, ROW_BLOCK), :], held.at[at, :], sems.at[i])
        for i, at in enumerate(blocks)
    ]
    copies.append(pltpu.make_async_copy(cot_ref.at[pl.ds(start, rows), :], cot_out, sems.at[steps]))
    for copy in copies:
        copy.start()
    gw[...] = jnp.zeros_like(gw)
    gw[:GATE_COLS, :] = gw_ref[...]
    gate = split(gw[...])
    lane = lax.broadcasted_iota(jnp.int32, (ROW_BLOCK, LANES), 1)
    sets = (lane < 4, (lane >= 4) & (lane < 8), (lane >= 8) & (lane < GATE_COLS))

    def per_set(values, empty, reduce):
        a, b, s = (reduce(jnp.where(m, values, empty), axis=1, keepdims=True) for m in sets)
        return jnp.where(sets[0], a, jnp.where(sets[1], b, s))

    for i, at in enumerate(blocks):
        copies[i].wait()
        events = split(held[at, :])
        high_ref[at, :], low_ref[at, :] = events
        logits = dot3(events, gate, NT)
        top = per_set(logits, -3e38, jnp.max)
        shares = jnp.where(lane < GATE_COLS, jnp.exp(logits - top), 0.0)
        p = shares / per_set(shares, 0.0, jnp.sum)
        row = start + at.start + lax.broadcasted_iota(jnp.int32, logits.shape, 0)
        p_ref[at, :] = jnp.where((row < valid) & (lane < GATE_COLS), p, 0.0)
    copies[-1].wait()


def gates(counts, events, cot, gate_w, rows, deps):
    vmem, hbm = pl.BlockSpec(memory_space=pltpu.VMEM), pl.BlockSpec(memory_space=pltpu.HBM)
    steps = rows // ROW_BLOCK
    return pl.pallas_call(
        functools.partial(gate_kernel, len(deps)),
        in_specs=[pl.BlockSpec(memory_space=pltpu.SMEM), hbm, hbm, vmem]
        + [pl.BlockSpec(memory_space=pl.ANY)] * len(deps),
        out_specs=[vmem] * 4,
        out_shape=[
            pltpu.VMEM((rows, D), BF16),
            pltpu.VMEM((rows, D), BF16),
            pltpu.VMEM((rows, LANES), F32),
            pltpu.VMEM((rows, 3 * O), F32),
        ],
        scratch_shapes=[
            pltpu.VMEM((LANES, D), F32),
            pltpu.VMEM((rows, D), F32),
            pltpu.SemaphoreType.DMA((steps + 1,)),
        ],
        compiler_params=params(GATE_MIB),
        cost_estimate=pl.CostEstimate(flops=6 * rows * D * LANES, bytes_accessed=rows * D * 8, transcendentals=0),
    )(counts, in_hbm(events), in_hbm(cot), in_hbm(gate_w), *deps)


def payload_kernel(groups, vectors, n_deps, w_in, w_out, *refs):
    given = refs[:4] if vectors else ()
    held = refs[-2]
    outs, sems = refs[len(given) + n_deps :][: len(groups)], refs[-1]
    copies = []
    for out, group in zip(outs, groups):
        for part, lanes in ((w_in, slice(0, D)), (w_out, slice(D, WIDE))):
            for i, e in enumerate(group):
                to = out.at[pl.ds(i * SLICE, SLICE), lanes] if vectors else out.at[i, :, lanes]
                copies.append(pltpu.make_async_copy(part.at[e], to, sems.at[len(copies)]))
    for k, v in enumerate(given):
        copies.append(pltpu.make_async_copy(v, held.at[k, slice(0, E), :], sems.at[len(copies)]))
    for copy in copies:
        copy.start()
    if vectors:
        for copy in copies[-len(given) :]:
            copy.wait()
        copies = copies[: -len(given)]
        rows = jnp.concatenate([held[k, :E, :] for k in range(4)], axis=0)
        end = len(groups[0]) * SLICE
        outs[0][end:, :] = jnp.zeros((8, WIDE), F32)
        for j in range(4 * E // 8):
            outs[0][end:, j * LANES : j * LANES + SLICE] = rows[8 * j : 8 * j + 8, :]
    for copy in copies:
        copy.wait()


def payload(groups, w_in, w_out, vectors, deps):
    vmem, hbm = pl.BlockSpec(memory_space=pltpu.VMEM), pl.BlockSpec(memory_space=pltpu.HBM)
    shapes = [(len(group) * SLICE + 8, WIDE) if vectors else (len(group), SLICE, WIDE) for group in groups]
    return pl.pallas_call(
        functools.partial(payload_kernel, groups, bool(vectors), len(deps)),
        in_specs=[hbm, hbm] + [hbm] * len(vectors) + [pl.BlockSpec(memory_space=pl.ANY)] * len(deps),
        out_specs=[vmem] * len(groups),
        out_shape=[pltpu.VMEM(shape, F32) for shape in shapes],
        scratch_shapes=[pltpu.VMEM((4, 8, SLICE), F32), pltpu.SemaphoreType.DMA((2 * E + 4,))],
        compiler_params=params(SMALL_MIB),
        cost_estimate=pl.CostEstimate(flops=0, bytes_accessed=SLICE * WIDE * 16, transcendentals=0),
    )(in_hbm(w_in), in_hbm(w_out), *[in_hbm(v) for v in vectors], *deps)


def expert_kernel(group, first, last, n_deps, *refs):
    n = len(group)
    sub = SUB * n
    refs = list(refs)
    evh_ref, evl_ref, cot_ref, p_ref = refs[:4]
    shards = refs[4:8]
    del refs[:8]
    small = None if first else refs.pop(0)
    mix_in = None if first else refs.pop(0)
    if last:
        dp_before, sums_before = refs[: len(GROUPS) - 1], refs[len(GROUPS) - 1 : 2 * len(GROUPS) - 2]
        del refs[: 2 * len(GROUPS) - 2]
    del refs[:n_deps]
    mix_ref, dp_ref, dph_ref, dpl_ref, winh, winl, own_ref, part_ref, sums_ref = refs[:9]
    del refs[:9]
    if first:
        small = refs.pop(0)
    wouth, woutl, acc, sums = refs[:4]
    gate_acc = refs[4] if last else None
    step, steps = pl.program_id(0), pl.num_programs(0)
    odd = lax.axis_index("tp") & 1
    chip = lax.axis_index("tp") >> 1

    def tile(start, other):
        return pl.ds(pl.multiple_of(start + (chip ^ other) * LANES, LANES), LANES)

    @pl.when(step == 0)
    def _():
        acc[...] = jnp.zeros_like(acc)
        sums[...] = jnp.zeros_like(sums)
        if last:
            gate_acc[...] = jnp.zeros_like(gate_acc)
        for j in range(4 * E // 8 if first else 0):
            vectors = [shard[n * SLICE :, j * LANES : j * LANES + SLICE] for shard in shards]
            even_order, odd_order = (jnp.concatenate([vectors[k ^ c] for k in range(4)], axis=1) for c in range(2))
            small[8 * j : 8 * j + 8, :] = jnp.where(odd == 1, odd_order, even_order)
        if first:
            bias = small[E : 2 * E, :]
            small[E : 2 * E, :] = bias - jnp.mean(bias, axis=1, keepdims=True)
        for i, e in enumerate(group):
            at = (slice(i * SLICE, (i + 1) * SLICE),) if first else (i, slice(0, SLICE))
            parts = [
                (shard[*at, slice(0, D)], jnp.concatenate([shard[*at, tile(D, k)] for k in range(2)], axis=1))
                for shard in shards
            ]
            centre = sum(jnp.sum(out, axis=0, keepdims=True) for _, out in parts) / O
            for k, (into, out) in enumerate(parts):
                at = pl.multiple_of((odd ^ k) * SLICE, SLICE)
                winh[pl.ds(i * H + at, SLICE), :], winl[pl.ds(i * H + at, SLICE), :] = split(into)
                wouth[i, pl.ds(at, SLICE), :], woutl[i, pl.ds(at, SLICE), :] = split(out - centre)

    subs = RB // sub
    rows_of = [slice(s * sub, (s + 1) * sub) for s in range(subs)]
    lane = lax.broadcasted_iota(jnp.int32, (sub, LANES), 1)
    vector = lambda k, e: small[k * E + e : k * E + e + 1, :]
    state = [dict() for _ in range(subs)]

    def m1(s):
        events = evh_ref[rows_of[s], :], evl_ref[rows_of[s], :]
        state[s]["events"] = events
        pre = dot3(events, (winh[...], winl[...]), NT)
        state[s]["pre"] = [pre[:, i * H : (i + 1) * H] for i in range(n)]

    def v1(s):
        st = state[s]
        st["sigma"], st["hidden"], st["hidden_parts"] = [], [], []
        for i, e in enumerate(group):
            pre = st["pre"][i] + vector(0, e)
            sigma = jax.nn.sigmoid(pre)
            hidden = pre * sigma
            st["sigma"].append(sigma)
            st["hidden"].append(hidden)
            st["hidden_parts"].append(split(hidden))

    def m2(s):
        st = state[s]
        st["centred"] = [dot3(st["hidden_parts"][i], (wouth[i], woutl[i]), NT) for i in range(n)]

    def v2(s):
        st = state[s]
        p = p_ref[rows_of[s], :]
        dp = jnp.zeros_like(p)
        mixed = {}
        cots = [
            jnp.concatenate([cot_ref[rows_of[s], tile(t * O, 0)], cot_ref[rows_of[s], tile(t * O, 1)]], axis=1)
            for t in range(3)
        ]
        st["dnormed"] = []
        for i, e in enumerate(group):
            gain, shift = vector(2, e), vector(3, e)
            centred = st["centred"][i] + vector(1, e)
            rstd = lax.rsqrt(jnp.mean(centred * centred, axis=1, keepdims=True) + EPSILON)
            unit = centred * rstd
            y = unit * gain + shift
            dy = None
            for t in range(3):
                if e not in COLUMN[t]:
                    continue
                column = COLUMN[t][e]
                coef = p[:, column : column + 1]
                mixed[t] = coef * y + mixed[t] if t in mixed else coef * y
                dp = jnp.where(lane == column, jnp.sum(cots[t] * y, axis=1, keepdims=True), dp)
                dy = coef * cots[t] if dy is None else dy + coef * cots[t]
            dunit = dy * gain
            back_first = jnp.mean(dunit, axis=1, keepdims=True)
            back_second = jnp.mean(dunit * unit, axis=1, keepdims=True)
            dnormed = rstd * (dunit - back_first - unit * back_second)
            st["dnormed"].append(split(dnormed))
            dy_half = dy[:, :LANES]
            for k, v in enumerate((dnormed[:, :LANES], dy_half * unit[:, :LANES], dy_half)):
                sums[4 * i + k + 1 : 4 * i + k + 2, :] += jnp.sum(v, axis=0, keepdims=True)
        for t in range(3):
            for other in range(2):
                at = tile(t * O, other)
                if t in mixed:
                    value = mixed[t][:, other * LANES : (other + 1) * LANES]
                    mix_ref[rows_of[s], at] = value if first else mix_in[rows_of[s], at] + value
                elif first:
                    mix_ref[rows_of[s], at] = jnp.zeros((sub, LANES), F32)
                else:
                    mix_ref[rows_of[s], at] = mix_in[rows_of[s], at]
        if last:
            for other in dp_before:
                dp = dp + other[rows_of[s], :]
            weighted = p * dp
            sets = (lane < 4, (lane >= 4) & (lane < 8), (lane >= 8) & (lane < GATE_COLS))
            a, b, c = (jnp.sum(jnp.where(m, weighted, 0.0), axis=1, keepdims=True) for m in sets)
            dp = weighted - p * jnp.where(sets[0], a, jnp.where(sets[1], b, c))
            st["dlogits"] = dp
        dp_ref[rows_of[s], :] = dp

    def m3(s):
        st = state[s]
        st["dhidden"] = [dot3(st["dnormed"][i], (wouth[i], woutl[i]), NN) for i in range(n)]

    def v3(s):
        st = state[s]
        st["dpre"] = []
        for i, e in enumerate(group):
            sigma, hidden = st["sigma"][i], st["hidden"][i]
            dpre = st["dhidden"][i] * (sigma + hidden * (1.0 - sigma))
            parts = split(dpre)
            dph_ref[rows_of[s], i * H : (i + 1) * H], dpl_ref[rows_of[s], i * H : (i + 1) * H] = parts
            st["dpre"].append(tuple(v[:, :LANES] for v in parts))
            sums[4 * i : 4 * i + 1, :] += jnp.sum(dpre[:, :LANES], axis=0, keepdims=True)

    def m4(s):
        st = state[s]
        for i in range(n):
            halves = tuple(v[:, :LANES] for v in st["dnormed"][i])
            acc[i * LANES : (i + 1) * LANES, D:] += dot3(halves, st["hidden_parts"][i], TN)
        beside = [split(st["dlogits"][:, :16])] if last else []
        left = tuple(jnp.concatenate([h[k] for h in st["dpre"] + beside], axis=1) for k in range(2))
        both = dot3(left, st["events"], TN)
        acc[:, :D] += both[: n * LANES]
        if last:
            gate_acc[...] += both[n * LANES : n * LANES + 16]

    stages = (m1, v1, m2, v2, m3, v3, m4)
    for turn in range(len(stages) + LAG * (subs - 1)):
        for s in range(subs):
            if 0 <= turn - LAG * s < len(stages):
                stages[turn - LAG * s](s)

    @pl.when(step == steps - 1)
    def _():
        mine = pl.multiple_of(odd * SLICE, SLICE)
        other = pl.multiple_of(SLICE - mine, SLICE)
        for i in range(n):
            for t in range(WIDE // LANES):
                at = slice((t * n + i) * SLICE, (t * n + i + 1) * SLICE)
                lanes = slice(t * LANES, (t + 1) * LANES) if t < D // LANES else tile(D, t - D // LANES)
                own_ref[at, :] = acc[pl.ds(i * LANES + mine, SLICE), lanes]
                part_ref[at, :] = acc[pl.ds(i * LANES + other, SLICE), lanes]
        if last:
            for g, before in enumerate(sums_before):
                sums_ref[8 * g : 8 * g + 8, :] = before[...]
            g = len(GROUPS) - 1
            sums_ref[8 * g : 8 * g + 8, :] = sums[...]
            for t in range(D // LANES):
                sums_ref[8 * g + 8 + 16 * t : 8 * g + 24 + 16 * t, :] = gate_acc[:, t * LANES : (t + 1) * LANES]
        else:
            sums_ref[...] = sums[...]


def experts(group, rows, high, low, cot, p, shards, small, mix, before, deps):
    n = len(group)
    first, last = mix is None, before is not None
    steps = rows // RB
    block = lambda width: pl.BlockSpec((RB, width), lambda i: (i, 0))
    whole = lambda shape: pl.BlockSpec(shape, lambda i: (0,) * len(shape))
    in_specs = [
        block(D),
        block(D),
        block(3 * O),
        block(LANES),
        *[whole(shards[0].shape)] * 4,
    ]
    args = [high, low, cot, p, *shards]
    aliases = {}
    if not first:
        aliases = {len(args) + 1: 0}
        in_specs += [whole((4 * E, H)), block(3 * O)]
        args += [small, mix]
    if last:
        in_specs += [block(LANES)] * len(before[0]) + [whole((8, LANES))] * len(before[1])
        args += [*before[0], *before[1]]
    in_specs += [pl.BlockSpec(memory_space=pl.ANY)] * len(deps)
    args += deps
    payload = WIDE // LANES * n * SLICE
    sums_shape = (8 * len(GROUPS) + 16 * (D // LANES), LANES) if last else (8, LANES)
    scratch = [
        pltpu.VMEM((n, O, H), BF16),
        pltpu.VMEM((n, O, H), BF16),
        pltpu.VMEM((n * LANES, WIDE), F32),
        pltpu.VMEM((8, LANES), F32),
    ]
    if last:
        scratch.append(pltpu.VMEM((16, D), F32))
    return pl.pallas_call(
        functools.partial(expert_kernel, group, first, last, len(deps)),
        grid=(steps,),
        in_specs=in_specs,
        out_specs=[
                block(3 * O),
                block(LANES),
                block(n * H),
                block(n * H),
                whole((n * H, D)),
                whole((n * H, D)),
                whole((payload, LANES)),
                whole((payload, LANES)),
                whole(sums_shape),
        ]
        + [whole((4 * E, H))] * first,
        scratch_shapes=scratch,
        out_shape=[
            jax.ShapeDtypeStruct((rows, 3 * O), F32),
            jax.ShapeDtypeStruct((rows, LANES), F32),
            jax.ShapeDtypeStruct((rows, n * H), BF16),
            jax.ShapeDtypeStruct((rows, n * H), BF16),
            jax.ShapeDtypeStruct((n * H, D), BF16),
            jax.ShapeDtypeStruct((n * H, D), BF16),
            jax.ShapeDtypeStruct((payload, LANES), F32),
            jax.ShapeDtypeStruct((payload, LANES), F32),
            jax.ShapeDtypeStruct(sums_shape, F32),
        ]
        + [jax.ShapeDtypeStruct((4 * E, H), F32)] * first,
        input_output_aliases=aliases,
        compiler_params=params(EXPERT_MIB),
        cost_estimate=pl.CostEstimate(flops=n * rows * 6 * 720896, bytes_accessed=rows * 14000, transcendentals=0),
    )(*args)


def event_kernel(n, last, added, n_deps, *refs):
    highs, lows, winh, winl = (refs[k * n : (k + 1) * n] for k in range(4))
    refs = list(refs[4 * n :])
    total = 0.0
    if last:
        dlogits, gw_ref, gw = refs.pop(0), refs.pop(0), refs[-1]
        gw[...] = jnp.zeros_like(gw)
        gw[:GATE_COLS, :] = gw_ref[...]
        total = dot3(split(dlogits[...]), split(gw[...]), NN)
    before = refs.pop(0) if added else None
    out, token = refs[n_deps : n_deps + 2]
    for g in range(n):
        total = total + dot3((highs[g][...], lows[g][...]), (winh[g][...], winl[g][...]), NN)
    out[...] = total + before[...] if added else total
    token[...] = jnp.zeros_like(token)


def event_grads(rows, highs, lows, winh, winl, gating, before, deps):
    block = lambda width: pl.BlockSpec((ROW_BLOCK, width), lambda i: (i, 0))
    whole = lambda shape: pl.BlockSpec(shape, lambda i: (0, 0))
    args = [*highs, *lows, *winh, *winl]
    in_specs = [block(v.shape[1]) for v in (*highs, *lows)] + [whole(v.shape) for v in (*winh, *winl)]
    aliases = {}
    if gating:
        args += gating
        in_specs += [block(LANES), whole((GATE_COLS, D))]
    if before is not None:
        aliases = {len(args): 0}
        args.append(before)
        in_specs.append(block(D))
    return pl.pallas_call(
        functools.partial(event_kernel, len(highs), bool(gating), before is not None, len(deps)),
        grid=(rows // ROW_BLOCK,),
        in_specs=in_specs + [pl.BlockSpec(memory_space=pl.ANY)] * len(deps),
        out_specs=[block(D), whole(TOKEN)],
        scratch_shapes=[pltpu.VMEM((LANES, D), F32)],
        out_shape=[pltpu.VMEM((rows, D), F32), jax.ShapeDtypeStruct(TOKEN, F32)],
        input_output_aliases=aliases,
        compiler_params=params(EVENT_MIB),
        cost_estimate=pl.CostEstimate(
            flops=6 * rows * D * sum(v.shape[1] for v in highs), bytes_accessed=rows * 4000, transcendentals=0
        ),
    )(*args, *deps)


def place_kernel(own, other, *refs):
    out, token, sems = refs[-3:]
    rows = own.shape[0]
    side = lax.axis_index("tp") & 1
    copies = [
        pltpu.make_async_copy(v, out.at[pl.ds(pl.multiple_of(at * rows, ROW_BLOCK), rows), :], sems.at[k])
        for k, (v, at) in enumerate(((own, side), (other, 1 - side)))
    ]
    for copy in copies:
        copy.start()
    token[...] = jnp.zeros_like(token)
    for copy in copies:
        copy.wait()


def place(own, other, deps):
    rows, width = own.shape
    anywhere = pl.BlockSpec(memory_space=pl.ANY)
    return pl.pallas_call(
        place_kernel,
        in_specs=[anywhere] * (2 + len(deps)),
        out_specs=[pl.BlockSpec(memory_space=pltpu.HBM), pl.BlockSpec(memory_space=pltpu.VMEM)],
        scratch_shapes=[pltpu.SemaphoreType.DMA((2,))],
        out_shape=[jax.ShapeDtypeStruct((2 * rows, width), F32), jax.ShapeDtypeStruct(TOKEN, F32)],
        compiler_params=params(SMALL_MIB),
        cost_estimate=pl.CostEstimate(flops=0, bytes_accessed=rows * width * 16, transcendentals=0),
    )(own, other, *deps)


class Job:
    def __init__(self, args, shapes, body, scratch=()):
        self.args, self.body, self.scratch = args, body, list(scratch)
        self.shapes = [jax.ShapeDtypeStruct(shape, F32) for shape in shapes]


def copy_job(*arrays):
    def body(ins, outs, scratch):
        for a, b in zip(ins, outs):
            b[...] = a[...]

    return Job(arrays, [a.shape for a in arrays], body)


def run(jobs, deps=(), through=()):
    args = [a for job in jobs for a in job.args]
    shapes = [o for job in jobs for o in job.shapes]
    scratch = [v for job in jobs for v in job.scratch]

    def kernel(*refs):
        ins, refs = refs[: len(args)], refs[len(args) + len(through) + len(deps) :]
        outs, token, kept = refs[: len(shapes)], refs[len(shapes) + len(through)], refs[len(shapes) + len(through) + 1 :]
        token[...] = jnp.zeros_like(token)
        i = o = k = 0
        for job in jobs:
            ni, no, nk = len(job.args), len(job.shapes), len(job.scratch)
            job.body(ins[i : i + ni], outs[o : o + no], kept[k : k + nk])
            i, o, k = i + ni, o + no, k + nk

    vmem, anywhere = pl.BlockSpec(memory_space=pltpu.VMEM), pl.BlockSpec(memory_space=pl.ANY)
    flat = pl.pallas_call(
        kernel,
        in_specs=[vmem] * len(args) + [anywhere] * (len(through) + len(deps)),
        out_specs=[vmem] * len(shapes) + [anywhere] * len(through) + [vmem],
        out_shape=shapes
        + [jax.ShapeDtypeStruct(v.shape, v.dtype) for v in through]
        + [jax.ShapeDtypeStruct(TOKEN, F32)],
        scratch_shapes=scratch,
        input_output_aliases={len(args) + k: len(shapes) + k for k in range(len(through))},
        compiler_params=params(SMALL_MIB),
        cost_estimate=pl.CostEstimate(flops=0, bytes_accessed=sum(8 * a.size for a in args), transcendentals=0),
    )(*args, *through, *deps)
    result = []
    for job in jobs:
        result.append(list(flat[: len(job.shapes)]))
        flat = flat[len(job.shapes) :]
    return result, list(flat[:-1]), flat[-1]


def part_of(ref, index, rows):
    return ref.at[pl.ds(pl.multiple_of(index * rows, 8), rows), :]


class Piece:
    def __init__(self, array, at=0, rows=None):
        self.array, self.at = array, at
        self.rows = array.shape[0] if rows is None else rows

    def of(self, ref):
        return ref.at[pl.ds(self.at, self.rows), :]


def bit_groups(bits, width):
    groups, start = [], 0
    while bits - start > width:
        groups.append((start, width))
        start += width
    return groups, (start, bits - start)


class Reduction:
    def __init__(self, own, got, n_dp, kind, spare):
        self.spare = spare
        self.keep, self.got = [Piece(v) for v in own], [Piece(v) for v in got]
        pairs, last = bit_groups(n_dp.bit_length() - 1, 2)
        singles, lone = bit_groups(n_dp.bit_length() - 1, 1)
        if kind == "single":
            scatter, last, gather = singles, lone, singles
        elif kind == "pair":
            scatter, gather = pairs, pairs
        else:
            scatter, gather = [(b + k, 1) for b, n in pairs for k in reversed(range(n))], pairs
        self.order = [*scatter, last, *reversed(gather)]
        self.scattered = len(scatter)
        unit = 8 << sum(n for _, n in scatter)
        self.rows = -(-sum(p.rows for p in self.keep) // unit) * unit
        self.n_dp = n_dp
        self.stage = 0

    @property
    def finished(self):
        return self.stage > len(self.order)

    @property
    def joining(self):
        return self.stage == len(self.order)

    def job(self):
        stage = self.stage
        gather, scatter = stage > self.scattered + 1, stage < self.scattered
        n = len(self.keep)
        pieces = [*self.keep, *self.got]
        came = self.order[stage - 1]
        goes = self.order[stage] if stage < len(self.order) else None
        rows = self.rows if stage == 0 else self.keep[0].rows * ((1 << came[1]) if gather else 1)
        parts = 1 << goes[1] if scatter else 1

        def body(ins, outs, scratch):
            ins = [p.of(ref) for p, ref in zip(pieces, ins)]
            to = scratch[0] if scatter else outs[0]
            if gather:
                join(ins, to, came)
                return
            at = 0
            for k, piece in enumerate(pieces[:n]):
                total = ins[k][...]
                for v in ins[k + n :: n]:
                    total = total + v[...]
                to[at : at + piece.rows, :] = total
                at += piece.rows
            if at < to.shape[0]:
                to[at:, :] = jnp.zeros((to.shape[0] - at, LANES), F32)
            if scatter:
                side = side_of(goes)
                for m in range(parts):
                    outs[m][...] = part_of(to, side ^ m, rows // parts)[...]

        arrays = [p.array for p in pieces]
        if scatter:
            return Job(arrays, [(rows // parts, LANES)] * parts, body, [pltpu.VMEM((rows, LANES), F32)])
        self.used = rows
        return Job(arrays, [(rows + (self.spare if stage == self.scattered else 0), LANES)], body)

    def take(self, outs):
        self.stage += 1
        scatters = self.stage <= self.scattered
        rows = None if scatters else self.used
        self.keep = [Piece(outs[0], 0, rows)]
        if self.stage <= len(self.order):
            sent = outs[1:] if scatters else None
            self.got = [Piece(v, 0, rows) for v in exchange(outs[0], sent, self.order[self.stage - 1], self.n_dp)]

    @staticmethod
    def take_together(units, out, rows):
        at = 0
        came = exchange(out, None, units[0].order[units[0].stage], units[0].n_dp)
        for unit, n in zip(units, rows):
            unit.stage += 1
            unit.keep, unit.got = [Piece(out, at, n)], [Piece(v, at, n) for v in came]
            at += n


def exchange(whole, parts, bits, n_dp):
    start, n = bits
    return [
        lax.ppermute(whole if parts is None else parts[m - 1], "dp", [(i, i ^ (m << start)) for i in range(n_dp)])
        for m in range(1, 1 << n)
    ]


def side_of(bits):
    return (lax.axis_index("dp") >> bits[0]) & ((1 << bits[1]) - 1)


def join(ins, to, bits):
    for m, v in enumerate(ins):
        part_of(to, side_of(bits) ^ m, v.shape[0])[...] = v[...]


def together(jobs):
    rows = [job.shapes[0].shape[0] for job in jobs]

    def body(ins, outs, scratch):
        at = i = 0
        for job, n in zip(jobs, rows):
            job.body(ins[i : i + len(job.args)], [outs[0].at[pl.ds(at, n), :]], [])
            i, at = i + len(job.args), at + n

    return Job([a for job in jobs for a in job.args], [(sum(rows), LANES)], body), rows


def finish_body(joining, ins, outs, both):
    in_grad, in_bias, out_grad, out_bias, gain, shift, gate = outs
    odd = (lax.axis_index("tp") & 1) == 1
    ins, both, summed = list(ins), list(both), []
    for bits, pieces in joining:
        parts = [piece.of(ins.pop(0)) for piece in pieces]
        if bits:
            join(parts, both[0], bits)
            summed.append(both.pop(0))
        else:
            summed.append(parts[0])
    for u, unit in enumerate(UNITS):
        at = 0
        for g in unit:
            group = GROUPS[g]
            for t in range(WIDE // LANES):
                for e in group:
                    tile = summed[u][at : at + SLICE, :]
                    at += SLICE
                    if t < D // LANES:
                        in_grad[e, :, t * LANES : (t + 1) * LANES] = tile
                    else:
                        out_grad[e, :, t * LANES - D : (t + 1) * LANES - D] = tile
    sums = summed[-1][at : at + 8 * len(GROUPS), :]
    sums = jnp.where(odd, sums[:, SLICE:], sums[:, :SLICE])
    start = at + 8 * len(GROUPS)
    for g, group in enumerate(GROUPS):
        for i, e in enumerate(group):
            for k, ref in enumerate((in_bias, out_bias, gain, shift)):
                ref[e : e + 1, :] = sums[8 * g + 4 * i + k : 8 * g + 4 * i + k + 1, :]
    for t in range(D // LANES):
        gate[:, t * LANES : (t + 1) * LANES] = summed[-1][start + 16 * t : start + 16 * t + GATE_COLS, :]


def per_device(
    events,
    valid_counts,
    mix_cotangent,
    expert_in,
    expert_in_bias,
    expert_out,
    expert_out_bias,
    norm_gain,
    norm_shift,
    gate_weight,
):
    n_dp = lax.axis_size("dp")
    rows = events.shape[0] // 2
    w_in = jnp.swapaxes(expert_in, 1, 2)
    w_out = jnp.swapaxes(expert_out, 1, 2)
    gate_w = jnp.swapaxes(gate_weight, 0, 1)
    core = [(i, i ^ 1) for i in range(4)]
    across = [(i, i ^ 2) for i in range(4)]
    vectors = [expert_in_bias, expert_out_bias, norm_gain, norm_shift]
    own = list(payload(GROUPS[:1], w_in, w_out, vectors, []))
    far = [lax.ppermute(own[0], "tp", across)]
    beside = [lax.ppermute(own[0], "tp", core)]
    own += payload(GROUPS[1:], w_in, w_out, [], own)
    high, low, p, cot = gates(valid_counts, events, mix_cotangent, gate_w, rows, own[1:2])
    relayed = []
    summing = {}
    partial = []
    made = []
    placed, unplaced = [], []
    mix = small = x_grad = None
    deps = [p]
    for kind, what, units, *holding in PLAN:
        if kind == "experts":
            last = what == len(GROUPS) - 1
            shards = (own[what], beside[what], far[what], relayed[what])
            before = ([m[1] for m in made], [m[8] for m in made]) if last else None
            made.append(experts(GROUPS[what], rows, high, low, cot, p, shards, small, mix, before, deps))
            mix = made[what][0]
            small = made[0][9]
            deps = [made[what][8]]
        elif kind == "events":
            ours = [[made[g][k] for g in what] for k in (2, 3, 4, 5)]
            gating = [made[-1][1], gate_w] if what[-1] == len(GROUPS) - 1 else []
            x_grad, token = event_grads(rows, *ours, gating, x_grad, deps)
            deps = [token]
        elif kind == "place":
            v, token = place(*unplaced.pop(0), deps)
            placed.append(v)
            deps = [token]
        else:
            joint = units if "joint" in what else ()
            alone = () if joint else units
            held = holding[0] if holding else ()
            jobs = [summing[u].job() for u in (*alone, *held)]
            sent, fetched, through = [], [], []
            if "send" in what:
                sent = [made[-1][7]] + ([made[-1][8]] if len(made) == len(GROUPS) else [])
                jobs.append(copy_job(*sent))
            if "fetch" in what:
                group = len(relayed)
                fetched = [far[group], *own[group + 1 : group + 2]]
                jobs.append(copy_job(*fetched))
            if "mix" in what:
                through.append(mix)
            if "grad" in what:
                through.append(x_grad)
            if joint:
                job, rows_of = together([summing[u].job() for u in joint])
                jobs.append(job)
            outs, through, token = run(jobs, deps, through)
            deps = [token]
            if joint:
                Reduction.take_together([summing[u] for u in joint], outs.pop()[0], rows_of)
            for u, o in zip(alone, outs):
                summing[u].take(o)
            for u, o in zip(held, outs[len(alone) :]):
                summing[u].keep, summing[u].got = [Piece(o[0])], []
            if fetched:
                relayed.append(lax.ppermute(outs[-1][0], "tp", core))
                if len(fetched) > 1:
                    far.append(lax.ppermute(outs[-1][1], "tp", across))
                    beside.append(lax.ppermute(outs[-1][1], "tp", core))
            if sent:
                got = [lax.ppermute(v, "tp", core) for v in outs[len(alone) + len(held)]]
                partial.append(([made[-1][6], *sent[1:]], got))
                for u, (unit, way, spare) in enumerate(zip(UNITS, WAY, SPARE)):
                    if unit[-1] == len(partial) - 1:
                        both = [partial[g] for g in unit]
                        summing[u] = Reduction([v for b in both for v in b[0]], [v for b in both for v in b[1]], n_dp, way, spare)
            unplaced += [(v, lax.ppermute(v, "tp", core)) for v in through]
    mixtures, x_grad = placed
    summing = [summing[u] for u in range(len(UNITS))]
    while not all(u.finished or u.joining for u in summing):
        ours = [u for u in summing if not u.finished and not u.joining]
        outs, _, token = run([u.job() for u in ours], deps)
        deps = [token]
        for u, o in zip(ours, outs):
            u.take(o)
    joining = [(u.order[-1], [*u.keep, *u.got]) if u.joining else (None, u.keep) for u in summing]
    halves = [p.array for _, pieces in joining for p in pieces]
    per_expert = (E, SLICE)
    shapes = [(E, SLICE, D), per_expert, (E, SLICE, H), per_expert, per_expert, per_expert, (GATE_COLS, D)]
    scratch = [pltpu.VMEM((u.rows, LANES), F32) for u in summing if u.joining]
    job = Job(halves, shapes, functools.partial(finish_body, joining), scratch)
    (((in_grad, in_bias, out_grad, out_bias, gain, shift, gate),), _, _) = run([job], deps)
    return (
        mixtures,
        x_grad,
        jnp.swapaxes(in_grad, 1, 2),
        in_bias,
        jnp.swapaxes(out_grad, 1, 2),
        out_bias,
        gain,
        shift,
        jnp.swapaxes(gate, 0, 1),
    )


def solution(mesh):
    return jax.shard_map(
        per_device,
        mesh=mesh,
        in_specs=(
            P("dp", None),
            P(),
            P("dp", None),
            P(None, None, "tp"),
            P(None, "tp"),
            P(None, None, "tp"),
            P(None, "tp"),
            P(None, "tp"),
            P(None, "tp"),
            P(),
        ),
        out_specs=(
            P("dp", None),
            P("dp", None),
            P(None, None, "tp"),
            P(None, "tp"),
            P(None, None, "tp"),
            P(None, "tp"),
            P(None, "tp"),
            P(None, "tp"),
            P(),
        ),
        check_vma=False,
    )
```
